32 devices in a mesh: tile: 8 (over z, x), member: 4 (over y, core).
Axes of the slice: x: 2, y: 2, z: 4, core: 2. Of those that a mesh axis runs over, the one named last changes fastest.
Arguments:
- log_perm: float32 [128, 4, 64, 256], P('member', None, 'tile'), may hold values from -3.4 to 3.4
- start_pressure: float32 [4, 64, 256], P(None, 'tile'), may hold values from -5 to 5
- start_sat: float32 [4, 64, 256], P(None, 'tile'), may hold values from 0.1 to 0.9
- source: float32 [4, 64, 256], P(None, 'tile'), may hold values from -5 to 5
- storage: float32 [4, 64, 256], P(None, 'tile'), may hold values from 0.05 to 0.5
- well_press: float32 [256], replicated, may hold values from -4 to 4
- perf_cell: int32 [2048], P('tile'), may hold values from 0 to 8191
- perf_well: int32 [2048], P('tile'), may hold values from 0 to 255
- perf_count: int32 [8], P('tile'), may hold values from 64 to 256, as said below
- observed: float32 [256], replicated, may hold values from -8 to 8
- obs_var: float32 [256], replicated, may hold values from 0.5 to 5
- obs_noise: float32 [128, 256], P('member'), may hold values from -5 to 5
Outputs:
- new_log_perm: float32 [128, 4, 64, 256], P('member', None, 'tile')
- pressure: float32 [128, 4, 64, 256], P('member', None, 'tile')
- saturation: float32 [128, 4, 64, 256], P('member', None, 'tile')
- well_rates: float32 [128, 256], P('member', 'tile')
The draws below stay inside these ranges and needn't reach their ends.
Inputs may be any that keep to these rules, and one draw needn't show every extreme that they name: `perf_count`: one strip has all 256 slots live.
All inputs are finite; a program needn't handle non-finite values.
Results may differ from the reference program's by a relative error of at most 0.017.
Values may be sent and summed in bfloat16 or wider, within the bound.
No kernel may reach another device: no remote copies, remote signals or barrier semaphores. Data moves between devices by JAX's collectives and lax.ppermute only.
A program may use at most 64 MiB of HBM per device.

```python
import math
import jax
import jax.numpy as jnp
from jax import lax

LAYERS = 4
CX = 8
NY = 256
PERF_DEV = 256
SWEEPS = 2
MEMBERS = 128
NX = 64
WELLS = 256
PERFS = 2048
N_TILE = 8


def draw_log_perm(key, part):
    mean_key = jax.random.fold_in(key, 11)
    member_key = jax.random.fold_in(key, 12)
    trend_field = jax.random.uniform(mean_key, (LAYERS, NX, NY), jnp.float32, -1.0, 1.0)
    deviation = jnp.clip(0.6 * jax.random.normal(member_key, (MEMBERS, LAYERS, NX, NY), jnp.float32), -2.4, 2.4)
    return trend_field[None] + deviation


def draw_perf_count(key, part):
    counts = jax.random.randint(jax.random.fold_in(key, 21), (N_TILE,), PERF_DEV // 4, PERF_DEV + 1)
    full_tile = jax.random.randint(jax.random.fold_in(key, 22), (), 0, N_TILE)
    return jnp.where(jnp.arange(N_TILE) == full_tile, PERF_DEV, counts).astype(jnp.int32)


def plant(result, own_key, least, top_value):
    dims = result.shape
    index_at = [jax.random.randint(jax.random.fold_in(own_key, axis), (), 0, dims[axis]) for axis in range(len(dims))]
    result = result.at[tuple(index_at)].set(least)
    longest = dims.index(max(dims))
    index_at[longest] = (index_at[longest] + 1) % dims[longest]
    return result.at[tuple(index_at)].set(top_value)


def steps_of(rng, shape, cuts, least, top_value):
    factor_of, own = 1.0, jax.random.fold_in(rng, 6)
    for axis_at, shards_of in cuts:
        draws = jnp.exp(jax.random.uniform(jax.random.fold_in(own, axis_at), (shards_of,), jnp.float32, least / len(cuts), top_value / len(cuts)))
        factor_of = factor_of * jnp.repeat(draws, shape[axis_at] // shards_of).reshape([-1 if axis == axis_at else 1 for axis in range(len(shape))])
    return factor_of


def centred(stream_key, shape, scale, bound, shards=(), kind=jnp.bfloat16):
    values = scale * jax.random.normal(stream_key, shape, jnp.float32)
    if shards:
        values = values * steps_of(stream_key, shape, shards, -0.22, 0.18)
    return jnp.clip(values, -bound, bound).astype(kind)


def setup_inputs(seed: int = 0) -> dict:
    arg_keys = jax.random.split(jax.random.key(seed), 13)
    log_perm = draw_log_perm(jax.random.fold_in(arg_keys[12], 71), 0)
    start_pressure = centred(arg_keys[1], (LAYERS, NX, NY), 1.0, 5.0, ((1, 8),), jnp.float32)
    start_sat = jnp.clip(0.1 + 0.79999997 * jax.random.uniform(arg_keys[2], (LAYERS, NX, NY), jnp.float32) ** steps_of(arg_keys[2], (LAYERS, NX, NY), ((1, 8),), -0.2, 0.2), 0.1, 0.9)
    source = centred(arg_keys[3], (LAYERS, NX, NY), 1.0, 5.0, ((1, 8),), jnp.float32)
    storage = jnp.clip(jnp.exp(math.log(0.5) - 2.3025851 * jax.random.uniform(arg_keys[4], (LAYERS, NX, NY), jnp.float32) ** steps_of(arg_keys[4], (LAYERS, NX, NY), ((1, 8),), -0.2, 0.2)), 0.05, 0.5)
    well_press = centred(arg_keys[5], (WELLS,), 1.0, 4.0, (), jnp.float32)
    perf_cell = plant(jax.random.randint(arg_keys[6], (PERFS,), 0, LAYERS * CX * NY), jax.random.fold_in(arg_keys[6], 1), 0, (LAYERS * CX * NY) - 1).astype(jnp.int32)
    perf_well = plant(jax.random.randint(arg_keys[7], (PERFS,), 0, WELLS), jax.random.fold_in(arg_keys[7], 1), 0, WELLS - 1).astype(jnp.int32)
    perf_count = draw_perf_count(jax.random.fold_in(arg_keys[12], 71), 0)
    observed = centred(arg_keys[9], (WELLS,), 2.0, 8.0, (), jnp.float32)
    obs_var = jnp.clip(jnp.exp(jax.random.uniform(arg_keys[10], (WELLS,), jnp.float32, math.log(0.5), math.log(5.0))), 0.5, 5.0)
    obs_noise = centred(arg_keys[11], (MEMBERS, WELLS), 1.0, 5.0, ((0, 4),), jnp.float32)
    return dict(log_perm=log_perm, start_pressure=start_pressure, start_sat=start_sat, source=source, storage=storage, well_press=well_press, perf_cell=perf_cell, perf_well=perf_well, perf_count=perf_count, observed=observed, obs_var=obs_var, obs_noise=obs_noise)


VERTICAL = 0.5
VISCOSITY_RATIO = 2.0
STEP_COEF = 0.1
INFLATION = 4.0

def harmonic(lower_val, upper_val):
    return 2.0 * lower_val * upper_val / (lower_val + upper_val)

def pad_face(values_in, along_dim, before):
    widths = [(0, 0)] * values_in.ndim
    widths[along_dim] = (1, 0) if before else (0, 1)
    return jnp.pad(values_in, widths)

def slide_by(values_in, along_dim, before):
    extent = values_in.shape[along_dim]
    if before:
        remain = lax.slice_in_dim(values_in, 0, extent - 1, axis=along_dim)
    else:
        remain = lax.slice_in_dim(values_in, 1, extent, axis=along_dim)
    return pad_face(remain, along_dim, before)

def face_terms(permeab, inside):
    face_x = harmonic(permeab[:, :, :-1, :], permeab[:, :, 1:, :]) * (inside[:-1] * inside[1:])[:, None]
    face_y = harmonic(permeab[:, :, :, :-1], permeab[:, :, :, 1:])
    face_z = VERTICAL * harmonic(permeab[:, :-1], permeab[:, 1:])
    return (face_x, face_y, face_z)

def neighbours(face_sets, values_in):
    flow_sum = 0.0
    weight_sum = 0.0
    for faces_dim, along_dim in zip(face_sets, (2, 3, 1)):
        lower = pad_face(faces_dim, along_dim, True)
        upper = pad_face(faces_dim, along_dim, False)
        flow_sum = flow_sum + lower * slide_by(values_in, along_dim, True) + upper * slide_by(values_in, along_dim, False)
        weight_sum = weight_sum + lower + upper
    return (flow_sum, weight_sum)

def jacobi(pressure, baseline, storage_term, face_sets):
    flow_sum, weight_sum = neighbours(face_sets, pressure)
    return (baseline + flow_sum) / (storage_term + weight_sum)

def water_frac(values_in):
    squared = values_in * values_in
    return squared / (squared + VISCOSITY_RATIO * (1.0 - values_in) * (1.0 - values_in))

def transport(pressure, saturation, face_sets):
    fraction = water_frac(saturation)
    change = 0.0
    for faces_dim, along_dim in zip(face_sets, (2, 3, 1)):
        extent = pressure.shape[along_dim]
        lower_press = lax.slice_in_dim(pressure, 0, extent - 1, axis=along_dim)
        upper_press = lax.slice_in_dim(pressure, 1, extent, axis=along_dim)
        lower_frac = lax.slice_in_dim(fraction, 0, extent - 1, axis=along_dim)
        upper_frac = lax.slice_in_dim(fraction, 1, extent, axis=along_dim)
        velocity = faces_dim * (lower_press - upper_press)
        carried = velocity * jnp.where(velocity > 0, lower_frac, upper_frac)
        change = change + pad_face(carried, along_dim, True) - pad_face(carried, along_dim, False)
    return saturation + STEP_COEF * change

def solve_spd(gram_matrix, cross_matrix):
    factor = jnp.linalg.cholesky(gram_matrix + jnp.eye(gram_matrix.shape[0], dtype=jnp.float32))
    halfway = lax.linalg.triangular_solve(factor, cross_matrix, left_side=True, lower=True)
    return lax.linalg.triangular_solve(factor, halfway, left_side=True, lower=True, transpose_a=True)

def reference(log_perm, start_pressure, start_sat, source, storage, well_press, perf_cell, perf_well, perf_count, observed, obs_var, obs_noise):
    permeab = jnp.exp(log_perm)
    face_sets = face_terms(permeab, jnp.ones((NX,), jnp.float32))
    baseline = (source + storage * start_pressure)[None]
    storage_term = storage[None]
    pressure = jnp.broadcast_to(start_pressure[None], log_perm.shape)
    for sweep_idx in range(SWEEPS):
        pressure = jacobi(pressure, baseline, storage_term, face_sets)
    saturation = transport(pressure, start_sat[None], face_sets)

    def by_strip(values_in):
        shaped = values_in.reshape(MEMBERS, LAYERS, N_TILE, CX, NY).transpose(0, 2, 1, 3, 4)
        return shaped.reshape(MEMBERS, N_TILE, LAYERS * CX * NY)
    mobility = by_strip(permeab * water_frac(saturation))
    cell_press = by_strip(pressure)
    slots = jnp.arange(PERFS, dtype=jnp.int32)
    owner_tile = slots // PERF_DEV
    live_mask = (slots % PERF_DEV < perf_count[owner_tile]).astype(jnp.float32)
    perf_mob = mobility[:, owner_tile, perf_cell]
    perf_press = cell_press[:, owner_tile, perf_cell]
    perf_terms = perf_mob * (perf_press - well_press[perf_well][None]) * live_mask[None]
    well_rates = jax.ops.segment_sum(perf_terms.T, perf_well, num_segments=WELLS).T
    member_root = (MEMBERS - 1) ** 0.5
    spread = jnp.sqrt(INFLATION * obs_var)
    mean_rate = lax.optimization_barrier(jnp.sum(well_rates, 0)) / MEMBERS
    scaled = (well_rates - mean_rate) / (spread * member_root)
    innovation = (observed - well_rates) / spread + obs_noise
    gram_matrix = jnp.dot(scaled.astype(jnp.float32), scaled.T.astype(jnp.float32), precision=lax.Precision.HIGHEST, preferred_element_type=jnp.float32)
    cross_matrix = jnp.dot(scaled.astype(jnp.float32), innovation.T.astype(jnp.float32), precision=lax.Precision.HIGHEST, preferred_element_type=jnp.float32)
    weights_low = solve_spd(gram_matrix, cross_matrix).astype(jnp.bfloat16)
    anomaly = (log_perm / member_root).astype(jnp.bfloat16)
    update_sum = jnp.dot(weights_low.astype(jnp.float32).T, anomaly.astype(jnp.float32).reshape(MEMBERS, -1), precision=lax.Precision.HIGHEST)
    new_log_perm = log_perm + update_sum.reshape(log_perm.shape)
    return (new_log_perm, pressure, saturation, well_rates)
```

```python
import jax
import jax.numpy as jnp
from jax import lax
from jax.sharding import PartitionSpec as P

SWEEPS = 2


VERTICAL = 0.5
VISCOSITY_RATIO = 2.0
STEP_COEF = 0.1
INFLATION = 4.0


def halo_rows(block, axis, dim, width):
    count = lax.axis_size(axis)
    forward = [(i, i + 1) for i in range(count - 1)]
    backward = [(target, source) for source, target in forward]
    low = lax.ppermute(
        lax.slice_in_dim(block, block.shape[dim] - width, None, axis=dim), axis, forward
    )
    high = lax.ppermute(lax.slice_in_dim(block, 0, width, axis=dim), axis, backward)
    return low.astype(jnp.float32), high.astype(jnp.float32)


def harmonic(lower_val, upper_val):
    return 2.0 * lower_val * upper_val / (lower_val + upper_val)


def pad_face(values_in, along_dim, before):
    widths = [(0, 0)] * values_in.ndim
    widths[along_dim] = (1, 0) if before else (0, 1)
    return jnp.pad(values_in, widths)


def slide_by(values_in, along_dim, before):
    extent = values_in.shape[along_dim]
    if before:
        remain = lax.slice_in_dim(values_in, 0, extent - 1, axis=along_dim)
    else:
        remain = lax.slice_in_dim(values_in, 1, extent, axis=along_dim)
    return pad_face(remain, along_dim, before)


def face_terms(permeab, inside):
    face_x = (
        harmonic(permeab[:, :, :-1, :], permeab[:, :, 1:, :]) * (inside[:-1] * inside[1:])[:, None]
    )
    face_y = harmonic(permeab[:, :, :, :-1], permeab[:, :, :, 1:])
    face_z = VERTICAL * harmonic(permeab[:, :-1], permeab[:, 1:])
    return (face_x, face_y, face_z)


def neighbours(face_sets, values_in):
    flow_sum = 0.0
    weight_sum = 0.0
    for faces_dim, along_dim in zip(face_sets, (2, 3, 1)):
        lower = pad_face(faces_dim, along_dim, True)
        upper = pad_face(faces_dim, along_dim, False)
        flow_sum = (
            flow_sum
            + lower * slide_by(values_in, along_dim, True)
            + upper * slide_by(values_in, along_dim, False)
        )
        weight_sum = weight_sum + lower + upper
    return (flow_sum, weight_sum)


def jacobi(pressure, baseline, storage_term, face_sets):
    flow_sum, weight_sum = neighbours(face_sets, pressure)
    return (baseline + flow_sum) / (storage_term + weight_sum)


def water_frac(values_in):
    squared = values_in * values_in
    return squared / (squared + VISCOSITY_RATIO * (1.0 - values_in) * (1.0 - values_in))


def transport(pressure, saturation, face_sets):
    fraction = water_frac(saturation)
    change = 0.0
    for faces_dim, along_dim in zip(face_sets, (2, 3, 1)):
        extent = pressure.shape[along_dim]
        lower_press = lax.slice_in_dim(pressure, 0, extent - 1, axis=along_dim)
        upper_press = lax.slice_in_dim(pressure, 1, extent, axis=along_dim)
        lower_frac = lax.slice_in_dim(fraction, 0, extent - 1, axis=along_dim)
        upper_frac = lax.slice_in_dim(fraction, 1, extent, axis=along_dim)
        velocity = faces_dim * (lower_press - upper_press)
        carried = velocity * jnp.where(velocity > 0, lower_frac, upper_frac)
        change = change + pad_face(carried, along_dim, True) - pad_face(carried, along_dim, False)
    return saturation + STEP_COEF * change


def solve_spd(gram_matrix, cross_matrix):
    factor = jnp.linalg.cholesky(gram_matrix + jnp.eye(gram_matrix.shape[0], dtype=jnp.float32))
    halfway = lax.linalg.triangular_solve(factor, cross_matrix, left_side=True, lower=True)
    return lax.linalg.triangular_solve(
        factor, halfway, left_side=True, lower=True, transpose_a=True
    )


def trim_rim(values_in, rim_cut):
    return values_in[:, :, rim_cut : values_in.shape[2] - rim_cut, :]


def per_device(
    log_perm,
    start_pressure,
    start_sat,
    source,
    storage,
    well_press,
    perf_cell,
    perf_well,
    perf_count,
    observed,
    obs_var,
    obs_noise,
):
    local_count, layers, strip_width, strip_depth = log_perm.shape
    tile_count = lax.axis_size("tile")
    members = local_count * lax.axis_size("member")
    well_count = well_press.shape[0]
    well_share = well_count // tile_count
    tile_rank = lax.axis_index("tile")
    member_rank = lax.axis_index("member")
    rim = SWEEPS + 1
    fields = jnp.stack([start_pressure, start_sat, source, storage])
    packed = jnp.concatenate([log_perm, fields], axis=0).astype(jnp.bfloat16)
    low, high = halo_rows(packed, "tile", 2, rim)
    wide_perm = jnp.concatenate([low[:local_count], log_perm, high[:local_count]], axis=2)
    wide_fields = jnp.concatenate([low[local_count:], fields, high[local_count:]], axis=2)
    wide_press, wide_sat, wide_source, wide_storage = (wide_fields[i] for i in range(4))
    anomaly = (log_perm / (members - 1) ** 0.5).astype(jnp.bfloat16).reshape(local_count, -1)
    anomaly_all = lax.all_gather(anomaly, "member", axis=0, tiled=True)
    permeab = jnp.exp(wide_perm)
    column = tile_rank * strip_width - rim + jnp.arange(strip_width + 2 * rim, dtype=jnp.int32)
    inside = ((column >= 0) & (column < strip_width * tile_count)).astype(jnp.float32)
    face_sets = face_terms(permeab, inside)
    baseline = (wide_source + wide_storage * wide_press)[None]
    storage_term = jnp.where(inside[:, None] > 0, wide_storage, 1.0)[None]
    extended = jnp.broadcast_to(wide_press[None], wide_perm.shape)
    for sweep_idx in range(SWEEPS):
        extended = jacobi(extended, baseline, storage_term, face_sets)
    pressure = trim_rim(extended, rim)
    saturation = trim_rim(transport(extended, wide_sat[None], face_sets), rim)
    permeab = trim_rim(permeab, rim)
    cell_count = layers * strip_width * strip_depth
    mobility = (permeab * water_frac(saturation)).reshape(local_count, cell_count)
    cell_press = pressure.reshape(local_count, cell_count)
    perf_mob = jnp.take(mobility, perf_cell, axis=1)
    perf_press = jnp.take(cell_press, perf_cell, axis=1)
    selector = (perf_well[:, None] == jnp.arange(well_count, dtype=jnp.int32)[None, :]).astype(
        jnp.float32
    )
    perf_bhp = jnp.dot(selector, well_press, precision=lax.Precision.HIGHEST)
    live_mask = (jnp.arange(perf_cell.shape[0], dtype=jnp.int32) < perf_count[0]).astype(
        jnp.float32
    )
    perf_terms = perf_mob * (perf_press - perf_bhp[None]) * live_mask[None]
    partial_rates = jnp.dot(
        perf_terms, selector, precision=lax.Precision.HIGHEST, preferred_element_type=jnp.float32
    )
    member_root = (members - 1) ** 0.5
    spread = jnp.sqrt(INFLATION * obs_var)
    traded = lax.all_to_all(
        partial_rates.reshape(local_count, tile_count, well_share).transpose(1, 0, 2), "tile", 0, 0
    )
    well_rates = jnp.sum(traded, 0)
    every = lax.all_gather(well_rates, ("member", "tile"), axis=0)
    every = every.reshape(members // local_count, tile_count, local_count, well_share)
    rates_all = every.transpose(0, 2, 1, 3).reshape(members, well_count)
    mean_rate = jnp.sum(rates_all, 0) / members
    scaled = (rates_all - mean_rate) / (spread * member_root)
    gram_matrix = jnp.dot(
        scaled, scaled.T, precision=lax.Precision.HIGHEST, preferred_element_type=jnp.float32
    )
    own_rates = lax.dynamic_slice_in_dim(rates_all, member_rank * local_count, local_count, 0)
    own_innov = (observed - own_rates) / spread + obs_noise
    cross_matrix = jnp.dot(
        scaled, own_innov.T, precision=lax.Precision.HIGHEST, preferred_element_type=jnp.float32
    )
    weights_low = solve_spd(gram_matrix, cross_matrix).astype(jnp.bfloat16)
    contract = (((0,), (0,)), ((), ()))
    update_sum = lax.dot_general(
        weights_low, anomaly_all, contract, preferred_element_type=jnp.float32
    )
    new_log_perm = log_perm + update_sum.reshape(log_perm.shape)
    return (new_log_perm, pressure, saturation, well_rates)


def solution(mesh):
    return jax.shard_map(
        per_device,
        mesh=mesh,
        in_specs=(
            P("member", None, "tile", None),
            P(None, "tile", None),
            P(None, "tile", None),
            P(None, "tile", None),
            P(None, "tile", None),
            P(),
            P("tile"),
            P("tile"),
            P("tile"),
            P(),
            P(),
            P("member", None),
        ),
        out_specs=(
            P("member", None, "tile", None),
            P("member", None, "tile", None),
            P("member", None, "tile", None),
            P("member", "tile"),
        ),
        check_vma=False,
    )
```

```python
import jax
import jax.numpy as jnp
from jax import lax
from jax.experimental import pallas as pl
from jax.experimental.pallas import tpu as pltpu
from jax.sharding import PartitionSpec as P

SWEEPS = 2


VERTICAL = 0.5
VISCOSITY_RATIO = 2.0
STEP_COEF = 0.1
INFLATION = 4.0


def halo_rows(block, axis, dim, width):
    count = lax.axis_size(axis)
    forward = [(i, i + 1) for i in range(count - 1)]
    backward = [(target, source) for source, target in forward]
    low = lax.ppermute(
        lax.slice_in_dim(block, block.shape[dim] - width, None, axis=dim), axis, forward
    )
    high = lax.ppermute(lax.slice_in_dim(block, 0, width, axis=dim), axis, backward)
    return low.astype(jnp.float32), high.astype(jnp.float32)


def harmonic(lower_val, upper_val):
    return 2.0 * lower_val * upper_val / (lower_val + upper_val)


def pad_face(values_in, along_dim, before):
    widths = [(0, 0)] * values_in.ndim
    widths[along_dim] = (1, 0) if before else (0, 1)
    return jnp.pad(values_in, widths)


def slide_by(values_in, along_dim, before):
    extent = values_in.shape[along_dim]
    if before:
        remain = lax.slice_in_dim(values_in, 0, extent - 1, axis=along_dim)
    else:
        remain = lax.slice_in_dim(values_in, 1, extent, axis=along_dim)
    return pad_face(remain, along_dim, before)


def face_terms(permeab, inside):
    face_x = (
        harmonic(permeab[:, :, :-1, :], permeab[:, :, 1:, :]) * (inside[:-1] * inside[1:])[:, None]
    )
    face_y = harmonic(permeab[:, :, :, :-1], permeab[:, :, :, 1:])
    face_z = VERTICAL * harmonic(permeab[:, :-1], permeab[:, 1:])
    return (face_x, face_y, face_z)


def neighbours(face_sets, values_in):
    flow_sum = 0.0
    weight_sum = 0.0
    for faces_dim, along_dim in zip(face_sets, (2, 3, 1)):
        lower = pad_face(faces_dim, along_dim, True)
        upper = pad_face(faces_dim, along_dim, False)
        flow_sum = (
            flow_sum
            + lower * slide_by(values_in, along_dim, True)
            + upper * slide_by(values_in, along_dim, False)
        )
        weight_sum = weight_sum + lower + upper
    return (flow_sum, weight_sum)


def jacobi(pressure, baseline, storage_term, face_sets):
    flow_sum, weight_sum = neighbours(face_sets, pressure)
    return (baseline + flow_sum) / (storage_term + weight_sum)


def water_frac(values_in):
    squared = values_in * values_in
    return squared / (squared + VISCOSITY_RATIO * (1.0 - values_in) * (1.0 - values_in))


def transport(pressure, saturation, face_sets):
    fraction = water_frac(saturation)
    change = 0.0
    for faces_dim, along_dim in zip(face_sets, (2, 3, 1)):
        extent = pressure.shape[along_dim]
        lower_press = lax.slice_in_dim(pressure, 0, extent - 1, axis=along_dim)
        upper_press = lax.slice_in_dim(pressure, 1, extent, axis=along_dim)
        lower_frac = lax.slice_in_dim(fraction, 0, extent - 1, axis=along_dim)
        upper_frac = lax.slice_in_dim(fraction, 1, extent, axis=along_dim)
        velocity = faces_dim * (lower_press - upper_press)
        carried = velocity * jnp.where(velocity > 0, lower_frac, upper_frac)
        change = change + pad_face(carried, along_dim, True) - pad_face(carried, along_dim, False)
    return saturation + STEP_COEF * change


PANEL = 8


def invert_panel(columns):
    row = lax.broadcasted_iota(jnp.int32, columns[0].shape, 0)
    columns = list(columns)
    for k in range(PANEL):
        inverse = 1.0 / columns[k][k : k + 1]
        pivot = columns[k]
        for j in range(PANEL):
            if j != k:
                factor = columns[j][k : k + 1] * inverse
                columns[j] = jnp.where(row == k, factor, columns[j] - pivot * factor)
        columns[k] = jnp.where(row == k, inverse, -pivot * inverse)
    return columns


def solve_blocks(gram_matrix, cross_matrix):
    size = gram_matrix.shape[0]
    count = size // PANEL
    row = lax.broadcasted_iota(jnp.int32, gram_matrix.shape, 0)
    lane = lax.broadcasted_iota(jnp.int32, gram_matrix.shape, 1)
    full = gram_matrix + (row == lane).astype(jnp.float32)
    left = [full[i * PANEL : (i + 1) * PANEL] for i in range(count)]
    right = [cross_matrix[i * PANEL : (i + 1) * PANEL] for i in range(count)]
    width = cross_matrix.shape[1]
    for p in range(count):
        columns = [
            [
                jnp.broadcast_to(left[i][:, p * PANEL + j : p * PANEL + j + 1], (PANEL, size))
                for j in range(PANEL)
            ]
            for i in range(count)
        ]
        inverse = invert_panel(columns[p])
        new_left = sum(inverse[j] * left[p][j : j + 1] for j in range(PANEL))
        new_right = sum(inverse[j][:, :width] * right[p][j : j + 1] for j in range(PANEL))
        for i in range(count):
            if i != p:
                for j in range(PANEL):
                    if p + 1 < count:
                        left[i] = left[i] - columns[i][j] * new_left[j : j + 1]
                    right[i] = right[i] - columns[i][j][:, :width] * new_right[j : j + 1]
        left[p], right[p] = new_left, new_right
    return jnp.concatenate(right, axis=0)


def weights_kernel(rates_ref, own_ref, noise_ref, observed_ref, var_ref, out_ref):
    rates = rates_ref[...]
    members = rates.shape[0]
    spread = jnp.sqrt(INFLATION * var_ref[...])
    mean_rate = jnp.sum(rates, 0, keepdims=True) / members
    scaled = (rates - mean_rate) / (spread * (members - 1) ** 0.5)
    innovation = (observed_ref[...] - own_ref[...]) / spread + noise_ref[...]
    contract = (((1,), (1,)), ((), ()))
    gram_matrix, cross_matrix = (
        lax.dot_general(
            scaled, other, contract, precision=lax.Precision.HIGHEST,
            preferred_element_type=jnp.float32,
        )
        for other in (scaled, innovation)
    )
    out_ref[...] = solve_blocks(gram_matrix, cross_matrix).astype(jnp.bfloat16)


def trim_rim(values_in, rim_cut):
    return values_in[:, :, rim_cut : values_in.shape[2] - rim_cut, :]


def per_device(
    log_perm,
    start_pressure,
    start_sat,
    source,
    storage,
    well_press,
    perf_cell,
    perf_well,
    perf_count,
    observed,
    obs_var,
    obs_noise,
):
    local_count, layers, strip_width, strip_depth = log_perm.shape
    tile_count = lax.axis_size("tile")
    members = local_count * lax.axis_size("member")
    well_count = well_press.shape[0]
    well_share = well_count // tile_count
    tile_rank = lax.axis_index("tile")
    member_rank = lax.axis_index("member")
    rim = SWEEPS + 1
    fields = jnp.stack([start_pressure, start_sat, source, storage])
    packed = jnp.concatenate([log_perm, fields], axis=0).astype(jnp.bfloat16)
    low, high = halo_rows(packed, "tile", 2, rim)
    wide_perm = jnp.concatenate([low[:local_count], log_perm, high[:local_count]], axis=2)
    wide_fields = jnp.concatenate([low[local_count:], fields, high[local_count:]], axis=2)
    wide_press, wide_sat, wide_source, wide_storage = (wide_fields[i] for i in range(4))
    anomaly = (log_perm / (members - 1) ** 0.5).astype(jnp.bfloat16).reshape(local_count, -1)
    anomaly_all = lax.all_gather(anomaly, "member", axis=0, tiled=True)
    permeab = jnp.exp(wide_perm)
    column = tile_rank * strip_width - rim + jnp.arange(strip_width + 2 * rim, dtype=jnp.int32)
    inside = ((column >= 0) & (column < strip_width * tile_count)).astype(jnp.float32)
    face_sets = face_terms(permeab, inside)
    baseline = (wide_source + wide_storage * wide_press)[None]
    storage_term = jnp.where(inside[:, None] > 0, wide_storage, 1.0)[None]
    extended = jnp.broadcast_to(wide_press[None], wide_perm.shape)
    for sweep_idx in range(SWEEPS):
        extended = jacobi(extended, baseline, storage_term, face_sets)
    pressure = trim_rim(extended, rim)
    saturation = trim_rim(transport(extended, wide_sat[None], face_sets), rim)
    permeab = trim_rim(permeab, rim)
    cell_count = layers * strip_width * strip_depth
    mobility = (permeab * water_frac(saturation)).reshape(local_count, cell_count)
    cell_press = pressure.reshape(local_count, cell_count)
    perf_mob = jnp.take(mobility, perf_cell, axis=1)
    perf_press = jnp.take(cell_press, perf_cell, axis=1)
    selector = (perf_well[:, None] == jnp.arange(well_count, dtype=jnp.int32)[None, :]).astype(
        jnp.float32
    )
    perf_bhp = jnp.dot(selector, well_press, precision=lax.Precision.HIGHEST)
    live_mask = (jnp.arange(perf_cell.shape[0], dtype=jnp.int32) < perf_count[0]).astype(
        jnp.float32
    )
    perf_terms = perf_mob * (perf_press - perf_bhp[None]) * live_mask[None]
    partial_rates = jnp.dot(
        perf_terms, selector, precision=lax.Precision.HIGHEST, preferred_element_type=jnp.float32
    )
    traded = lax.all_to_all(
        jnp.broadcast_to(partial_rates[None], (tile_count,) + partial_rates.shape), "tile", 0, 0
    )
    own_rates = jnp.sum(traded, 0)
    well_rates = lax.dynamic_slice_in_dim(own_rates, tile_rank * well_share, well_share, 1)
    rates_all = lax.all_gather(own_rates, "member", axis=0, tiled=True)
    weights_low = pl.pallas_call(
        weights_kernel,
        out_shape=jax.ShapeDtypeStruct((members, local_count), jnp.bfloat16),
        compiler_params=pltpu.CompilerParams(vmem_limit_bytes=32 * 2**20),
        cost_estimate=pl.CostEstimate(
            flops=12 * members**3, bytes_accessed=8 * members * well_count, transcendentals=0
        ),
    )(rates_all, own_rates, obs_noise, observed[None], obs_var[None])
    contract = (((0,), (0,)), ((), ()))
    update_sum = lax.dot_general(
        weights_low, anomaly_all, contract, preferred_element_type=jnp.float32
    )
    new_log_perm = log_perm + update_sum.reshape(log_perm.shape)
    return (new_log_perm, pressure, saturation, well_rates)


def solution(mesh):
    return jax.shard_map(
        per_device,
        mesh=mesh,
        in_specs=(
            P("member", None, "tile", None),
            P(None, "tile", None),
            P(None, "tile", None),
            P(None, "tile", None),
            P(None, "tile", None),
            P(),
            P("tile"),
            P("tile"),
            P("tile"),
            P(),
            P(),
            P("member", None),
        ),
        out_specs=(
            P("member", None, "tile", None),
            P("member", None, "tile", None),
            P("member", None, "tile", None),
            P("member", "tile"),
        ),
        check_vma=False,
    )
```

```python
import functools

import jax
import jax.numpy as jnp
from jax import lax
from jax.experimental import pallas as pl
from jax.experimental.pallas import tpu as pltpu
from jax.sharding import PartitionSpec as P

SWEEPS = 2
RIM = SWEEPS + 1


VERTICAL = 0.5
VISCOSITY_RATIO = 2.0
STEP_COEF = 0.1
INFLATION = 4.0
PANEL = 8
GROUP = 16
LANES = 128


def fold(array):
    members, layers, width, depth = array.shape
    array = array.reshape(members, layers, width, depth // LANES, LANES)
    return array.transpose(0, 1, 3, 2, 4).reshape(-1, LANES)


def unfold(rows, shape):
    members, layers, width, depth = shape
    array = rows.reshape(members, layers, depth // LANES, width, LANES)
    return array.transpose(0, 1, 3, 2, 4).reshape(shape)


def load_rows(ref, count, layer, x, layers, width, halves):
    return jnp.concatenate(
        [
            ref[pl.ds((layer * halves + h) * width + x, count, stride=layers * width * halves), :]
            for h in range(halves)
        ],
        axis=1,
    )


def store_rows(ref, values, count, layer, x, layers, width, halves):
    for h in range(halves):
        at = pl.ds((layer * halves + h) * width + x, count, stride=layers * width * halves)
        ref[at, :] = values[:, h * LANES : (h + 1) * LANES]


def send_both(up_rows, down_rows, axis):
    count = lax.axis_size(axis)
    forward = [(i, i + 1) for i in range(count - 1)]
    backward = [(target, source) for source, target in forward]
    return lax.ppermute(up_rows, axis, forward), lax.ppermute(down_rows, axis, backward)


def reciprocal(values_in):
    guess = pl.reciprocal(values_in, approx=True)
    return guess * (2.0 - values_in * guess)


def water_frac(values_in):
    squared = values_in * values_in
    rest = 1.0 - values_in
    return squared * reciprocal(squared + VISCOSITY_RATIO * rest * rest)


def pack_kernel(dims, root, perm_ref, *refs):
    local_count, layers, width = dims
    field_refs, (up_ref, down_ref, anomaly_ref, up_rows, down_rows) = refs[:4], refs[4:]
    up_rows[...] = jnp.zeros_like(up_rows)
    down_rows[...] = jnp.zeros_like(down_rows)
    for f, field_ref in enumerate(field_refs):
        for layer in range(layers):
            at = f * GROUP + layer * RIM
            first = layer * width
            down_rows[at : at + RIM, :] = field_ref[first : first + RIM, :]
            up_rows[at : at + RIM, :] = field_ref[first + width - RIM : first + width, :]
    halves = anomaly_ref.shape[1] // LANES
    block = RIM * layers * local_count
    up_ref[block:, :] = up_rows[...].astype(jnp.bfloat16)
    down_ref[block:, :] = down_rows[...].astype(jnp.bfloat16)
    for layer in range(layers):
        for x in range(width):
            row = layer * width + x
            values = load_rows(perm_ref, local_count, layer, x, layers, width, halves)
            anomaly_ref[row * local_count : (row + 1) * local_count, :] = (values / root).astype(
                jnp.bfloat16
            )
            low_values = values.astype(jnp.bfloat16)
            if x < RIM:
                at = (x * layers + layer) * local_count
                down_ref[at : at + local_count, :] = low_values
            if x >= width - RIM:
                at = ((x - width + RIM) * layers + layer) * local_count
                up_ref[at : at + local_count, :] = low_values


def physics_kernel(dims, count_ref, rank_ref, perm_ref, low_ref, high_ref, *refs):
    local_count, layers, width, tile_count = dims
    own_refs = refs[:4]
    cell_ref, well_ref, bhp_ref, press_ref, sat_ref, rates_ref, half_inv, face_y = refs[4:12]
    face_x, face_z, inverse, first_press, last_press = refs[12:]
    depth = low_ref.shape[1]
    halves = depth // LANES
    group = pl.program_id(0)
    rim_rows = RIM * layers * local_count
    lane = lax.broadcasted_iota(jnp.int32, (1, depth), 1)
    open_y = (lane < depth - 1).astype(jnp.float32)
    has_low = (rank_ref[0] > 0).astype(jnp.float32)
    has_high = (rank_ref[0] < tile_count - 1).astype(jnp.float32)
    span = width + 2 * RIM

    def slot(r, layer):
        return (r + RIM) * layers + layer

    def ahead(values_in):
        return pltpu.roll(values_in, depth - 1, 1)

    def behind(values_in):
        return pltpu.roll(values_in, 1, 1)

    own = [ref[...] for ref in own_refs]
    rims = [
        [
            ref[rim_rows + f * GROUP : rim_rows + (f + 1) * GROUP, :].astype(jnp.float32)
            for f in range(4)
        ]
        for ref in (low_ref, high_ref)
    ]

    def with_shifts(p0, sat, source, storage):
        frac = water_frac(sat)
        return dict(
            p0=p0, sat=sat, storage=storage, base=source + storage * p0,
            ahead=ahead(p0), behind=behind(p0), frac=frac, frac_ahead=ahead(frac),
        )

    shared = [with_shifts(*fields) for fields in (own, rims[0], rims[1])]

    def field(name, r, layer):
        if 0 <= r < width:
            part, at = shared[0], layer * width + r
        elif r < 0:
            part, at = shared[1], layer * RIM + r + RIM
        else:
            part, at = shared[2], layer * RIM + r - width
        return part[name][at : at + 1, :]

    for r in range(-RIM, width + RIM):
        for layer in range(layers):
            if 0 <= r < width:
                values = load_rows(perm_ref, GROUP, layer, r, layers, width, halves)
            else:
                ref, i = (low_ref, r + RIM) if r < 0 else (high_ref, r - width)
                at = (i * layers + layer) * local_count + group * GROUP
                values = ref[pl.ds(pl.multiple_of(at, GROUP), GROUP), :].astype(jnp.float32)
            half_inv[slot(r, layer)] = 0.5 * jnp.exp(-values)

    for r in range(-RIM, width + RIM - 1):
        for layer in range(layers):
            face = reciprocal(half_inv[slot(r, layer)] + half_inv[slot(r + 1, layer)])
            if r == -1:
                face = face * has_low
            if r == width - 1:
                face = face * has_high
            face_x[slot(r, layer)] = face

    for r in range(1 - RIM, width + RIM - 1):
        for layer in range(layers):
            at = slot(r, layer)
            here = half_inv[at]
            up_y = reciprocal(here + ahead(here)) * open_y
            low_y = behind(up_y)
            face_y[at] = up_y
            low_x, up_x = face_x[slot(r - 1, layer)], face_x[at]
            flow = (
                low_x * field("p0", r - 1, layer)
                + up_x * field("p0", r + 1, layer)
                + up_y * field("ahead", r, layer)
                + low_y * field("behind", r, layer)
            )
            weight = (low_x + up_x) + (up_y + low_y)
            if layer + 1 < layers:
                up_z = VERTICAL * reciprocal(here + half_inv[slot(r, layer + 1)])
                face_z[at] = up_z
                flow = flow + up_z * field("p0", r, layer + 1)
                weight = weight + up_z
            if layer > 0:
                low_z = face_z[slot(r, layer - 1)]
                flow = flow + low_z * field("p0", r, layer - 1)
                weight = weight + low_z
            scale = reciprocal(field("storage", r, layer) + weight)
            inverse[at] = scale
            first_press[at] = (field("base", r, layer) + flow) * scale

    for r in range(-1, width + 1):
        for layer in range(layers):
            at = slot(r, layer)
            here = first_press[at]
            up_y = face_y[at]
            flow = (
                face_x[slot(r - 1, layer)] * first_press[slot(r - 1, layer)]
                + face_x[at] * first_press[slot(r + 1, layer)]
                + up_y * ahead(here)
                + behind(up_y * here)
            )
            if layer + 1 < layers:
                flow = flow + face_z[at] * first_press[slot(r, layer + 1)]
            if layer > 0:
                flow = flow + face_z[slot(r, layer - 1)] * first_press[slot(r, layer - 1)]
            last_press[at] = (field("base", r, layer) + flow) * inverse[at]

    perf_cell = cell_ref[...]
    slots = perf_cell.shape[1]
    parts = slots // LANES
    lane_at = perf_cell % LANES
    row_at = perf_cell // LANES
    lane_of = [
        jnp.broadcast_to(lane_at[:, p * LANES : (p + 1) * LANES], (GROUP, LANES))
        for p in range(parts)
    ]
    row_of = [
        jnp.broadcast_to(row_at[:, p * LANES : (p + 1) * LANES], (GROUP, LANES))
        for p in range(parts)
    ]
    zeros = jnp.zeros((GROUP, LANES), jnp.float32)
    perf_mob, perf_press = [zeros] * parts, [zeros] * parts

    def carried(face, low_press, up_press, low_frac, up_frac):
        velocity = face * (low_press - up_press)
        return velocity * jnp.where(velocity > 0, low_frac, up_frac)

    for layer in range(layers):
        low_x = carried(
            face_x[slot(-1, layer)], last_press[slot(-1, layer)], last_press[slot(0, layer)],
            field("frac", -1, layer), field("frac", 0, layer),
        )
        for r in range(width):
            at = slot(r, layer)
            here = last_press[at]
            frac = field("frac", r, layer)
            up_x = carried(
                face_x[at], here, last_press[slot(r + 1, layer)], frac, field("frac", r + 1, layer)
            )
            up_y = carried(face_y[at], here, ahead(here), frac, field("frac_ahead", r, layer))
            change = (low_x - up_x) + (behind(up_y) - up_y)
            low_x = up_x
            if layer + 1 < layers:
                up_z = carried(
                    face_z[at], here, last_press[slot(r, layer + 1)], frac,
                    field("frac", r, layer + 1),
                )
                change = change - up_z
                first_press[at] = up_z
            if layer > 0:
                change = change + first_press[slot(r, layer - 1)]
            saturation = field("sat", r, layer) + STEP_COEF * change
            row = layer * width + r
            store_rows(press_ref, here, GROUP, layer, r, layers, width, halves)
            store_rows(sat_ref, saturation, GROUP, layer, r, layers, width, halves)
            mobility = water_frac(saturation) * reciprocal(2.0 * half_inv[at])
            for half in range(halves):
                mob_part = mobility[:, half * LANES : (half + 1) * LANES]
                press_part = here[:, half * LANES : (half + 1) * LANES]
                for p in range(parts):
                    mine = row_of[p] == row * halves + half
                    perf_mob[p] = jnp.where(
                        mine, jnp.take_along_axis(mob_part, lane_of[p], axis=1, mode="promise_in_bounds"), perf_mob[p]
                    )
                    perf_press[p] = jnp.where(
                        mine,
                        jnp.take_along_axis(press_part, lane_of[p], axis=1, mode="promise_in_bounds"),
                        perf_press[p],
                    )

    wells = bhp_ref.shape[1]
    chosen = (
        lax.broadcasted_iota(jnp.int32, (wells, slots), 0) == well_ref[...]
    ).astype(jnp.float32)
    bhp = jnp.broadcast_to(bhp_ref[...], (8, wells))
    perf_bhp = jnp.dot(
        bhp, chosen, precision=lax.Precision.HIGHEST, preferred_element_type=jnp.float32
    )[:1]
    live = (lax.broadcasted_iota(jnp.int32, (1, slots), 1) < count_ref[0]).astype(jnp.float32)
    terms = (
        jnp.concatenate(perf_mob, axis=1)
        * (jnp.concatenate(perf_press, axis=1) - perf_bhp)
        * live
    )
    partial_rates = lax.dot_general(
        terms, chosen, (((1,), (1,)), ((), ())), precision=lax.Precision.HIGHEST,
        preferred_element_type=jnp.float32,
    )
    rates_ref[...] = jnp.broadcast_to(partial_rates[None], rates_ref.shape)


def invert_panel(columns):
    row = lax.broadcasted_iota(jnp.int32, columns[0].shape, 0)
    columns = list(columns)
    for k in range(PANEL):
        inverse = 1.0 / columns[k][k : k + 1]
        pivot = columns[k]
        for j in range(PANEL):
            if j != k:
                factor = columns[j][k : k + 1] * inverse
                columns[j] = jnp.where(row == k, factor, columns[j] - pivot * factor)
        columns[k] = jnp.where(row == k, inverse, -pivot * inverse)
    return columns


def solve_blocks(gram_matrix, cross_matrix):
    size = gram_matrix.shape[0]
    count = size // PANEL
    row = lax.broadcasted_iota(jnp.int32, gram_matrix.shape, 0)
    lane = lax.broadcasted_iota(jnp.int32, gram_matrix.shape, 1)
    full = gram_matrix + (row == lane).astype(jnp.float32)
    left = [full[i * PANEL : (i + 1) * PANEL] for i in range(count)]
    right = [cross_matrix[i * PANEL : (i + 1) * PANEL] for i in range(count)]
    width = cross_matrix.shape[1]
    for p in range(count):
        columns = [
            [
                jnp.broadcast_to(left[i][:, p * PANEL + j : p * PANEL + j + 1], (PANEL, size))
                for j in range(PANEL)
            ]
            for i in range(count)
        ]
        inverse = invert_panel(columns[p])
        new_left = sum(inverse[j] * left[p][j : j + 1] for j in range(PANEL))
        new_right = sum(inverse[j][:, :width] * right[p][j : j + 1] for j in range(PANEL))
        for i in range(count):
            if i != p:
                for j in range(PANEL):
                    if p + 1 < count:
                        left[i] = left[i] - columns[i][j] * new_left[j : j + 1]
                    right[i] = right[i] - columns[i][j][:, :width] * new_right[j : j + 1]
        left[p], right[p] = new_left, new_right
    return jnp.concatenate(right, axis=0)


def update_kernel(
    dims, rates_ref, own_ref, noise_ref, observed_ref, var_ref, anomaly_ref, perm_ref, out_ref,
    anomaly_buf, perm_buf, sems,
):
    local_count, layers, width = dims
    rows = layers * width
    halves = anomaly_ref.shape[1] // LANES
    copies = [
        pltpu.make_async_copy(anomaly_ref, anomaly_buf, sems.at[0]),
        pltpu.make_async_copy(perm_ref, perm_buf, sems.at[1]),
    ]
    for copy in copies:
        copy.start()
    rates = rates_ref[...]
    members = rates.shape[0]
    spread = jnp.sqrt(INFLATION * var_ref[...])
    mean_rate = jnp.sum(rates, 0, keepdims=True) / members
    scaled = (rates - mean_rate) / (spread * (members - 1) ** 0.5)
    innovation = (observed_ref[...] - own_ref[...]) / spread + noise_ref[...]
    contract = (((1,), (1,)), ((), ()))
    gram_matrix, cross_matrix = (
        lax.dot_general(
            scaled, other, contract, precision=lax.Precision.HIGHEST,
            preferred_element_type=jnp.float32,
        )
        for other in (scaled, innovation)
    )
    weights = solve_blocks(gram_matrix, cross_matrix).T.astype(jnp.bfloat16)
    for copy in copies:
        copy.wait()
    for row in range(rows):
        layer, x = row // width, row % width
        at = row * local_count
        every = jnp.concatenate(
            [
                anomaly_buf[k * rows * local_count + at : k * rows * local_count + at + local_count, :]
                for k in range(members // local_count)
            ],
            axis=0,
        )
        update = jnp.dot(weights, every, preferred_element_type=jnp.float32)
        place = (local_count, layer, x, layers, width, halves)
        store_rows(out_ref, load_rows(perm_buf, *place) + update, *place)


def per_device(
    log_perm,
    start_pressure,
    start_sat,
    source,
    storage,
    well_press,
    perf_cell,
    perf_well,
    perf_count,
    observed,
    obs_var,
    obs_noise,
):
    local_count, layers, strip_width, strip_depth = log_perm.shape
    tile_count = lax.axis_size("tile")
    members = local_count * lax.axis_size("member")
    well_count = well_press.shape[0]
    well_share = well_count // tile_count
    tile_rank = lax.axis_index("tile")
    rows = layers * strip_width
    slots = perf_cell.shape[0]
    flat_perm = fold(log_perm)
    fields = [
        array.reshape(rows, strip_depth) for array in (start_pressure, start_sat, source, storage)
    ]
    rim_shape = (RIM * layers * local_count + 4 * GROUP, strip_depth)
    field_scratch = pltpu.VMEM((4 * GROUP, strip_depth), jnp.float32)
    params = pltpu.CompilerParams(vmem_limit_bytes=40 * 2**20)
    up_rows, down_rows, anomaly = pl.pallas_call(
        functools.partial(
            pack_kernel, (local_count, layers, strip_width), (members - 1) ** 0.5
        ),
        out_shape=(
            jax.ShapeDtypeStruct(rim_shape, jnp.bfloat16),
            jax.ShapeDtypeStruct(rim_shape, jnp.bfloat16),
            jax.ShapeDtypeStruct((local_count * rows, strip_depth), jnp.bfloat16),
        ),
        scratch_shapes=[field_scratch, field_scratch],
        compiler_params=params,
        cost_estimate=pl.CostEstimate(
            flops=4 * flat_perm.size, bytes_accessed=8 * flat_perm.size, transcendentals=0
        ),
    )(flat_perm, *fields)
    low_rows, high_rows = send_both(up_rows, down_rows, "tile")
    anomaly_all = lax.all_gather(anomaly, "member", axis=0, tiled=True)

    def whole(array):
        return pl.BlockSpec(array.shape, lambda g: (0,) * array.ndim)

    block = pl.BlockSpec((GROUP * rows * (strip_depth // LANES), LANES), lambda g: (g, 0))
    smem = pl.BlockSpec(memory_space=pltpu.SMEM)
    perfs = [perf_cell[None], perf_well[None], well_press[None]]
    span = strip_width + 2 * RIM
    flat_press, flat_sat, partial_rates = pl.pallas_call(
        functools.partial(physics_kernel, (local_count, layers, strip_width, tile_count)),
        grid=(local_count // GROUP,),
        in_specs=[smem, smem, block, whole(low_rows), whole(high_rows)]
        + [whole(array) for array in fields + perfs],
        out_specs=(
            block,
            block,
            pl.BlockSpec((tile_count, GROUP, well_count), lambda g: (0, g, 0)),
        ),
        out_shape=(
            jax.ShapeDtypeStruct(flat_perm.shape, jnp.float32),
            jax.ShapeDtypeStruct(flat_perm.shape, jnp.float32),
            jax.ShapeDtypeStruct((tile_count, local_count, well_count), jnp.float32),
        ),
        scratch_shapes=[pltpu.VMEM((span * layers, GROUP, strip_depth), jnp.float32)] * 7,
        compiler_params=params,
        cost_estimate=pl.CostEstimate(
            flops=200 * flat_perm.size, bytes_accessed=16 * flat_perm.size, transcendentals=0
        ),
    )(perf_count, tile_rank[None], flat_perm, low_rows, high_rows, *fields, *perfs)
    traded = lax.all_to_all(partial_rates, "tile", 0, 0)
    own_rates = jnp.sum(traded, 0)
    well_rates = lax.dynamic_slice_in_dim(own_rates, tile_rank * well_share, well_share, 1)
    rates_all = lax.all_gather(own_rates, "member", axis=0, tiled=True)
    vmem, anywhere = pl.BlockSpec(memory_space=pltpu.VMEM), pl.BlockSpec(memory_space=pl.ANY)
    new_flat = pl.pallas_call(
        functools.partial(update_kernel, (local_count, layers, strip_width)),
        out_shape=jax.ShapeDtypeStruct(flat_perm.shape, jnp.float32),
        in_specs=[vmem] * 5 + [anywhere] * 2,
        out_specs=vmem,
        scratch_shapes=[
            pltpu.VMEM(anomaly_all.shape, jnp.bfloat16),
            pltpu.VMEM(flat_perm.shape, jnp.float32),
            pltpu.SemaphoreType.DMA((2,)),
        ],
        compiler_params=params,
        cost_estimate=pl.CostEstimate(
            flops=12 * members**3, bytes_accessed=16 * flat_perm.size, transcendentals=0
        ),
    )(rates_all, own_rates, obs_noise, observed[None], obs_var[None], anomaly_all, flat_perm)
    new_log_perm = unfold(new_flat, log_perm.shape)
    pressure = unfold(flat_press, log_perm.shape)
    saturation = unfold(flat_sat, log_perm.shape)
    return (new_log_perm, pressure, saturation, well_rates)


def solution(mesh):
    return jax.shard_map(
        per_device,
        mesh=mesh,
        in_specs=(
            P("member", None, "tile", None),
            P(None, "tile", None),
            P(None, "tile", None),
            P(None, "tile", None),
            P(None, "tile", None),
            P(),
            P("tile"),
            P("tile"),
            P("tile"),
            P(),
            P(),
            P("member", None),
        ),
        out_specs=(
            P("member", None, "tile", None),
            P("member", None, "tile", None),
            P("member", None, "tile", None),
            P("member", "tile"),
        ),
        check_vma=False,
    )
```

```python
import functools

import jax
import jax.numpy as jnp
from jax import lax
from jax.experimental import pallas as pl
from jax.experimental.pallas import tpu as pltpu
from jax.sharding import PartitionSpec as P

SWEEPS = 2
RIM = SWEEPS + 1


VERTICAL = 0.5
VISCOSITY_RATIO = 2.0
STEP_COEF = 0.1
INFLATION = 4.0
PANEL = 8
GROUP = 16
LANES = 128


def fold(array):
    members, layers, width, depth = array.shape
    array = array.reshape(members, layers, width, depth // LANES, LANES)
    return array.transpose(0, 1, 3, 2, 4).reshape(-1, LANES)


def unfold(rows, shape):
    members, layers, width, depth = shape
    array = rows.reshape(members, layers, depth // LANES, width, LANES)
    return array.transpose(0, 1, 3, 2, 4).reshape(shape)


def load_rows(ref, count, layer, x, layers, width, halves):
    return jnp.concatenate(
        [
            ref[pl.ds((layer * halves + h) * width + x, count, stride=layers * width * halves), :]
            for h in range(halves)
        ],
        axis=1,
    )


def store_rows(ref, values, count, layer, x, layers, width, halves):
    for h in range(halves):
        at = pl.ds((layer * halves + h) * width + x, count, stride=layers * width * halves)
        ref[at, :] = values[:, h * LANES : (h + 1) * LANES]


def send_both(up_rows, down_rows, axis):
    count = lax.axis_size(axis)
    forward = [(i, i + 1) for i in range(count - 1)]
    backward = [(target, source) for source, target in forward]
    return lax.ppermute(up_rows, axis, forward), lax.ppermute(down_rows, axis, backward)


def sum_over(array, axis):
    count = lax.axis_size(axis)
    stride = count
    while stride > 1:
        radix = 4 if stride % 4 == 0 else 2
        stride //= radix
        groups = [
            [base + low + i * stride for i in range(radix)]
            for base in range(0, count, stride * radix)
            for low in range(stride)
        ]
        array = jnp.sum(lax.all_gather(array, axis, axis_index_groups=groups), 0)
    return array


def reciprocal(values_in):
    guess = pl.reciprocal(values_in, approx=True)
    return guess * (2.0 - values_in * guess)


def pieces(values_in):
    parts = []
    for _ in range(3):
        parts.append(values_in.astype(jnp.bfloat16))
        values_in = values_in - parts[-1].astype(jnp.float32)
    return jnp.concatenate(parts, axis=0)


def water_frac(values_in):
    squared = values_in * values_in
    rest = 1.0 - values_in
    return squared * reciprocal(squared + VISCOSITY_RATIO * rest * rest)


def pack_kernel(dims, root, perm_ref, fields_ref, up_ref, down_ref, anomaly_ref, up_rows, down_rows):
    local_count, layers, width = dims
    up_rows[...] = jnp.zeros_like(up_rows)
    down_rows[...] = jnp.zeros_like(down_rows)
    for f in range(4):
        for layer in range(layers):
            at = f * GROUP + layer * RIM
            first = (f * layers + layer) * width
            down_rows[at : at + RIM, :] = fields_ref[first : first + RIM, :]
            up_rows[at : at + RIM, :] = fields_ref[first + width - RIM : first + width, :]
    halves = anomaly_ref.shape[1] // LANES
    block = RIM * layers * local_count
    up_ref[block:, :] = up_rows[...].astype(jnp.bfloat16)
    down_ref[block:, :] = down_rows[...].astype(jnp.bfloat16)
    for layer in range(layers):
        for x in range(width):
            row = layer * width + x
            values = load_rows(perm_ref, local_count, layer, x, layers, width, halves)
            anomaly_ref[row * local_count : (row + 1) * local_count, :] = (values / root).astype(
                jnp.bfloat16
            )
            low_values = values.astype(jnp.bfloat16)
            if x < RIM:
                at = (x * layers + layer) * local_count
                down_ref[at : at + local_count, :] = low_values
            if x >= width - RIM:
                at = ((x - width + RIM) * layers + layer) * local_count
                up_ref[at : at + local_count, :] = low_values


def physics_kernel(dims, count_ref, rank_ref, perm_ref, low_ref, high_ref, *refs):
    local_count, layers, width, tile_count = dims
    fields_ref, cell_ref, well_ref, bhp_ref, press_ref, sat_ref, rates_ref = refs[:7]
    half_inv, face_y, face_x, face_z, inverse, first_press, last_press = refs[7:]
    depth = low_ref.shape[1]
    halves = depth // LANES
    group = pl.program_id(0)
    rim_rows = RIM * layers * local_count
    lane = lax.broadcasted_iota(jnp.int32, (1, depth), 1)
    open_y = (lane < depth - 1).astype(jnp.float32)
    has_low = (rank_ref[0] > 0).astype(jnp.float32)
    has_high = (rank_ref[0] < tile_count - 1).astype(jnp.float32)
    span = width + 2 * RIM

    def slot(r, layer):
        return (r + RIM) * layers + layer

    def ahead(values_in):
        return pltpu.roll(values_in, depth - 1, 1)

    def behind(values_in):
        return pltpu.roll(values_in, 1, 1)

    own = [fields_ref[f * layers * width : (f + 1) * layers * width, :] for f in range(4)]
    rims = [
        [
            ref[rim_rows + f * GROUP : rim_rows + (f + 1) * GROUP, :].astype(jnp.float32)
            for f in range(4)
        ]
        for ref in (low_ref, high_ref)
    ]

    def with_shifts(p0, sat, source, storage):
        frac = water_frac(sat)
        return dict(
            p0=p0, sat=sat, storage=storage, base=source + storage * p0,
            ahead=ahead(p0), behind=behind(p0), frac=frac, frac_ahead=ahead(frac),
        )

    shared = [with_shifts(*fields) for fields in (own, rims[0], rims[1])]

    def field(name, r, layer):
        if 0 <= r < width:
            part, at = shared[0], layer * width + r
        elif r < 0:
            part, at = shared[1], layer * RIM + r + RIM
        else:
            part, at = shared[2], layer * RIM + r - width
        return part[name][at : at + 1, :]

    for r in range(-RIM, width + RIM):
        for layer in range(layers):
            if 0 <= r < width:
                values = load_rows(perm_ref, GROUP, layer, r, layers, width, halves)
            else:
                ref, i = (low_ref, r + RIM) if r < 0 else (high_ref, r - width)
                at = (i * layers + layer) * local_count + group * GROUP
                values = ref[pl.ds(pl.multiple_of(at, GROUP), GROUP), :].astype(jnp.float32)
            half_inv[slot(r, layer)] = 0.5 * jnp.exp(-values)

    for r in range(-RIM, width + RIM - 1):
        for layer in range(layers):
            face = reciprocal(half_inv[slot(r, layer)] + half_inv[slot(r + 1, layer)])
            if r == -1:
                face = face * has_low
            if r == width - 1:
                face = face * has_high
            face_x[slot(r, layer)] = face

    for r in range(1 - RIM, width + RIM - 1):
        for layer in range(layers):
            at = slot(r, layer)
            here = half_inv[at]
            up_y = reciprocal(here + ahead(here)) * open_y
            low_y = behind(up_y)
            face_y[at] = up_y
            low_x, up_x = face_x[slot(r - 1, layer)], face_x[at]
            flow = (
                low_x * field("p0", r - 1, layer)
                + up_x * field("p0", r + 1, layer)
                + up_y * field("ahead", r, layer)
                + low_y * field("behind", r, layer)
            )
            weight = (low_x + up_x) + (up_y + low_y)
            if layer + 1 < layers:
                up_z = VERTICAL * reciprocal(here + half_inv[slot(r, layer + 1)])
                face_z[at] = up_z
                flow = flow + up_z * field("p0", r, layer + 1)
                weight = weight + up_z
            if layer > 0:
                low_z = face_z[slot(r, layer - 1)]
                flow = flow + low_z * field("p0", r, layer - 1)
                weight = weight + low_z
            scale = reciprocal(field("storage", r, layer) + weight)
            inverse[at] = scale
            first_press[at] = (field("base", r, layer) + flow) * scale

    for r in range(-1, width + 1):
        for layer in range(layers):
            at = slot(r, layer)
            here = first_press[at]
            up_y = face_y[at]
            flow = (
                face_x[slot(r - 1, layer)] * first_press[slot(r - 1, layer)]
                + face_x[at] * first_press[slot(r + 1, layer)]
                + up_y * ahead(here)
                + behind(up_y * here)
            )
            if layer + 1 < layers:
                flow = flow + face_z[at] * first_press[slot(r, layer + 1)]
            if layer > 0:
                flow = flow + face_z[slot(r, layer - 1)] * first_press[slot(r, layer - 1)]
            last_press[at] = (field("base", r, layer) + flow) * inverse[at]

    perf_cell = cell_ref[...]
    slots = perf_cell.shape[1]
    parts = slots // LANES
    lane_at = perf_cell % LANES
    row_at = perf_cell // LANES
    lane_of = [
        jnp.broadcast_to(lane_at[:, p * LANES : (p + 1) * LANES], (GROUP, LANES))
        for p in range(parts)
    ]
    row_of = [
        jnp.broadcast_to(row_at[:, p * LANES : (p + 1) * LANES], (GROUP, LANES))
        for p in range(parts)
    ]
    zeros = jnp.zeros((GROUP, LANES), jnp.float32)
    perf_mob, perf_press = [zeros] * parts, [zeros] * parts

    def carried(face, low_press, up_press, low_frac, up_frac):
        velocity = face * (low_press - up_press)
        return velocity * jnp.where(velocity > 0, low_frac, up_frac)

    for layer in range(layers):
        low_x = carried(
            face_x[slot(-1, layer)], last_press[slot(-1, layer)], last_press[slot(0, layer)],
            field("frac", -1, layer), field("frac", 0, layer),
        )
        for r in range(width):
            at = slot(r, layer)
            here = last_press[at]
            frac = field("frac", r, layer)
            up_x = carried(
                face_x[at], here, last_press[slot(r + 1, layer)], frac, field("frac", r + 1, layer)
            )
            up_y = carried(face_y[at], here, ahead(here), frac, field("frac_ahead", r, layer))
            change = (low_x - up_x) + (behind(up_y) - up_y)
            low_x = up_x
            if layer + 1 < layers:
                up_z = carried(
                    face_z[at], here, last_press[slot(r, layer + 1)], frac,
                    field("frac", r, layer + 1),
                )
                change = change - up_z
                first_press[at] = up_z
            if layer > 0:
                change = change + first_press[slot(r, layer - 1)]
            saturation = field("sat", r, layer) + STEP_COEF * change
            row = layer * width + r
            store_rows(press_ref, here, GROUP, layer, r, layers, width, halves)
            store_rows(sat_ref, saturation, GROUP, layer, r, layers, width, halves)
            mobility = water_frac(saturation) * reciprocal(2.0 * half_inv[at])
            for half in range(halves):
                mob_part = mobility[:, half * LANES : (half + 1) * LANES]
                press_part = here[:, half * LANES : (half + 1) * LANES]
                for p in range(parts):
                    mine = row_of[p] == row * halves + half
                    perf_mob[p] = jnp.where(
                        mine, jnp.take_along_axis(mob_part, lane_of[p], axis=1, mode="promise_in_bounds"), perf_mob[p]
                    )
                    perf_press[p] = jnp.where(
                        mine,
                        jnp.take_along_axis(press_part, lane_of[p], axis=1, mode="promise_in_bounds"),
                        perf_press[p],
                    )

    wells = bhp_ref.shape[1]
    chosen = (
        (lax.broadcasted_iota(jnp.int32, (wells, slots), 0) == well_ref[...])
        .astype(jnp.float32)
        .astype(jnp.bfloat16)
    )
    bhp = pieces(jnp.broadcast_to(bhp_ref[...], (GROUP, wells)))
    bhp = jnp.dot(bhp, chosen, preferred_element_type=jnp.float32)
    perf_bhp = (bhp[:1] + bhp[GROUP : GROUP + 1]) + bhp[2 * GROUP : 2 * GROUP + 1]
    live = (lax.broadcasted_iota(jnp.int32, (1, slots), 1) < count_ref[0]).astype(jnp.float32)
    terms = (
        jnp.concatenate(perf_mob, axis=1)
        * (jnp.concatenate(perf_press, axis=1) - perf_bhp)
        * live
    )
    sums = lax.dot_general(
        pieces(terms), chosen, (((1,), (1,)), ((), ())), preferred_element_type=jnp.float32
    )
    partial_rates = (sums[:GROUP] + sums[GROUP : 2 * GROUP]) + sums[2 * GROUP :]
    rates_ref[...] = partial_rates


def invert_panel(columns):
    row = lax.broadcasted_iota(jnp.int32, columns[0].shape, 0)
    columns = list(columns)
    for k in range(PANEL):
        inverse = 1.0 / columns[k][k : k + 1]
        pivot = columns[k]
        for j in range(PANEL):
            if j != k:
                factor = columns[j][k : k + 1] * inverse
                columns[j] = jnp.where(row == k, factor, columns[j] - pivot * factor)
        columns[k] = jnp.where(row == k, inverse, -pivot * inverse)
    return columns


def solve_blocks(gram_matrix, cross_matrix):
    size = gram_matrix.shape[0]
    count = size // PANEL
    row = lax.broadcasted_iota(jnp.int32, gram_matrix.shape, 0)
    lane = lax.broadcasted_iota(jnp.int32, gram_matrix.shape, 1)
    full = gram_matrix + (row == lane).astype(jnp.float32)
    left = [full[i * PANEL : (i + 1) * PANEL] for i in range(count)]
    right = [cross_matrix[i * PANEL : (i + 1) * PANEL] for i in range(count)]
    width = cross_matrix.shape[1]
    for p in range(count):
        columns = [
            [
                jnp.broadcast_to(left[i][:, p * PANEL + j : p * PANEL + j + 1], (PANEL, size))
                for j in range(PANEL)
            ]
            for i in range(count)
        ]
        inverse = invert_panel(columns[p])
        new_left = sum(inverse[j] * left[p][j : j + 1] for j in range(PANEL))
        new_right = sum(inverse[j][:, :width] * right[p][j : j + 1] for j in range(PANEL))
        for i in range(count):
            if i != p:
                for j in range(PANEL):
                    if p + 1 < count:
                        left[i] = left[i] - columns[i][j] * new_left[j : j + 1]
                    right[i] = right[i] - columns[i][j][:, :width] * new_right[j : j + 1]
        left[p], right[p] = new_left, new_right
    return jnp.concatenate(right, axis=0)


def update_kernel(
    dims, rates_ref, own_ref, noise_ref, observed_ref, var_ref, anomaly_ref, perm_ref, out_ref,
    anomaly_buf, perm_buf, sems,
):
    local_count, layers, width = dims
    rows = layers * width
    halves = anomaly_ref.shape[1] // LANES
    copies = [
        pltpu.make_async_copy(anomaly_ref, anomaly_buf, sems.at[0]),
        pltpu.make_async_copy(perm_ref, perm_buf, sems.at[1]),
    ]
    for copy in copies:
        copy.start()
    rates = rates_ref[...]
    members = rates.shape[0]
    spread = jnp.sqrt(INFLATION * var_ref[...])
    mean_rate = jnp.sum(rates, 0, keepdims=True) / members
    scaled = (rates - mean_rate) / (spread * (members - 1) ** 0.5)
    innovation = (observed_ref[...] - own_ref[...]) / spread + noise_ref[...]
    contract = (((1,), (1,)), ((), ()))
    gram_matrix, cross_matrix = (
        lax.dot_general(
            scaled, other, contract, precision=lax.Precision.HIGHEST,
            preferred_element_type=jnp.float32,
        )
        for other in (scaled, innovation)
    )
    weights = solve_blocks(gram_matrix, cross_matrix).T.astype(jnp.bfloat16)
    for copy in copies:
        copy.wait()
    for row in range(rows):
        layer, x = row // width, row % width
        at = row * local_count
        every = jnp.concatenate(
            [
                anomaly_buf[k * rows * local_count + at : k * rows * local_count + at + local_count, :]
                for k in range(members // local_count)
            ],
            axis=0,
        )
        update = jnp.dot(weights, every, preferred_element_type=jnp.float32)
        place = (local_count, layer, x, layers, width, halves)
        store_rows(out_ref, load_rows(perm_buf, *place) + update, *place)


def per_device(
    log_perm,
    start_pressure,
    start_sat,
    source,
    storage,
    well_press,
    perf_cell,
    perf_well,
    perf_count,
    observed,
    obs_var,
    obs_noise,
):
    local_count, layers, strip_width, strip_depth = log_perm.shape
    tile_count = lax.axis_size("tile")
    members = local_count * lax.axis_size("member")
    well_count = well_press.shape[0]
    well_share = well_count // tile_count
    tile_rank = lax.axis_index("tile")
    rows = layers * strip_width
    slots = perf_cell.shape[0]
    flat_perm = fold(log_perm)
    fields = jnp.stack([start_pressure, start_sat, source, storage]).reshape(-1, strip_depth)
    rim_shape = (RIM * layers * local_count + 4 * GROUP, strip_depth)
    field_scratch = pltpu.VMEM((4 * GROUP, strip_depth), jnp.float32)
    params = pltpu.CompilerParams(vmem_limit_bytes=60 * 2**20)
    up_rows, down_rows, anomaly = pl.pallas_call(
        functools.partial(
            pack_kernel, (local_count, layers, strip_width), (members - 1) ** 0.5
        ),
        out_shape=(
            jax.ShapeDtypeStruct(rim_shape, jnp.bfloat16),
            jax.ShapeDtypeStruct(rim_shape, jnp.bfloat16),
            jax.ShapeDtypeStruct((local_count * rows, strip_depth), jnp.bfloat16),
        ),
        scratch_shapes=[field_scratch, field_scratch],
        compiler_params=params,
        cost_estimate=pl.CostEstimate(
            flops=4 * flat_perm.size, bytes_accessed=8 * flat_perm.size, transcendentals=0
        ),
    )(flat_perm, fields)
    low_rows, high_rows = send_both(up_rows, down_rows, "tile")
    anomaly_all = lax.all_gather(anomaly, "member", axis=0, tiled=True)

    def whole(array):
        return pl.BlockSpec(array.shape, lambda g: (0,) * array.ndim)

    block = pl.BlockSpec((GROUP * rows * (strip_depth // LANES), LANES), lambda g: (g, 0))
    smem = pl.BlockSpec(memory_space=pltpu.SMEM)
    perfs = [perf_cell[None], perf_well[None], well_press[None]]
    span = strip_width + 2 * RIM
    flat_press, flat_sat, partial_rates = pl.pallas_call(
        functools.partial(physics_kernel, (local_count, layers, strip_width, tile_count)),
        grid=(local_count // GROUP,),
        in_specs=[smem, smem, block, whole(low_rows), whole(high_rows)]
        + [whole(array) for array in [fields] + perfs],
        out_specs=(
            block,
            block,
            pl.BlockSpec((GROUP, well_count), lambda g: (g, 0)),
        ),
        out_shape=(
            jax.ShapeDtypeStruct(flat_perm.shape, jnp.float32),
            jax.ShapeDtypeStruct(flat_perm.shape, jnp.float32),
            jax.ShapeDtypeStruct((local_count, well_count), jnp.float32),
        ),
        scratch_shapes=[pltpu.VMEM((span * layers, GROUP, strip_depth), jnp.float32)] * 7,
        compiler_params=params,
        cost_estimate=pl.CostEstimate(
            flops=200 * flat_perm.size, bytes_accessed=16 * flat_perm.size, transcendentals=0
        ),
    )(perf_count, tile_rank[None], flat_perm, low_rows, high_rows, fields, *perfs)
    own_rates = sum_over(partial_rates, "tile")
    well_rates = lax.dynamic_slice_in_dim(own_rates, tile_rank * well_share, well_share, 1)
    rates_all = lax.all_gather(own_rates, "member", axis=0, tiled=True)
    vmem, anywhere = pl.BlockSpec(memory_space=pltpu.VMEM), pl.BlockSpec(memory_space=pl.ANY)
    new_flat = pl.pallas_call(
        functools.partial(update_kernel, (local_count, layers, strip_width)),
        out_shape=jax.ShapeDtypeStruct(flat_perm.shape, jnp.float32),
        in_specs=[vmem] * 5 + [anywhere] * 2,
        out_specs=vmem,
        scratch_shapes=[
            pltpu.VMEM(anomaly_all.shape, jnp.bfloat16),
            pltpu.VMEM(flat_perm.shape, jnp.float32),
            pltpu.SemaphoreType.DMA((2,)),
        ],
        compiler_params=params,
        cost_estimate=pl.CostEstimate(
            flops=12 * members**3, bytes_accessed=16 * flat_perm.size, transcendentals=0
        ),
    )(rates_all, own_rates, obs_noise, observed[None], obs_var[None], anomaly_all, flat_perm)
    new_log_perm = unfold(new_flat, log_perm.shape)
    pressure = unfold(flat_press, log_perm.shape)
    saturation = unfold(flat_sat, log_perm.shape)
    return (new_log_perm, pressure, saturation, well_rates)


def solution(mesh):
    return jax.shard_map(
        per_device,
        mesh=mesh,
        in_specs=(
            P("member", None, "tile", None),
            P(None, "tile", None),
            P(None, "tile", None),
            P(None, "tile", None),
            P(None, "tile", None),
            P(),
            P("tile"),
            P("tile"),
            P("tile"),
            P(),
            P(),
            P("member", None),
        ),
        out_specs=(
            P("member", None, "tile", None),
            P("member", None, "tile", None),
            P("member", None, "tile", None),
            P("member", "tile"),
        ),
        check_vma=False,
    )
```

```python
import functools

import jax
import jax.numpy as jnp
from jax import lax
from jax.experimental import pallas as pl
from jax.experimental.pallas import tpu as pltpu
from jax.sharding import PartitionSpec as P

SWEEPS = 2
RIM = SWEEPS + 1


VERTICAL = 0.5
VISCOSITY_RATIO = 2.0
STEP_COEF = 0.1
INFLATION = 4.0
PANEL = 8
GROUP = 16
LANES = 128


def fold(array):
    members, layers, width, depth = array.shape
    array = array.reshape(members, layers, width, depth // LANES, LANES)
    return array.transpose(0, 1, 3, 2, 4).reshape(-1, LANES)


def unfold(rows, shape):
    members, layers, width, depth = shape
    array = rows.reshape(members, layers, depth // LANES, width, LANES)
    return array.transpose(0, 1, 3, 2, 4).reshape(shape)


def load_rows(ref, count, layer, x, layers, width, halves):
    return jnp.concatenate(
        [
            ref[pl.ds((layer * halves + h) * width + x, count, stride=layers * width * halves), :]
            for h in range(halves)
        ],
        axis=1,
    )


def store_rows(ref, values, count, layer, x, layers, width, halves):
    for h in range(halves):
        at = pl.ds((layer * halves + h) * width + x, count, stride=layers * width * halves)
        ref[at, :] = values[:, h * LANES : (h + 1) * LANES]


def send_both(up_rows, down_rows, axis):
    count = lax.axis_size(axis)
    forward = [(i, i + 1) for i in range(count - 1)]
    backward = [(target, source) for source, target in forward]
    return lax.ppermute(up_rows, axis, forward), lax.ppermute(down_rows, axis, backward)


def sum_over(array, axis):
    count = lax.axis_size(axis)
    stride = count
    while stride > 1:
        radix = 2
        stride //= radix
        groups = [
            [base + low + i * stride for i in range(radix)]
            for base in range(0, count, stride * radix)
            for low in range(stride)
        ]
        array = jnp.sum(lax.all_gather(array, axis, axis_index_groups=groups), 0)
    return array


def reciprocal(values_in):
    guess = pl.reciprocal(values_in, approx=True)
    return guess * (2.0 - values_in * guess)


def pieces(values_in):
    parts = []
    for _ in range(3):
        parts.append(values_in.astype(jnp.bfloat16))
        values_in = values_in - parts[-1].astype(jnp.float32)
    return jnp.concatenate(parts, axis=0)


def water_frac(values_in):
    squared = values_in * values_in
    rest = 1.0 - values_in
    return squared * reciprocal(squared + VISCOSITY_RATIO * rest * rest)


def pack_kernel(dims, root, perm_ref, fields_ref, up_ref, down_ref, anomaly_ref, up_rows, down_rows):
    local_count, layers, width = dims
    up_rows[...] = jnp.zeros_like(up_rows)
    down_rows[...] = jnp.zeros_like(down_rows)
    for f in range(4):
        for layer in range(layers):
            at = f * GROUP + layer * RIM
            first = (f * layers + layer) * width
            down_rows[at : at + RIM, :] = fields_ref[first : first + RIM, :]
            up_rows[at : at + RIM, :] = fields_ref[first + width - RIM : first + width, :]
    halves = anomaly_ref.shape[1] // LANES
    block = RIM * layers * local_count
    up_ref[block:, :] = up_rows[...].astype(jnp.bfloat16)
    down_ref[block:, :] = down_rows[...].astype(jnp.bfloat16)
    for layer in range(layers):
        for x in range(width):
            row = layer * width + x
            values = load_rows(perm_ref, local_count, layer, x, layers, width, halves)
            anomaly_ref[row * local_count : (row + 1) * local_count, :] = (values / root).astype(
                jnp.bfloat16
            )
            low_values = values.astype(jnp.bfloat16)
            if x < RIM:
                at = (x * layers + layer) * local_count
                down_ref[at : at + local_count, :] = low_values
            if x >= width - RIM:
                at = ((x - width + RIM) * layers + layer) * local_count
                up_ref[at : at + local_count, :] = low_values


FIELD_NAMES = ("p0", "sat", "storage", "base", "ahead", "behind", "frac", "frac_ahead")


def state_slots(layers, width):
    kept, added = {}, {}
    rim = list(range(-RIM, 0)) + list(range(width, width + RIM))
    near = [-2, -1, width, width + 1]

    def place(where, kind, rows, count=layers):
        for r in rows:
            for layer in range(count):
                where[kind, r, layer] = len(where)

    place(kept, "half", (0, width - 1))
    place(kept, "face_x", range(width - 1))
    place(kept, "face_y", range(width))
    place(kept, "face_z", range(width), layers - 1)
    place(kept, "inverse", range(width))
    place(kept, "first", range(width))
    place(kept, "last", range(2, width - 2))
    place(kept, "sat", range(3, width - 3))
    place(added, "half", rim)
    place(added, "face_x", [-3, -2, -1, width - 1, width, width + 1])
    place(added, "face_y", near)
    place(added, "face_z", near, layers - 1)
    place(added, "inverse", near + [0, width - 1])
    place(added, "first", near + [0, width - 1])
    place(added, "last", [-1, 0, 1, width - 2, width - 1, width])
    return kept, added


def ahead(values_in):
    return pltpu.roll(values_in, values_in.shape[1] - 1, 1)


def behind(values_in):
    return pltpu.roll(values_in, 1, 1)


def derived_fields(p0, sat, source, storage):
    frac = water_frac(sat)
    return dict(
        p0=p0, sat=sat, storage=storage, base=source + storage * p0,
        ahead=ahead(p0), behind=behind(p0), frac=frac, frac_ahead=ahead(frac),
    )


def cell_faces(load, store, field, r, layer, layers, sides):
    here = load("half", r, layer)
    lane = lax.broadcasted_iota(jnp.int32, here.shape, 1)
    up_y = jnp.where(lane < here.shape[1] - 1, reciprocal(here + ahead(here)), 0.0)
    low_y = behind(up_y)
    store("face_y", r, layer, up_y)
    flow = up_y * field("ahead", r, layer) + low_y * field("behind", r, layer)
    weight = up_y + low_y
    for face, towards in sides:
        flow = flow + face * field("p0", towards, layer)
        weight = weight + face
    if layer + 1 < layers:
        up_z = VERTICAL * reciprocal(here + load("half", r, layer + 1))
        store("face_z", r, layer, up_z)
        flow = flow + up_z * field("p0", r, layer + 1)
        weight = weight + up_z
    if layer > 0:
        low_z = load("face_z", r, layer - 1)
        flow = flow + low_z * field("p0", r, layer - 1)
        weight = weight + low_z
    return field("base", r, layer) + flow, field("storage", r, layer) + weight


def second_sweep(load, store, field, r, layers):
    for layer in range(layers):
        here = load("first", r, layer)
        up_y = load("face_y", r, layer)
        flow = (
            load("face_x", r - 1, layer) * load("first", r - 1, layer)
            + load("face_x", r, layer) * load("first", r + 1, layer)
            + up_y * ahead(here)
            + behind(up_y * here)
        )
        if layer + 1 < layers:
            flow = flow + load("face_z", r, layer) * load("first", r, layer + 1)
        if layer > 0:
            flow = flow + load("face_z", r, layer - 1) * load("first", r, layer - 1)
        store("last", r, layer, (field("base", r, layer) + flow) * load("inverse", r, layer))


def carried(face, low_press, up_press, low_frac, up_frac):
    velocity = face * (low_press - up_press)
    return velocity * jnp.where(velocity > 0, low_frac, up_frac)


def transported(load, field, first_row, last_row, layers):
    def side(r, layer):
        return carried(
            load("face_x", r, layer), load("last", r, layer), load("last", r + 1, layer),
            field("frac", r, layer), field("frac", r + 1, layer),
        )

    low_x = [side(first_row - 1, layer) for layer in range(layers)]
    for r in range(first_row, last_row + 1):
        low_z = None
        for layer in range(layers):
            here = load("last", r, layer)
            frac = field("frac", r, layer)
            up_x = side(r, layer)
            up_y = carried(
                load("face_y", r, layer), here, ahead(here), frac, field("frac_ahead", r, layer)
            )
            change = (low_x[layer] - up_x) + (behind(up_y) - up_y)
            low_x[layer] = up_x
            if low_z is not None:
                change = change + low_z
            if layer + 1 < layers:
                low_z = carried(
                    load("face_z", r, layer), here, load("last", r, layer + 1), frac,
                    field("frac", r, layer + 1),
                )
                change = change - low_z
            yield r, layer, field("sat", r, layer) + STEP_COEF * change


def pick(picked, values_in, row, lane_of, row_of):
    halves = values_in.shape[1] // LANES
    for half in range(halves):
        part = values_in[:, half * LANES : (half + 1) * LANES]
        for p in range(len(picked)):
            found = jnp.take_along_axis(part, lane_of[p], axis=1, mode="promise_in_bounds")
            picked[p] = jnp.where(row_of[p] == row * halves + half, found, picked[p])


def slot_parts(array):
    parts = [array[:, p * LANES : (p + 1) * LANES] for p in range(array.shape[1] // LANES)]
    return [jnp.concatenate([part] * (GROUP // part.shape[0]), axis=0) for part in parts]


def inner_kernel(
    dims, count_ref, perm_ref, fields_ref, cell_ref, well_ref, bhp_ref,
    state_ref, shared_ref, perf_ref, place_ref, chosen_ref, slot_ref, half_ref,
):
    local_count, layers, width = dims
    rows = layers * width
    depth = fields_ref.shape[1]
    halves = depth // LANES
    kept, _ = state_slots(layers, width)
    fields = derived_fields(*(fields_ref[f * rows : (f + 1) * rows, :] for f in range(4)))
    for n, name in enumerate(FIELD_NAMES):
        for row in range(rows):
            shared_ref[n * rows + row] = jnp.broadcast_to(
                fields[name][row : row + 1, :], (8, depth)
            )
    slots = cell_ref.shape[1]
    wells = bhp_ref.shape[1]
    cells = jnp.broadcast_to(cell_ref[...], (8, slots))
    place_ref[:8, :] = cells % LANES
    place_ref[8:, :] = cells // LANES
    chosen = (
        (lax.broadcasted_iota(jnp.int32, (wells, slots), 0) == well_ref[...])
        .astype(jnp.float32)
        .astype(jnp.bfloat16)
    )
    chosen_ref[...] = chosen
    bhp = pieces(jnp.broadcast_to(bhp_ref[...], (GROUP, wells)))
    bhp = jnp.dot(bhp, chosen, preferred_element_type=jnp.float32)
    live = (lax.broadcasted_iota(jnp.int32, (8, slots), 1) < count_ref[0]).astype(jnp.float32)
    slot_ref[:8, :] = (bhp[:8] + bhp[GROUP : GROUP + 8]) + bhp[2 * GROUP : 2 * GROUP + 8]
    slot_ref[8:, :] = live

    def field(name, r, layer):
        tile = shared_ref[FIELD_NAMES.index(name) * rows + layer * width + r]
        return jnp.concatenate([tile] * (GROUP // 8), axis=0)

    @pl.loop(0, local_count // GROUP)
    def _(group):
        at_group = pl.ds(pl.multiple_of(group * GROUP, GROUP), GROUP)
        lane_of, row_of = slot_parts(place_ref[:8, :]), slot_parts(place_ref[8:, :])
        zeros = [jnp.zeros((GROUP, LANES), jnp.float32)] * (slots // LANES)
        picked = [list(zeros) for _ in range(3)]

        def load(kind, r, layer):
            if kind == "half":
                return half_ref[layer * width + r]
            return state_ref[kept[kind, r, layer], at_group, :]

        def store(kind, r, layer, values_in):
            state_ref[kept[kind, r, layer], at_group, :] = values_in

        for r in range(width):
            for layer in range(layers):
                values = jnp.concatenate(
                    [
                        perm_ref[
                            pl.ds(
                                group * GROUP * rows * halves + (layer * halves + h) * width + r,
                                GROUP, stride=rows * halves,
                            ),
                            :,
                        ]
                        for h in range(halves)
                    ],
                    axis=1,
                )
                half = 0.5 * jnp.exp(-values)
                half_ref[layer * width + r] = half
                if r in (0, width - 1):
                    store("half", r, layer, half)
                pick(picked[0], half, layer * width + r, lane_of, row_of)
        for r in range(width - 1):
            for layer in range(layers):
                store(
                    "face_x", r, layer,
                    reciprocal(load("half", r, layer) + load("half", r + 1, layer)),
                )
        for r in range(width):
            for layer in range(layers):
                sides = []
                if r > 0:
                    sides.append((load("face_x", r - 1, layer), r - 1))
                if r < width - 1:
                    sides.append((load("face_x", r, layer), r + 1))
                top, bottom = cell_faces(load, store, field, r, layer, layers, sides)
                if 0 < r < width - 1:
                    bottom = reciprocal(bottom)
                    top = top * bottom
                store("first", r, layer, top)
                store("inverse", r, layer, bottom)
        for r in range(2, width - 2):
            second_sweep(load, store, field, r, layers)
            for layer in range(layers):
                pick(picked[1], load("last", r, layer), layer * width + r, lane_of, row_of)
        for r, layer, saturation in transported(load, field, 3, width - 4, layers):
            store("sat", r, layer, saturation)
            pick(picked[2], saturation, layer * width + r, lane_of, row_of)
        for n in range(3):
            perf_ref[n, at_group, :] = jnp.concatenate(picked[n], axis=1)


def edge_kernel(
    dims, rank_ref, low_ref, high_ref, state_ref, shared_ref, perf_ref, place_ref, chosen_ref,
    slot_ref, press_ref, sat_ref, rates_ref, added_ref, gathered_ref,
):
    local_count, layers, width, tile_count = dims
    rows = layers * width
    depth = low_ref.shape[1]
    halves = depth // LANES
    kept, added = state_slots(layers, width)
    rim_rows = RIM * layers * local_count
    has_low = (rank_ref[0] > 0).astype(jnp.float32)
    has_high = (rank_ref[0] < tile_count - 1).astype(jnp.float32)
    rims = [
        derived_fields(
            *(
                ref[rim_rows + f * GROUP : rim_rows + (f + 1) * GROUP, :].astype(jnp.float32)
                for f in range(4)
            )
        )
        for ref in (low_ref, high_ref)
    ]
    slots = place_ref.shape[1]

    def field(name, r, layer):
        if 0 <= r < width:
            tile = shared_ref[FIELD_NAMES.index(name) * rows + layer * width + r]
            return jnp.concatenate([tile] * (GROUP // 8), axis=0)
        part, at = (rims[0], r + RIM) if r < 0 else (rims[1], r - width)
        at = layer * RIM + at
        return part[name][at : at + 1, :]

    @pl.loop(0, local_count // GROUP)
    def _(group):
        at_group = pl.ds(pl.multiple_of(group * GROUP, GROUP), GROUP)
        lane_of, row_of = slot_parts(place_ref[:8, :]), slot_parts(place_ref[8:, :])
        parts = slots // LANES
        picked = [
            [perf_ref[n, at_group, p * LANES : (p + 1) * LANES] for p in range(parts)]
            for n in range(3)
        ]

        def load(kind, r, layer):
            if (kind, r, layer) in added:
                return added_ref[added[kind, r, layer]]
            return state_ref[kept[kind, r, layer], at_group, :]

        def store(kind, r, layer, values_in):
            added_ref[added[kind, r, layer]] = values_in

        for r in list(range(-RIM, 0)) + list(range(width, width + RIM)):
            ref, i = (low_ref, r + RIM) if r < 0 else (high_ref, r - width)
            for layer in range(layers):
                at = (i * layers + layer) * local_count + group * GROUP
                values = ref[pl.ds(pl.multiple_of(at, GROUP), GROUP), :].astype(jnp.float32)
                store("half", r, layer, 0.5 * jnp.exp(-values))
        for r in (-3, -2, -1, width - 1, width, width + 1):
            for layer in range(layers):
                face = reciprocal(load("half", r, layer) + load("half", r + 1, layer))
                if r == -1:
                    face = face * has_low
                if r == width - 1:
                    face = face * has_high
                store("face_x", r, layer, face)
        for r in (-2, -1, width, width + 1):
            for layer in range(layers):
                sides = [
                    (load("face_x", r - 1, layer), r - 1), (load("face_x", r, layer), r + 1)
                ]
                top, bottom = cell_faces(load, store, field, r, layer, layers, sides)
                bottom = reciprocal(bottom)
                store("first", r, layer, top * bottom)
                store("inverse", r, layer, bottom)
        for r, face_row, towards in ((0, -1, -1), (width - 1, width - 1, width)):
            for layer in range(layers):
                face = load("face_x", face_row, layer)
                top = state_ref[kept["first", r, layer], at_group, :]
                bottom = state_ref[kept["inverse", r, layer], at_group, :]
                bottom = reciprocal(bottom + face)
                store("first", r, layer, (top + face * field("p0", towards, layer)) * bottom)
                store("inverse", r, layer, bottom)
        for r in (-1, 0, 1, width - 2, width - 1, width):
            second_sweep(load, store, field, r, layers)

        def put(ref, r, layer, values_in):
            for h in range(halves):
                at = pl.ds(
                    group * GROUP * rows * halves + (layer * halves + h) * width + r,
                    GROUP, stride=rows * halves,
                )
                ref[at, :] = values_in[:, h * LANES : (h + 1) * LANES]

        for r in range(width):
            for layer in range(layers):
                here = load("last", r, layer)
                put(press_ref, r, layer, here)
                if ("last", r, layer) in added:
                    pick(picked[1], here, layer * width + r, lane_of, row_of)
        for first_row, last_row in ((0, 2), (width - 3, width - 1)):
            for r, layer, saturation in transported(load, field, first_row, last_row, layers):
                put(sat_ref, r, layer, saturation)
                pick(picked[2], saturation, layer * width + r, lane_of, row_of)
        for r in range(3, width - 3):
            for layer in range(layers):
                put(sat_ref, r, layer, load("sat", r, layer))
        for n in range(3):
            gathered_ref[n, at_group, :] = jnp.concatenate(picked[n], axis=1)

    mobility = water_frac(gathered_ref[2]) * reciprocal(2.0 * gathered_ref[0])
    terms = mobility * (gathered_ref[1] - slot_ref[:1, :]) * slot_ref[8:9, :]
    sums = lax.dot_general(
        pieces(terms), chosen_ref[...], (((1,), (1,)), ((), ())),
        preferred_element_type=jnp.float32,
    )
    rates_ref[...] = (sums[:local_count] + sums[local_count : 2 * local_count]) + sums[
        2 * local_count :
    ]


def invert_panel(columns):
    row = lax.broadcasted_iota(jnp.int32, columns[0].shape, 0)
    columns = list(columns)
    for k in range(PANEL):
        inverse = 1.0 / columns[k][k : k + 1]
        pivot = columns[k]
        for j in range(PANEL):
            if j != k:
                factor = columns[j][k : k + 1] * inverse
                columns[j] = jnp.where(row == k, factor, columns[j] - pivot * factor)
        columns[k] = jnp.where(row == k, inverse, -pivot * inverse)
    return columns


def solve_blocks(gram_matrix, cross_matrix):
    size = gram_matrix.shape[0]
    count = size // PANEL
    row = lax.broadcasted_iota(jnp.int32, gram_matrix.shape, 0)
    lane = lax.broadcasted_iota(jnp.int32, gram_matrix.shape, 1)
    full = gram_matrix + (row == lane).astype(jnp.float32)
    left = [full[i * PANEL : (i + 1) * PANEL] for i in range(count)]
    right = [cross_matrix[i * PANEL : (i + 1) * PANEL] for i in range(count)]
    width = cross_matrix.shape[1]
    for p in range(count):
        columns = [
            [
                jnp.broadcast_to(left[i][:, p * PANEL + j : p * PANEL + j + 1], (PANEL, size))
                for j in range(PANEL)
            ]
            for i in range(count)
        ]
        inverse = invert_panel(columns[p])
        new_left = sum(inverse[j] * left[p][j : j + 1] for j in range(PANEL))
        new_right = sum(inverse[j][:, :width] * right[p][j : j + 1] for j in range(PANEL))
        for i in range(count):
            if i != p:
                for j in range(PANEL):
                    if p + 1 < count:
                        left[i] = left[i] - columns[i][j] * new_left[j : j + 1]
                    right[i] = right[i] - columns[i][j][:, :width] * new_right[j : j + 1]
        left[p], right[p] = new_left, new_right
    return jnp.concatenate(right, axis=0)


def update_kernel(
    dims, rates_ref, own_ref, noise_ref, observed_ref, var_ref, anomaly_ref, perm_ref, out_ref,
    anomaly_buf, perm_buf, sems,
):
    local_count, layers, width = dims
    rows = layers * width
    halves = anomaly_ref.shape[1] // LANES
    copies = [
        pltpu.make_async_copy(anomaly_ref, anomaly_buf, sems.at[0]),
        pltpu.make_async_copy(perm_ref, perm_buf, sems.at[1]),
    ]
    for copy in copies:
        copy.start()
    rates = rates_ref[...]
    members = rates.shape[0]
    spread = jnp.sqrt(INFLATION * var_ref[...])
    mean_rate = jnp.sum(rates, 0, keepdims=True) / members
    scaled = (rates - mean_rate) / (spread * (members - 1) ** 0.5)
    innovation = (observed_ref[...] - own_ref[...]) / spread + noise_ref[...]
    contract = (((1,), (1,)), ((), ()))
    gram_matrix, cross_matrix = (
        lax.dot_general(
            scaled, other, contract, precision=lax.Precision.HIGHEST,
            preferred_element_type=jnp.float32,
        )
        for other in (scaled, innovation)
    )
    weights = solve_blocks(gram_matrix, cross_matrix).T.astype(jnp.bfloat16)
    for copy in copies:
        copy.wait()
    for row in range(rows):
        layer, x = row // width, row % width
        at = row * local_count
        every = jnp.concatenate(
            [
                anomaly_buf[k * rows * local_count + at : k * rows * local_count + at + local_count, :]
                for k in range(members // local_count)
            ],
            axis=0,
        )
        update = jnp.dot(weights, every, preferred_element_type=jnp.float32)
        place = (local_count, layer, x, layers, width, halves)
        store_rows(out_ref, load_rows(perm_buf, *place) + update, *place)


def per_device(
    log_perm,
    start_pressure,
    start_sat,
    source,
    storage,
    well_press,
    perf_cell,
    perf_well,
    perf_count,
    observed,
    obs_var,
    obs_noise,
):
    local_count, layers, strip_width, strip_depth = log_perm.shape
    tile_count = lax.axis_size("tile")
    members = local_count * lax.axis_size("member")
    well_count = well_press.shape[0]
    well_share = well_count // tile_count
    tile_rank = lax.axis_index("tile")
    rows = layers * strip_width
    slots = perf_cell.shape[0]
    flat_perm = fold(log_perm)
    fields = jnp.stack([start_pressure, start_sat, source, storage]).reshape(-1, strip_depth)
    rim_shape = (RIM * layers * local_count + 4 * GROUP, strip_depth)
    field_scratch = pltpu.VMEM((4 * GROUP, strip_depth), jnp.float32)
    params = pltpu.CompilerParams(vmem_limit_bytes=60 * 2**20)
    up_rows, down_rows, anomaly = pl.pallas_call(
        functools.partial(
            pack_kernel, (local_count, layers, strip_width), (members - 1) ** 0.5
        ),
        out_shape=(
            jax.ShapeDtypeStruct(rim_shape, jnp.bfloat16),
            jax.ShapeDtypeStruct(rim_shape, jnp.bfloat16),
            jax.ShapeDtypeStruct((local_count * rows, strip_depth), jnp.bfloat16),
        ),
        scratch_shapes=[field_scratch, field_scratch],
        compiler_params=params,
        cost_estimate=pl.CostEstimate(
            flops=4 * flat_perm.size, bytes_accessed=8 * flat_perm.size, transcendentals=0
        ),
    )(flat_perm, fields)
    low_rows, high_rows = send_both(up_rows, down_rows, "tile")
    anomaly_all = lax.all_gather(anomaly, "member", axis=0, tiled=True)

    kept, added = state_slots(layers, strip_width)
    smem, vmem = pl.BlockSpec(memory_space=pltpu.SMEM), pl.BlockSpec(memory_space=pltpu.VMEM)
    anywhere = pl.BlockSpec(memory_space=pl.ANY)
    inner_params = pltpu.CompilerParams(vmem_limit_bytes=28 * 2**20)

    def f32(*shape):
        return jax.ShapeDtypeStruct(shape, jnp.float32)

    handed = pl.pallas_call(
        functools.partial(inner_kernel, (local_count, layers, strip_width)),
        in_specs=[smem] + [vmem] * 5,
        out_specs=(vmem,) * 6,
        out_shape=(
            f32(len(kept), local_count, strip_depth),
            f32(len(FIELD_NAMES) * rows, 8, strip_depth),
            f32(3, local_count, slots),
            jax.ShapeDtypeStruct((16, slots), jnp.int32),
            jax.ShapeDtypeStruct((well_count, slots), jnp.bfloat16),
            f32(16, slots),
        ),
        scratch_shapes=[pltpu.VMEM((rows, GROUP, strip_depth), jnp.float32)],
        compiler_params=inner_params,
        cost_estimate=pl.CostEstimate(
            flops=10**10, bytes_accessed=24 * flat_perm.size, transcendentals=0
        ),
    )(perf_count, flat_perm, fields, perf_cell[None], perf_well[None], well_press[None])
    flat_press, flat_sat, partial_rates = pl.pallas_call(
        functools.partial(edge_kernel, (local_count, layers, strip_width, tile_count)),
        in_specs=[smem] + [vmem] * 8,
        out_specs=(vmem,) * 3,
        out_shape=(
            f32(*flat_perm.shape), f32(*flat_perm.shape), f32(local_count, well_count)
        ),
        scratch_shapes=[
            pltpu.VMEM((len(added), GROUP, strip_depth), jnp.float32),
            pltpu.VMEM((3, local_count, slots), jnp.float32),
        ],
        compiler_params=inner_params,
        cost_estimate=pl.CostEstimate(
            flops=10**10, bytes_accessed=24 * flat_perm.size, transcendentals=0
        ),
    )(tile_rank[None], low_rows, high_rows, *handed)
    own_rates = sum_over(partial_rates, "tile")
    well_rates = lax.dynamic_slice_in_dim(own_rates, tile_rank * well_share, well_share, 1)
    rates_all = lax.all_gather(own_rates, "member", axis=0, tiled=True)
    new_flat = pl.pallas_call(
        functools.partial(update_kernel, (local_count, layers, strip_width)),
        out_shape=jax.ShapeDtypeStruct(flat_perm.shape, jnp.float32),
        in_specs=[vmem] * 5 + [anywhere] * 2,
        out_specs=vmem,
        scratch_shapes=[
            pltpu.VMEM(anomaly_all.shape, jnp.bfloat16),
            pltpu.VMEM(flat_perm.shape, jnp.float32),
            pltpu.SemaphoreType.DMA((2,)),
        ],
        compiler_params=params,
        cost_estimate=pl.CostEstimate(
            flops=12 * members**3, bytes_accessed=16 * flat_perm.size, transcendentals=0
        ),
    )(rates_all, own_rates, obs_noise, observed[None], obs_var[None], anomaly_all, flat_perm)
    new_log_perm = unfold(new_flat, log_perm.shape)
    pressure = unfold(flat_press, log_perm.shape)
    saturation = unfold(flat_sat, log_perm.shape)
    return (new_log_perm, pressure, saturation, well_rates)


def solution(mesh):
    return jax.shard_map(
        per_device,
        mesh=mesh,
        in_specs=(
            P("member", None, "tile", None),
            P(None, "tile", None),
            P(None, "tile", None),
            P(None, "tile", None),
            P(None, "tile", None),
            P(),
            P("tile"),
            P("tile"),
            P("tile"),
            P(),
            P(),
            P("member", None),
        ),
        out_specs=(
            P("member", None, "tile", None),
            P("member", None, "tile", None),
            P("member", None, "tile", None),
            P("member", "tile"),
        ),
        check_vma=False,
    )
```

```python
import functools

import jax
import jax.numpy as jnp
from jax import lax
from jax.experimental import pallas as pl
from jax.experimental.pallas import tpu as pltpu
from jax.sharding import PartitionSpec as P

SWEEPS = 2
RIM = SWEEPS + 1


VERTICAL = 0.5
VISCOSITY_RATIO = 2.0
STEP_COEF = 0.1
INFLATION = 4.0
PANEL = 8
GROUP = 16
LANES = 128


def fold(array):
    members, layers, width, depth = array.shape
    array = array.reshape(members, layers, width, depth // LANES, LANES)
    return array.transpose(0, 1, 3, 2, 4).reshape(-1, LANES)


def unfold(rows, shape):
    members, layers, width, depth = shape
    array = rows.reshape(members, layers, depth // LANES, width, LANES)
    return array.transpose(0, 1, 3, 2, 4).reshape(shape)


def load_rows(ref, count, layer, x, layers, width, halves):
    return jnp.concatenate(
        [
            ref[pl.ds((layer * halves + h) * width + x, count, stride=layers * width * halves), :]
            for h in range(halves)
        ],
        axis=1,
    )


def store_rows(ref, values, count, layer, x, layers, width, halves):
    for h in range(halves):
        at = pl.ds((layer * halves + h) * width + x, count, stride=layers * width * halves)
        ref[at, :] = values[:, h * LANES : (h + 1) * LANES]


def send_both(up_rows, down_rows, axis):
    count = lax.axis_size(axis)
    forward = [(i, i + 1) for i in range(count - 1)]
    backward = [(target, source) for source, target in forward]
    return lax.ppermute(up_rows, axis, forward), lax.ppermute(down_rows, axis, backward)


def sum_over(array, axis):
    count = lax.axis_size(axis)
    stride = 1
    while stride < count:
        around = (0, 1, 3, 2) if count // stride % 4 == 0 else (0, 1)
        groups = [
            [base + low + i * stride for i in around]
            for base in range(0, count, stride * len(around))
            for low in range(stride)
        ]
        array = jnp.sum(lax.all_gather(array, axis, axis_index_groups=groups), 0)
        stride *= len(around)
    return array


def reciprocal(values_in):
    guess = pl.reciprocal(values_in, approx=True)
    return guess * (2.0 - values_in * guess)


def pieces(values_in):
    parts = []
    for _ in range(3):
        parts.append(values_in.astype(jnp.bfloat16))
        values_in = values_in - parts[-1].astype(jnp.float32)
    return jnp.concatenate(parts, axis=0)


def water_frac(values_in):
    squared = values_in * values_in
    rest = 1.0 - values_in
    return squared * reciprocal(squared + VISCOSITY_RATIO * rest * rest)


def pack_kernel(
    dims, root, perm_ref, fields_ref, up_ref, down_ref, anomaly_ref, up_rows, down_rows
):
    local_count, layers, width = dims
    up_rows[...] = jnp.zeros_like(up_rows)
    down_rows[...] = jnp.zeros_like(down_rows)
    for f in range(4):
        for layer in range(layers):
            at = f * GROUP + layer * RIM
            first = (f * layers + layer) * width
            down_rows[at : at + RIM, :] = fields_ref[first : first + RIM, :]
            up_rows[at : at + RIM, :] = fields_ref[first + width - RIM : first + width, :]
    halves = anomaly_ref.shape[1] // LANES
    block = RIM * layers * local_count
    up_ref[block:, :] = up_rows[...].astype(jnp.bfloat16)
    down_ref[block:, :] = down_rows[...].astype(jnp.bfloat16)
    for layer in range(layers):
        for x in range(width):
            row = layer * width + x
            values = load_rows(perm_ref, local_count, layer, x, layers, width, halves)
            anomaly_ref[row * local_count : (row + 1) * local_count, :] = (values / root).astype(
                jnp.bfloat16
            )
            low_values = values.astype(jnp.bfloat16)
            if x < RIM:
                at = (x * layers + layer) * local_count
                down_ref[at : at + local_count, :] = low_values
            if x >= width - RIM:
                at = ((x - width + RIM) * layers + layer) * local_count
                up_ref[at : at + local_count, :] = low_values


FIELD_NAMES = ("p0", "sat", "storage", "base", "ahead", "behind", "frac", "frac_ahead")


def state_slots(layers, width):
    kept, added = {}, {}
    rim = list(range(-RIM, 0)) + list(range(width, width + RIM))
    near = [-2, -1, width, width + 1]

    def place(where, kind, rows, count=layers):
        where[kind] = {}
        for r in rows:
            for layer in range(count):
                where[kind][r, layer] = len(where[kind])

    place(kept, "half", (0, width - 1))
    place(kept, "face_x", range(width - 1))
    place(kept, "face_y", range(width))
    place(kept, "face_z", range(width), layers - 1)
    place(kept, "inverse", range(width))
    place(kept, "first", range(width))
    place(kept, "last", range(2, width - 2))
    place(kept, "sat", range(3, width - 3))
    place(added, "half", rim)
    place(added, "face_x", [-3, -2, -1, width - 1, width, width + 1])
    place(added, "face_y", near)
    place(added, "face_z", near, layers - 1)
    place(added, "inverse", near + [0, width - 1])
    place(added, "first", near + [0, width - 1])
    place(added, "last", [-1, 0, 1, width - 2, width - 1, width])
    first = 0
    for places in added.values():
        for key in places:
            places[key], first = first, first + 1
    return kept, added


def ahead(values_in):
    return pltpu.roll(values_in, values_in.shape[1] - 1, 1)


def behind(values_in):
    return pltpu.roll(values_in, 1, 1)


def derived_fields(p0, sat, source, storage):
    frac = water_frac(sat)
    return dict(
        p0=p0, sat=sat, storage=storage, base=source + storage * p0,
        ahead=ahead(p0), behind=behind(p0), frac=frac, frac_ahead=ahead(frac),
    )


def cell_faces(load, store, field, r, layer, layers, sides):
    here = load("half", r, layer)
    lane = lax.broadcasted_iota(jnp.int32, here.shape, 1)
    up_y = jnp.where(lane < here.shape[1] - 1, reciprocal(here + ahead(here)), 0.0)
    low_y = behind(up_y)
    store("face_y", r, layer, up_y)
    flow = up_y * field("ahead", r, layer) + low_y * field("behind", r, layer)
    weight = up_y + low_y
    for face, towards in sides:
        flow = flow + face * field("p0", towards, layer)
        weight = weight + face
    if layer + 1 < layers:
        up_z = VERTICAL * reciprocal(here + load("half", r, layer + 1))
        store("face_z", r, layer, up_z)
        flow = flow + up_z * field("p0", r, layer + 1)
        weight = weight + up_z
    if layer > 0:
        low_z = load("face_z", r, layer - 1)
        flow = flow + low_z * field("p0", r, layer - 1)
        weight = weight + low_z
    return field("base", r, layer) + flow, field("storage", r, layer) + weight


def second_sweep(load, store, field, r, layers):
    for layer in range(layers):
        here = load("first", r, layer)
        up_y = load("face_y", r, layer)
        flow = (
            load("face_x", r - 1, layer) * load("first", r - 1, layer)
            + load("face_x", r, layer) * load("first", r + 1, layer)
            + up_y * ahead(here)
            + behind(up_y * here)
        )
        if layer + 1 < layers:
            flow = flow + load("face_z", r, layer) * load("first", r, layer + 1)
        if layer > 0:
            flow = flow + load("face_z", r, layer - 1) * load("first", r, layer - 1)
        store("last", r, layer, (field("base", r, layer) + flow) * load("inverse", r, layer))


def carried(face, low_press, up_press, low_frac, up_frac):
    velocity = face * (low_press - up_press)
    return velocity * jnp.where(velocity > 0, low_frac, up_frac)


def transported(load, field, first_row, last_row, layers):
    def side(r, layer):
        return carried(
            load("face_x", r, layer), load("last", r, layer), load("last", r + 1, layer),
            field("frac", r, layer), field("frac", r + 1, layer),
        )

    low_x = [side(first_row - 1, layer) for layer in range(layers)]
    for r in range(first_row, last_row + 1):
        low_z = None
        for layer in range(layers):
            here = load("last", r, layer)
            frac = field("frac", r, layer)
            up_x = side(r, layer)
            up_y = carried(
                load("face_y", r, layer), here, ahead(here), frac, field("frac_ahead", r, layer)
            )
            change = (low_x[layer] - up_x) + (behind(up_y) - up_y)
            low_x[layer] = up_x
            if low_z is not None:
                change = change + low_z
            if layer + 1 < layers:
                low_z = carried(
                    load("face_z", r, layer), here, load("last", r, layer + 1), frac,
                    field("frac", r, layer + 1),
                )
                change = change - low_z
            yield r, layer, field("sat", r, layer) + STEP_COEF * change


def pick(picked, values_in, row, lane_of, row_of):
    halves = values_in.shape[1] // LANES
    for half in range(halves):
        part = values_in[:, half * LANES : (half + 1) * LANES]
        for p in range(len(picked)):
            found = jnp.take_along_axis(part, lane_of[p], axis=1, mode="promise_in_bounds")
            picked[p] = jnp.where(row_of[p] == row * halves + half, found, picked[p])


def slot_parts(array):
    parts = [array[:, p * LANES : (p + 1) * LANES] for p in range(array.shape[1] // LANES)]
    return [jnp.concatenate([part] * (GROUP // part.shape[0]), axis=0) for part in parts]


def inner_kernel(dims, count_ref, *refs):
    local_count, layers, width = dims
    rows = layers * width
    kept, _ = state_slots(layers, width)
    perm_ref, fields_ref, refs = refs[0], refs[1], refs[2:]
    states, refs = dict(zip(kept, refs)), refs[len(kept) :]
    shared_ref, perf_ref, place_ref, chosen_ref, slot_ref, half_ref = refs
    depth = fields_ref.shape[1]
    halves = depth // LANES
    fields = derived_fields(*(fields_ref[f * rows : (f + 1) * rows, :] for f in range(4)))
    for n, name in enumerate(FIELD_NAMES):
        for row in range(rows):
            shared_ref[n * rows + row] = jnp.broadcast_to(
                fields[name][row : row + 1, :], (8, depth)
            )
    wells, slots = chosen_ref.shape
    cell, well, bhp = (
        jnp.concatenate(
            [fields_ref[i : i + 1, :] for i in range(first, first + size // depth)], axis=1
        )
        for first, size in (
            (4 * rows, slots),
            (4 * rows + slots // depth, slots),
            (4 * rows + 2 * slots // depth, wells),
        )
    )
    cells = jnp.broadcast_to(cell.astype(jnp.int32), (8, slots))
    place_ref[:8, :] = cells % LANES
    place_ref[8:, :] = cells // LANES
    chosen = (
        (lax.broadcasted_iota(jnp.int32, (wells, slots), 0) == well.astype(jnp.int32))
        .astype(jnp.float32)
        .astype(jnp.bfloat16)
    )
    chosen_ref[...] = chosen
    bhp = pieces(jnp.broadcast_to(bhp, (GROUP, wells)))
    bhp = jnp.dot(bhp, chosen, preferred_element_type=jnp.float32)
    live = (lax.broadcasted_iota(jnp.int32, (8, slots), 1) < count_ref[0]).astype(jnp.float32)
    slot_ref[:8, :] = (bhp[:8] + bhp[GROUP : GROUP + 8]) + bhp[2 * GROUP : 2 * GROUP + 8]
    slot_ref[8:, :] = live

    def field(name, r, layer):
        tile = shared_ref[FIELD_NAMES.index(name) * rows + layer * width + r]
        return jnp.concatenate([tile] * (GROUP // 8), axis=0)

    @pl.loop(0, local_count // GROUP)
    def _(group):
        at_group = pl.ds(pl.multiple_of(group * GROUP, GROUP), GROUP)
        lane_of, row_of = slot_parts(place_ref[:8, :]), slot_parts(place_ref[8:, :])
        zeros = [jnp.zeros((GROUP, LANES), jnp.float32)] * (slots // LANES)
        picked = [list(zeros) for _ in range(3)]

        def load(kind, r, layer):
            if kind == "half":
                return half_ref[layer * width + r]
            return states[kind][kept[kind][r, layer], at_group, :]

        def store(kind, r, layer, values_in):
            states[kind][kept[kind][r, layer], at_group, :] = values_in

        for r in range(width):
            for layer in range(layers):
                values = jnp.concatenate(
                    [
                        perm_ref[
                            pl.ds(
                                group * GROUP * rows * halves + (layer * halves + h) * width + r,
                                GROUP, stride=rows * halves,
                            ),
                            :,
                        ]
                        for h in range(halves)
                    ],
                    axis=1,
                )
                half = 0.5 * jnp.exp(-values)
                half_ref[layer * width + r] = half
                if r in (0, width - 1):
                    store("half", r, layer, half)
                pick(picked[0], half, layer * width + r, lane_of, row_of)
        for r in range(width - 1):
            for layer in range(layers):
                store(
                    "face_x", r, layer,
                    reciprocal(load("half", r, layer) + load("half", r + 1, layer)),
                )
        for r in range(width):
            for layer in range(layers):
                sides = []
                if r > 0:
                    sides.append((load("face_x", r - 1, layer), r - 1))
                if r < width - 1:
                    sides.append((load("face_x", r, layer), r + 1))
                top, bottom = cell_faces(load, store, field, r, layer, layers, sides)
                if 0 < r < width - 1:
                    bottom = reciprocal(bottom)
                    top = top * bottom
                store("first", r, layer, top)
                store("inverse", r, layer, bottom)
        for r in range(2, width - 2):
            second_sweep(load, store, field, r, layers)
            for layer in range(layers):
                pick(picked[1], load("last", r, layer), layer * width + r, lane_of, row_of)
        for r, layer, saturation in transported(load, field, 3, width - 4, layers):
            store("sat", r, layer, saturation)
            pick(picked[2], saturation, layer * width + r, lane_of, row_of)
        for n in range(3):
            perf_ref[n, at_group, :] = jnp.concatenate(picked[n], axis=1)


def edge_kernel(dims, rank_ref, low_ref, high_ref, *refs):
    local_count, layers, width, tile_count = dims
    rows = layers * width
    depth = low_ref.shape[1]
    halves = depth // LANES
    kept, added = state_slots(layers, width)
    states, refs = dict(zip(kept, refs)), refs[len(kept) :]
    shared_ref, perf_ref, place_ref, chosen_ref, slot_ref = refs[:5]
    press_ref, sat_ref, rates_ref, added_ref, gathered_ref = refs[5:]
    rim_rows = RIM * layers * local_count
    has_low = (rank_ref[0] > 0).astype(jnp.float32)
    has_high = (rank_ref[0] < tile_count - 1).astype(jnp.float32)
    rims = [
        derived_fields(
            *(
                ref[rim_rows + f * GROUP : rim_rows + (f + 1) * GROUP, :].astype(jnp.float32)
                for f in range(4)
            )
        )
        for ref in (low_ref, high_ref)
    ]
    slots = place_ref.shape[1]

    def field(name, r, layer):
        if 0 <= r < width:
            tile = shared_ref[FIELD_NAMES.index(name) * rows + layer * width + r]
            return jnp.concatenate([tile] * (GROUP // 8), axis=0)
        part, at = (rims[0], r + RIM) if r < 0 else (rims[1], r - width)
        at = layer * RIM + at
        return part[name][at : at + 1, :]

    @pl.loop(0, local_count // GROUP)
    def _(group):
        at_group = pl.ds(pl.multiple_of(group * GROUP, GROUP), GROUP)
        lane_of, row_of = slot_parts(place_ref[:8, :]), slot_parts(place_ref[8:, :])
        parts = slots // LANES
        picked = [
            [perf_ref[n, at_group, p * LANES : (p + 1) * LANES] for p in range(parts)]
            for n in range(3)
        ]

        def load(kind, r, layer):
            if (r, layer) in added.get(kind, {}):
                return added_ref[added[kind][r, layer]]
            return states[kind][kept[kind][r, layer], at_group, :]

        def store(kind, r, layer, values_in):
            added_ref[added[kind][r, layer]] = values_in

        for r in list(range(-RIM, 0)) + list(range(width, width + RIM)):
            ref, i = (low_ref, r + RIM) if r < 0 else (high_ref, r - width)
            for layer in range(layers):
                at = (i * layers + layer) * local_count + group * GROUP
                values = ref[pl.ds(pl.multiple_of(at, GROUP), GROUP), :].astype(jnp.float32)
                store("half", r, layer, 0.5 * jnp.exp(-values))
        for r in (-3, -2, -1, width - 1, width, width + 1):
            for layer in range(layers):
                face = reciprocal(load("half", r, layer) + load("half", r + 1, layer))
                if r == -1:
                    face = face * has_low
                if r == width - 1:
                    face = face * has_high
                store("face_x", r, layer, face)
        for r in (-2, -1, width, width + 1):
            for layer in range(layers):
                sides = [
                    (load("face_x", r - 1, layer), r - 1), (load("face_x", r, layer), r + 1)
                ]
                top, bottom = cell_faces(load, store, field, r, layer, layers, sides)
                bottom = reciprocal(bottom)
                store("first", r, layer, top * bottom)
                store("inverse", r, layer, bottom)
        for r, face_row, towards in ((0, -1, -1), (width - 1, width - 1, width)):
            for layer in range(layers):
                face = load("face_x", face_row, layer)
                top = states["first"][kept["first"][r, layer], at_group, :]
                bottom = states["inverse"][kept["inverse"][r, layer], at_group, :]
                bottom = reciprocal(bottom + face)
                store("first", r, layer, (top + face * field("p0", towards, layer)) * bottom)
                store("inverse", r, layer, bottom)
        for r in (-1, 0, 1, width - 2, width - 1, width):
            second_sweep(load, store, field, r, layers)

        def put(ref, r, layer, values_in):
            for h in range(halves):
                at = pl.ds(
                    group * GROUP * rows * halves + (layer * halves + h) * width + r,
                    GROUP, stride=rows * halves,
                )
                ref[at, :] = values_in[:, h * LANES : (h + 1) * LANES]

        for r in range(width):
            for layer in range(layers):
                here = load("last", r, layer)
                put(press_ref, r, layer, here)
                if (r, layer) in added["last"]:
                    pick(picked[1], here, layer * width + r, lane_of, row_of)
        for first_row, last_row in ((0, 2), (width - 3, width - 1)):
            for r, layer, saturation in transported(load, field, first_row, last_row, layers):
                put(sat_ref, r, layer, saturation)
                pick(picked[2], saturation, layer * width + r, lane_of, row_of)
        for r in range(3, width - 3):
            for layer in range(layers):
                put(sat_ref, r, layer, load("sat", r, layer))
        for n in range(3):
            gathered_ref[n, at_group, :] = jnp.concatenate(picked[n], axis=1)

    mobility = water_frac(gathered_ref[2]) * reciprocal(2.0 * gathered_ref[0])
    terms = mobility * (gathered_ref[1] - slot_ref[:1, :]) * slot_ref[8:9, :]
    sums = lax.dot_general(
        pieces(terms), chosen_ref[...], (((1,), (1,)), ((), ())),
        preferred_element_type=jnp.float32,
    )
    rates_ref[...] = (sums[:local_count] + sums[local_count : 2 * local_count]) + sums[
        2 * local_count :
    ]


def invert_panel(columns):
    row = lax.broadcasted_iota(jnp.int32, columns[0].shape, 0)
    columns = list(columns)
    for k in range(PANEL):
        inverse = 1.0 / columns[k][k : k + 1]
        pivot = columns[k]
        for j in range(PANEL):
            if j != k:
                factor = columns[j][k : k + 1] * inverse
                columns[j] = jnp.where(row == k, factor, columns[j] - pivot * factor)
        columns[k] = jnp.where(row == k, inverse, -pivot * inverse)
    return columns


def solve_blocks(gram_matrix, cross_matrix):
    size = gram_matrix.shape[0]
    count = size // PANEL
    row = lax.broadcasted_iota(jnp.int32, gram_matrix.shape, 0)
    lane = lax.broadcasted_iota(jnp.int32, gram_matrix.shape, 1)
    full = gram_matrix + (row == lane).astype(jnp.float32)
    left = [full[i * PANEL : (i + 1) * PANEL] for i in range(count)]
    right = [cross_matrix[i * PANEL : (i + 1) * PANEL] for i in range(count)]
    width = cross_matrix.shape[1]
    for p in range(count):
        columns = [
            [
                jnp.broadcast_to(left[i][:, p * PANEL + j : p * PANEL + j + 1], (PANEL, size))
                for j in range(PANEL)
            ]
            for i in range(count)
        ]
        inverse = invert_panel(columns[p])
        new_left = sum(inverse[j] * left[p][j : j + 1] for j in range(PANEL))
        new_right = sum(inverse[j][:, :width] * right[p][j : j + 1] for j in range(PANEL))
        for i in range(count):
            if i != p:
                for j in range(PANEL):
                    if p + 1 < count:
                        left[i] = left[i] - columns[i][j] * new_left[j : j + 1]
                    right[i] = right[i] - columns[i][j][:, :width] * new_right[j : j + 1]
        left[p], right[p] = new_left, new_right
    return jnp.concatenate(right, axis=0)


def update_kernel(
    dims, rates_ref, own_ref, noise_ref, observed_ref, var_ref, anomaly_ref, perm_ref, out_ref,
    anomaly_buf, perm_buf, sems,
):
    local_count, layers, width = dims
    rows = layers * width
    halves = anomaly_ref.shape[1] // LANES
    copies = [
        pltpu.make_async_copy(anomaly_ref, anomaly_buf, sems.at[0]),
        pltpu.make_async_copy(perm_ref, perm_buf, sems.at[1]),
    ]
    for copy in copies:
        copy.start()
    rates = rates_ref[...]
    members = rates.shape[0]
    spread = jnp.sqrt(INFLATION * var_ref[...])
    mean_rate = jnp.sum(rates, 0, keepdims=True) / members
    scaled = (rates - mean_rate) / (spread * (members - 1) ** 0.5)
    innovation = (observed_ref[...] - own_ref[...]) / spread + noise_ref[...]
    contract = (((1,), (1,)), ((), ()))
    gram_matrix, cross_matrix = (
        lax.dot_general(
            scaled, other, contract, precision=lax.Precision.HIGHEST,
            preferred_element_type=jnp.float32,
        )
        for other in (scaled, innovation)
    )
    weights = solve_blocks(gram_matrix, cross_matrix).T.astype(jnp.bfloat16)
    for copy in copies:
        copy.wait()
    for row in range(rows):
        layer, x = row // width, row % width
        at = row * local_count
        every = jnp.concatenate(
            [
                anomaly_buf[k * rows * local_count + at : k * rows * local_count + at + local_count, :]
                for k in range(members // local_count)
            ],
            axis=0,
        )
        update = jnp.dot(weights, every, preferred_element_type=jnp.float32)
        place = (local_count, layer, x, layers, width, halves)
        store_rows(out_ref, load_rows(perm_buf, *place) + update, *place)


def per_device(
    log_perm,
    start_pressure,
    start_sat,
    source,
    storage,
    well_press,
    perf_cell,
    perf_well,
    perf_count,
    observed,
    obs_var,
    obs_noise,
):
    local_count, layers, strip_width, strip_depth = log_perm.shape
    tile_count = lax.axis_size("tile")
    members = local_count * lax.axis_size("member")
    well_count = well_press.shape[0]
    well_share = well_count // tile_count
    tile_rank = lax.axis_index("tile")
    rows = layers * strip_width
    slots = perf_cell.shape[0]
    flat_perm = fold(log_perm)
    fields = jnp.concatenate(
        [
            array.astype(jnp.float32).reshape(-1, strip_depth)
            for array in (
                start_pressure, start_sat, source, storage, perf_cell, perf_well, well_press
            )
        ]
    )
    in_hbm = pl.BlockSpec(memory_space=pltpu.HBM)
    rim_shape = (RIM * layers * local_count + 4 * GROUP, strip_depth)
    field_scratch = pltpu.VMEM((4 * GROUP, strip_depth), jnp.float32)
    params = pltpu.CompilerParams(vmem_limit_bytes=20 * 2**20)
    up_rows, down_rows, anomaly = pl.pallas_call(
        functools.partial(
            pack_kernel, (local_count, layers, strip_width), (members - 1) ** 0.5
        ),
        out_shape=(
            jax.ShapeDtypeStruct(rim_shape, jnp.bfloat16),
            jax.ShapeDtypeStruct(rim_shape, jnp.bfloat16),
            jax.ShapeDtypeStruct((local_count * rows, strip_depth), jnp.bfloat16),
        ),
        scratch_shapes=[field_scratch, field_scratch],
        compiler_params=params,
        cost_estimate=pl.CostEstimate(
            flops=4 * flat_perm.size, bytes_accessed=8 * flat_perm.size, transcendentals=0
        ),
    )(flat_perm, fields)
    low_rows, high_rows = send_both(up_rows, down_rows, "tile")
    anomaly_all = lax.all_gather(anomaly, "member", axis=0, tiled=True)

    kept, added = state_slots(layers, strip_width)
    smem, vmem = pl.BlockSpec(memory_space=pltpu.SMEM), pl.BlockSpec(memory_space=pltpu.VMEM)

    def f32(*shape):
        return jax.ShapeDtypeStruct(shape, jnp.float32)

    handed = pl.pallas_call(
        functools.partial(inner_kernel, (local_count, layers, strip_width)),
        in_specs=[smem] + [vmem] * 2,
        out_specs=(vmem,) * (len(kept) + 5),
        out_shape=(
            *(f32(len(places), local_count, strip_depth) for places in kept.values()),
            f32(len(FIELD_NAMES) * rows, 8, strip_depth),
            f32(3, local_count, slots),
            jax.ShapeDtypeStruct((16, slots), jnp.int32),
            jax.ShapeDtypeStruct((well_count, slots), jnp.bfloat16),
            f32(16, slots),
        ),
        scratch_shapes=[pltpu.VMEM((rows, GROUP, strip_depth), jnp.float32)],
        compiler_params=params,
        cost_estimate=pl.CostEstimate(
            flops=10**10, bytes_accessed=24 * flat_perm.size, transcendentals=0
        ),
    )(perf_count, flat_perm, fields)
    flat_press, flat_sat, partial_rates = pl.pallas_call(
        functools.partial(edge_kernel, (local_count, layers, strip_width, tile_count)),
        in_specs=[smem] + [vmem] * (len(kept) + 7),
        out_specs=(vmem,) * 3,
        out_shape=(
            f32(*flat_perm.shape), f32(*flat_perm.shape), f32(local_count, well_count)
        ),
        scratch_shapes=[
            pltpu.VMEM((sum(map(len, added.values())), GROUP, strip_depth), jnp.float32),
            pltpu.VMEM((3, local_count, slots), jnp.float32),
        ],
        compiler_params=params,
        cost_estimate=pl.CostEstimate(
            flops=10**10, bytes_accessed=24 * flat_perm.size, transcendentals=0
        ),
    )(tile_rank[None], low_rows, high_rows, *handed)
    own_rates = sum_over(partial_rates, "tile")
    well_rates = lax.dynamic_slice_in_dim(own_rates, tile_rank * well_share, well_share, 1)
    rates_all = lax.all_gather(own_rates, "member", axis=0, tiled=True)
    new_flat = pl.pallas_call(
        functools.partial(update_kernel, (local_count, layers, strip_width)),
        out_shape=jax.ShapeDtypeStruct(flat_perm.shape, jnp.float32),
        in_specs=[vmem] * 5 + [in_hbm] * 2,
        out_specs=vmem,
        scratch_shapes=[
            pltpu.VMEM(anomaly_all.shape, jnp.bfloat16),
            pltpu.VMEM(flat_perm.shape, jnp.float32),
            pltpu.SemaphoreType.DMA((2,)),
        ],
        compiler_params=pltpu.CompilerParams(vmem_limit_bytes=60 * 2**20),
        cost_estimate=pl.CostEstimate(
            flops=12 * members**3, bytes_accessed=16 * flat_perm.size, transcendentals=0
        ),
    )(rates_all, own_rates, obs_noise, observed[None], obs_var[None], anomaly_all, flat_perm)
    new_log_perm = unfold(new_flat, log_perm.shape)
    pressure = unfold(flat_press, log_perm.shape)
    saturation = unfold(flat_sat, log_perm.shape)
    return (new_log_perm, pressure, saturation, well_rates)


def solution(mesh):
    return jax.shard_map(
        per_device,
        mesh=mesh,
        in_specs=(
            P("member", None, "tile", None),
            P(None, "tile", None),
            P(None, "tile", None),
            P(None, "tile", None),
            P(None, "tile", None),
            P(),
            P("tile"),
            P("tile"),
            P("tile"),
            P(),
            P(),
            P("member", None),
        ),
        out_specs=(
            P("member", None, "tile", None),
            P("member", None, "tile", None),
            P("member", None, "tile", None),
            P("member", "tile"),
        ),
        check_vma=False,
    )
```

```python
import functools

import jax
import jax.numpy as jnp
from jax import lax
from jax.experimental import pallas as pl
from jax.experimental.pallas import tpu as pltpu
from jax.sharding import PartitionSpec as P

SWEEPS = 2
RIM = SWEEPS + 1


VERTICAL = 0.5
VISCOSITY_RATIO = 2.0
STEP_COEF = 0.1
INFLATION = 4.0
PANEL = 8
GROUP = 16
LANES = 128


def fold(array):
    members, layers, width, depth = array.shape
    array = array.reshape(members, layers, width, depth // LANES, LANES)
    return array.transpose(0, 1, 3, 2, 4).reshape(-1, LANES)


def unfold(rows, shape):
    members, layers, width, depth = shape
    array = rows.reshape(members, layers, depth // LANES, width, LANES)
    return array.transpose(0, 1, 3, 2, 4).reshape(shape)


def load_rows(ref, count, layer, x, layers, width, halves):
    return jnp.concatenate(
        [
            ref[pl.ds((layer * halves + h) * width + x, count, stride=layers * width * halves), :]
            for h in range(halves)
        ],
        axis=1,
    )


def store_rows(ref, values, count, layer, x, layers, width, halves):
    for h in range(halves):
        at = pl.ds((layer * halves + h) * width + x, count, stride=layers * width * halves)
        ref[at, :] = values[:, h * LANES : (h + 1) * LANES]


def send_both(up_rows, down_rows, axis):
    count = lax.axis_size(axis)
    forward = [(i, i + 1) for i in range(count - 1)]
    backward = [(target, source) for source, target in forward]
    return lax.ppermute(up_rows, axis, forward), lax.ppermute(down_rows, axis, backward)


def sum_over(array, axis):
    count = lax.axis_size(axis)
    stride = count
    while stride > 1:
        radix = 2
        stride //= radix
        groups = [
            [base + low + i * stride for i in range(radix)]
            for base in range(0, count, stride * radix)
            for low in range(stride)
        ]
        array = jnp.sum(lax.all_gather(array, axis, axis_index_groups=groups), 0)
    return array


def reciprocal(values_in):
    guess = pl.reciprocal(values_in, approx=True)
    return guess * (2.0 - values_in * guess)


def pieces(values_in):
    parts = []
    for _ in range(3):
        parts.append(values_in.astype(jnp.bfloat16))
        values_in = values_in - parts[-1].astype(jnp.float32)
    return jnp.concatenate(parts, axis=0)


def water_frac(values_in):
    squared = values_in * values_in
    rest = 1.0 - values_in
    return squared * reciprocal(squared + VISCOSITY_RATIO * rest * rest)


def pack_kernel(
    dims, root, perm_ref, p0_ref, sat_ref, source_ref, storage_ref, up_ref, down_ref, anomaly_ref,
    up_rows, down_rows,
):
    local_count, layers, width = dims
    up_rows[...] = jnp.zeros_like(up_rows)
    down_rows[...] = jnp.zeros_like(down_rows)
    for f, fields_ref in enumerate((p0_ref, sat_ref, source_ref, storage_ref)):
        for layer in range(layers):
            at = f * GROUP + layer * RIM
            first = layer * width
            down_rows[at : at + RIM, :] = fields_ref[first : first + RIM, :]
            up_rows[at : at + RIM, :] = fields_ref[first + width - RIM : first + width, :]
    halves = anomaly_ref.shape[1] // LANES
    block = RIM * layers * local_count
    up_ref[block:, :] = up_rows[...].astype(jnp.bfloat16)
    down_ref[block:, :] = down_rows[...].astype(jnp.bfloat16)
    for layer in range(layers):
        for x in range(width):
            row = layer * width + x
            values = load_rows(perm_ref, local_count, layer, x, layers, width, halves)
            anomaly_ref[row * local_count : (row + 1) * local_count, :] = (values / root).astype(
                jnp.bfloat16
            )
            low_values = values.astype(jnp.bfloat16)
            if x < RIM:
                at = (x * layers + layer) * local_count
                down_ref[at : at + local_count, :] = low_values
            if x >= width - RIM:
                at = ((x - width + RIM) * layers + layer) * local_count
                up_ref[at : at + local_count, :] = low_values


WORK = ("half", "face_x", "face_y", "face_z", "inverse", "first", "last")
FIELD_NAMES = ("p0", "sat", "storage", "base", "ahead", "behind", "frac", "frac_ahead")


def state_slots(layers, width):
    kept, added = {}, {}
    rim = list(range(-RIM, 0)) + list(range(width, width + RIM))
    near = [-2, -1, width, width + 1]

    def place(where, kind, rows, count=layers):
        where[kind] = {}
        for r in rows:
            for layer in range(count):
                where[kind][r, layer] = len(where[kind])

    place(kept, "half", (0, width - 1))
    place(kept, "face_x", [0, 1, 2, width - 4, width - 3, width - 2])
    outer = [0, 1, 2, width - 3, width - 2, width - 1]
    place(kept, "face_y", outer)
    place(kept, "face_z", outer, layers - 1)
    place(kept, "inverse", [0, 1, width - 2, width - 1])
    place(kept, "first", outer)
    place(kept, "last", range(2, width - 2))
    place(kept, "sat", range(3, width - 3))
    place(added, "half", rim)
    place(added, "face_x", [-3, -2, -1, width - 1, width, width + 1])
    place(added, "face_y", near)
    place(added, "face_z", near, layers - 1)
    place(added, "inverse", near + [0, width - 1])
    place(added, "first", near + [0, width - 1])
    place(added, "last", [-1, 0, 1, width - 2, width - 1, width])
    first = 0
    for places in added.values():
        for key in places:
            places[key], first = first, first + 1
    return kept, added


def ahead(values_in):
    return pltpu.roll(values_in, values_in.shape[1] - 1, 1)


def behind(values_in):
    return pltpu.roll(values_in, 1, 1)


def derived_fields(p0, sat, source, storage):
    frac = water_frac(sat)
    return dict(
        p0=p0, sat=sat, storage=storage, base=source + storage * p0,
        ahead=ahead(p0), behind=behind(p0), frac=frac, frac_ahead=ahead(frac),
    )


def cell_faces(load, store, field, r, layer, layers, sides):
    here = load("half", r, layer)
    lane = lax.broadcasted_iota(jnp.int32, here.shape, 1)
    up_y = jnp.where(lane < here.shape[1] - 1, reciprocal(here + ahead(here)), 0.0)
    low_y = behind(up_y)
    store("face_y", r, layer, up_y)
    flow = up_y * field("ahead", r, layer) + low_y * field("behind", r, layer)
    weight = up_y + low_y
    for face, towards in sides:
        flow = flow + face * field("p0", towards, layer)
        weight = weight + face
    if layer + 1 < layers:
        up_z = VERTICAL * reciprocal(here + load("half", r, layer + 1))
        store("face_z", r, layer, up_z)
        flow = flow + up_z * field("p0", r, layer + 1)
        weight = weight + up_z
    if layer > 0:
        low_z = load("face_z", r, layer - 1)
        flow = flow + low_z * field("p0", r, layer - 1)
        weight = weight + low_z
    return field("base", r, layer) + flow, field("storage", r, layer) + weight


def second_sweep(load, store, field, r, layers):
    for layer in range(layers):
        here = load("first", r, layer)
        up_y = load("face_y", r, layer)
        flow = (
            load("face_x", r - 1, layer) * load("first", r - 1, layer)
            + load("face_x", r, layer) * load("first", r + 1, layer)
            + up_y * ahead(here)
            + behind(up_y * here)
        )
        if layer + 1 < layers:
            flow = flow + load("face_z", r, layer) * load("first", r, layer + 1)
        if layer > 0:
            flow = flow + load("face_z", r, layer - 1) * load("first", r, layer - 1)
        store("last", r, layer, (field("base", r, layer) + flow) * load("inverse", r, layer))


def carried(face, low_press, up_press, low_frac, up_frac):
    velocity = face * (low_press - up_press)
    return velocity * jnp.where(velocity > 0, low_frac, up_frac)


def transported(load, field, first_row, last_row, layers):
    def side(r, layer):
        return carried(
            load("face_x", r, layer), load("last", r, layer), load("last", r + 1, layer),
            field("frac", r, layer), field("frac", r + 1, layer),
        )

    low_x = [side(first_row - 1, layer) for layer in range(layers)]
    for r in range(first_row, last_row + 1):
        low_z = None
        for layer in range(layers):
            here = load("last", r, layer)
            frac = field("frac", r, layer)
            up_x = side(r, layer)
            up_y = carried(
                load("face_y", r, layer), here, ahead(here), frac, field("frac_ahead", r, layer)
            )
            change = (low_x[layer] - up_x) + (behind(up_y) - up_y)
            low_x[layer] = up_x
            if low_z is not None:
                change = change + low_z
            if layer + 1 < layers:
                low_z = carried(
                    load("face_z", r, layer), here, load("last", r, layer + 1), frac,
                    field("frac", r, layer + 1),
                )
                change = change - low_z
            yield r, layer, field("sat", r, layer) + STEP_COEF * change


def pick(picked, values_in, row, lane_of, row_of):
    halves = values_in.shape[1] // LANES
    for half in range(halves):
        part = values_in[:, half * LANES : (half + 1) * LANES]
        for p in range(len(picked)):
            found = jnp.take_along_axis(part, lane_of[p], axis=1, mode="promise_in_bounds")
            picked[p] = jnp.where(row_of[p] == row * halves + half, found, picked[p])


def slot_parts(array):
    parts = [array[:, p * LANES : (p + 1) * LANES] for p in range(array.shape[1] // LANES)]
    return [jnp.concatenate([part] * (GROUP // part.shape[0]), axis=0) for part in parts]


def put_fields(dest_ref, field_refs):
    fields = derived_fields(*(ref[...] for ref in field_refs))
    rows, depth = field_refs[0].shape
    for n, name in enumerate(FIELD_NAMES):
        for row in range(rows):
            dest_ref[n * rows + row] = jnp.broadcast_to(fields[name][row : row + 1, :], (8, depth))


def cell_places(cell_ref):
    cells = jnp.broadcast_to(cell_ref[...], (GROUP, cell_ref.shape[1]))
    return slot_parts(cells % LANES), slot_parts(cells // LANES)


def inner_kernel(dims, perm_ref, *refs):
    layers, width = dims
    rows = layers * width
    kept, _ = state_slots(layers, width)
    field_refs, cell_ref, refs = refs[:4], refs[4], refs[5:]
    states, refs = dict(zip(kept, refs)), refs[len(kept) :]
    perf_ref, shared_ref, work_refs = refs[0], refs[1], dict(zip(WORK, refs[2:]))
    slots = cell_ref.shape[1]
    depth = field_refs[0].shape[1]
    halves = depth // LANES

    @pl.when(pl.program_id(0) == 0)
    def _():
        put_fields(shared_ref, field_refs)

    def field(name, r, layer):
        tile = shared_ref[FIELD_NAMES.index(name) * rows + layer * width + r]
        return jnp.concatenate([tile] * (GROUP // 8), axis=0)

    lane_of, row_of = cell_places(cell_ref)
    zeros = [jnp.zeros((GROUP, LANES), jnp.float32)] * (slots // LANES)
    picked = [list(zeros) for _ in range(3)]

    def load(kind, r, layer):
        return work_refs[kind][layer * width + r]

    def store(kind, r, layer, values_in):
        if kind in work_refs:
            work_refs[kind][layer * width + r] = values_in
        if (r, layer) in kept[kind]:
            states[kind][kept[kind][r, layer]] = values_in

    for r in range(width):
        for layer in range(layers):
            values = load_rows(perm_ref, GROUP, layer, r, layers, width, halves)
            half = 0.5 * jnp.exp(-values)
            store("half", r, layer, half)
            pick(picked[0], half, layer * width + r, lane_of, row_of)
    for r in range(width - 1):
        for layer in range(layers):
            store(
                "face_x", r, layer,
                reciprocal(load("half", r, layer) + load("half", r + 1, layer)),
            )
    for r in range(width):
        for layer in range(layers):
            sides = []
            if r > 0:
                sides.append((load("face_x", r - 1, layer), r - 1))
            if r < width - 1:
                sides.append((load("face_x", r, layer), r + 1))
            top, bottom = cell_faces(load, store, field, r, layer, layers, sides)
            if 0 < r < width - 1:
                bottom = reciprocal(bottom)
                top = top * bottom
            store("first", r, layer, top)
            store("inverse", r, layer, bottom)
    for r in range(2, width - 2):
        second_sweep(load, store, field, r, layers)
        for layer in range(layers):
            pick(picked[1], load("last", r, layer), layer * width + r, lane_of, row_of)
    for r, layer, saturation in transported(load, field, 3, width - 4, layers):
        store("sat", r, layer, saturation)
        pick(picked[2], saturation, layer * width + r, lane_of, row_of)
    for n in range(3):
        perf_ref[n] = jnp.concatenate(picked[n], axis=1)


def edge_kernel(dims, rank_ref, low_ref, high_ref, *refs):
    local_count, layers, width, tile_count = dims
    rows = layers * width
    depth = low_ref.shape[1]
    halves = depth // LANES
    group = pl.program_id(0)
    kept, added = state_slots(layers, width)
    field_refs, count_ref, cell_ref, well_ref, bhp_ref = refs[:4], refs[4], refs[5], refs[6], refs[7]
    refs = refs[8:]
    states, refs = dict(zip(kept, refs)), refs[len(kept) :]
    perf_ref, press_ref, sat_ref, rates_ref, added_ref, gathered_ref, shared_ref = refs
    rim_rows = RIM * layers * local_count
    has_low = (rank_ref[0] > 0).astype(jnp.float32)
    has_high = (rank_ref[0] < tile_count - 1).astype(jnp.float32)
    rims = [
        derived_fields(
            *(
                ref[rim_rows + f * GROUP : rim_rows + (f + 1) * GROUP, :].astype(jnp.float32)
                for f in range(4)
            )
        )
        for ref in (low_ref, high_ref)
    ]
    slots, wells = cell_ref.shape[1], bhp_ref.shape[1]

    @pl.when(group == 0)
    def _():
        put_fields(shared_ref, field_refs)

    def field(name, r, layer):
        if 0 <= r < width:
            tile = shared_ref[FIELD_NAMES.index(name) * rows + layer * width + r]
            return jnp.concatenate([tile] * (GROUP // 8), axis=0)
        part, at = (rims[0], r + RIM) if r < 0 else (rims[1], r - width)
        at = layer * RIM + at
        return part[name][at : at + 1, :]

    lane_of, row_of = cell_places(cell_ref)
    parts = slots // LANES
    picked = [
        [perf_ref[n, :, p * LANES : (p + 1) * LANES] for p in range(parts)]
        for n in range(3)
    ]

    def load(kind, r, layer):
        if (r, layer) in added.get(kind, {}):
            return added_ref[added[kind][r, layer]]
        return states[kind][kept[kind][r, layer]]

    def store(kind, r, layer, values_in):
        added_ref[added[kind][r, layer]] = values_in

    for r in list(range(-RIM, 0)) + list(range(width, width + RIM)):
        ref, i = (low_ref, r + RIM) if r < 0 else (high_ref, r - width)
        for layer in range(layers):
            at = (i * layers + layer) * local_count + group * GROUP
            values = ref[pl.ds(pl.multiple_of(at, GROUP), GROUP), :].astype(jnp.float32)
            store("half", r, layer, 0.5 * jnp.exp(-values))
    for r in (-3, -2, -1, width - 1, width, width + 1):
        for layer in range(layers):
            face = reciprocal(load("half", r, layer) + load("half", r + 1, layer))
            if r == -1:
                face = face * has_low
            if r == width - 1:
                face = face * has_high
            store("face_x", r, layer, face)
    for r in (-2, -1, width, width + 1):
        for layer in range(layers):
            sides = [
                (load("face_x", r - 1, layer), r - 1), (load("face_x", r, layer), r + 1)
            ]
            top, bottom = cell_faces(load, store, field, r, layer, layers, sides)
            bottom = reciprocal(bottom)
            store("first", r, layer, top * bottom)
            store("inverse", r, layer, bottom)
    for r, face_row, towards in ((0, -1, -1), (width - 1, width - 1, width)):
        for layer in range(layers):
            face = load("face_x", face_row, layer)
            top = states["first"][kept["first"][r, layer]]
            bottom = states["inverse"][kept["inverse"][r, layer]]
            bottom = reciprocal(bottom + face)
            store("first", r, layer, (top + face * field("p0", towards, layer)) * bottom)
            store("inverse", r, layer, bottom)
    for r in (-1, 0, 1, width - 2, width - 1, width):
        second_sweep(load, store, field, r, layers)

    def put(ref, r, layer, values_in):
        store_rows(ref, values_in, GROUP, layer, r, layers, width, halves)

    for r in range(width):
        for layer in range(layers):
            here = load("last", r, layer)
            put(press_ref, r, layer, here)
            if (r, layer) in added["last"]:
                pick(picked[1], here, layer * width + r, lane_of, row_of)
    for first_row, last_row in ((0, 2), (width - 3, width - 1)):
        for r, layer, saturation in transported(load, field, first_row, last_row, layers):
            put(sat_ref, r, layer, saturation)
            pick(picked[2], saturation, layer * width + r, lane_of, row_of)
    for r in range(3, width - 3):
        for layer in range(layers):
            put(sat_ref, r, layer, load("sat", r, layer))
    for n in range(3):
        gathered_ref[n, pl.ds(pl.multiple_of(group * GROUP, GROUP), GROUP), :] = jnp.concatenate(picked[n], axis=1)

    @pl.when(group == local_count // GROUP - 1)
    def _():
        chosen = (
            (lax.broadcasted_iota(jnp.int32, (wells, slots), 0) == well_ref[...])
            .astype(jnp.float32)
            .astype(jnp.bfloat16)
        )
        bhp = pieces(jnp.broadcast_to(bhp_ref[...], (GROUP, wells)))
        bhp = jnp.dot(bhp, chosen, preferred_element_type=jnp.float32)
        perf_bhp = (bhp[:1] + bhp[GROUP : GROUP + 1]) + bhp[2 * GROUP : 2 * GROUP + 1]
        live = (lax.broadcasted_iota(jnp.int32, (1, slots), 1) < count_ref[0]).astype(jnp.float32)
        mobility = water_frac(gathered_ref[2]) * reciprocal(2.0 * gathered_ref[0])
        terms = mobility * (gathered_ref[1] - perf_bhp) * live
        sums = lax.dot_general(
            pieces(terms), chosen, (((1,), (1,)), ((), ())), preferred_element_type=jnp.float32
        )
        rates_ref[...] = (sums[:local_count] + sums[local_count : 2 * local_count]) + sums[
            2 * local_count :
        ]


def invert_panel(columns):
    row = lax.broadcasted_iota(jnp.int32, columns[0].shape, 0)
    columns = list(columns)
    for k in range(PANEL):
        inverse = 1.0 / columns[k][k : k + 1]
        pivot = columns[k]
        for j in range(PANEL):
            if j != k:
                factor = columns[j][k : k + 1] * inverse
                columns[j] = jnp.where(row == k, factor, columns[j] - pivot * factor)
        columns[k] = jnp.where(row == k, inverse, -pivot * inverse)
    return columns


def solve_blocks(gram_matrix, cross_matrix):
    size = gram_matrix.shape[0]
    count = size // PANEL
    row = lax.broadcasted_iota(jnp.int32, gram_matrix.shape, 0)
    lane = lax.broadcasted_iota(jnp.int32, gram_matrix.shape, 1)
    full = gram_matrix + (row == lane).astype(jnp.float32)
    left = [full[i * PANEL : (i + 1) * PANEL] for i in range(count)]
    right = [cross_matrix[i * PANEL : (i + 1) * PANEL] for i in range(count)]
    width = cross_matrix.shape[1]
    for p in range(count):
        columns = [
            [
                jnp.broadcast_to(left[i][:, p * PANEL + j : p * PANEL + j + 1], (PANEL, size))
                for j in range(PANEL)
            ]
            for i in range(count)
        ]
        inverse = invert_panel(columns[p])
        new_left = sum(inverse[j] * left[p][j : j + 1] for j in range(PANEL))
        new_right = sum(inverse[j][:, :width] * right[p][j : j + 1] for j in range(PANEL))
        for i in range(count):
            if i != p:
                for j in range(PANEL):
                    if p + 1 < count:
                        left[i] = left[i] - columns[i][j] * new_left[j : j + 1]
                    right[i] = right[i] - columns[i][j][:, :width] * new_right[j : j + 1]
        left[p], right[p] = new_left, new_right
    return jnp.concatenate(right, axis=0)


def update_kernel(
    dims, rates_ref, own_ref, noise_ref, observed_ref, var_ref, anomaly_ref, perm_ref, out_ref,
    anomaly_buf, perm_buf, sems,
):
    local_count, layers, width = dims
    rows = layers * width
    halves = anomaly_ref.shape[1] // LANES
    copies = [
        pltpu.make_async_copy(anomaly_ref, anomaly_buf, sems.at[0]),
        pltpu.make_async_copy(perm_ref, perm_buf, sems.at[1]),
    ]
    for copy in copies:
        copy.start()
    rates = rates_ref[...]
    members = rates.shape[0]
    spread = jnp.sqrt(INFLATION * var_ref[...])
    mean_rate = jnp.sum(rates, 0, keepdims=True) / members
    scaled = (rates - mean_rate) / (spread * (members - 1) ** 0.5)
    innovation = (observed_ref[...] - own_ref[...]) / spread + noise_ref[...]
    contract = (((1,), (1,)), ((), ()))
    gram_matrix, cross_matrix = (
        lax.dot_general(
            scaled, other, contract, precision=lax.Precision.HIGHEST,
            preferred_element_type=jnp.float32,
        )
        for other in (scaled, innovation)
    )
    weights = solve_blocks(gram_matrix, cross_matrix).T.astype(jnp.bfloat16)
    for copy in copies:
        copy.wait()
    for row in range(rows):
        layer, x = row // width, row % width
        at = row * local_count
        every = jnp.concatenate(
            [
                anomaly_buf[k * rows * local_count + at : k * rows * local_count + at + local_count, :]
                for k in range(members // local_count)
            ],
            axis=0,
        )
        update = jnp.dot(weights, every, preferred_element_type=jnp.float32)
        place = (local_count, layer, x, layers, width, halves)
        store_rows(out_ref, load_rows(perm_buf, *place) + update, *place)


def per_device(
    log_perm,
    start_pressure,
    start_sat,
    source,
    storage,
    well_press,
    perf_cell,
    perf_well,
    perf_count,
    observed,
    obs_var,
    obs_noise,
):
    local_count, layers, strip_width, strip_depth = log_perm.shape
    tile_count = lax.axis_size("tile")
    members = local_count * lax.axis_size("member")
    well_count = well_press.shape[0]
    well_share = well_count // tile_count
    tile_rank = lax.axis_index("tile")
    rows = layers * strip_width
    slots = perf_cell.shape[0]
    flat_perm = fold(log_perm)
    fields = [
        array.reshape(rows, strip_depth) for array in (start_pressure, start_sat, source, storage)
    ]
    in_hbm = pl.BlockSpec(memory_space=pltpu.HBM)
    rim_shape = (RIM * layers * local_count + 4 * GROUP, strip_depth)
    field_scratch = pltpu.VMEM((4 * GROUP, strip_depth), jnp.float32)
    params = pltpu.CompilerParams(vmem_limit_bytes=60 * 2**20)
    up_rows, down_rows, anomaly = pl.pallas_call(
        functools.partial(
            pack_kernel, (local_count, layers, strip_width), (members - 1) ** 0.5
        ),
        out_shape=(
            jax.ShapeDtypeStruct(rim_shape, jnp.bfloat16),
            jax.ShapeDtypeStruct(rim_shape, jnp.bfloat16),
            jax.ShapeDtypeStruct((local_count * rows, strip_depth), jnp.bfloat16),
        ),
        scratch_shapes=[field_scratch, field_scratch],
        compiler_params=params,
        cost_estimate=pl.CostEstimate(
            flops=4 * flat_perm.size, bytes_accessed=8 * flat_perm.size, transcendentals=0
        ),
    )(flat_perm, *fields)
    low_rows, high_rows = send_both(up_rows, down_rows, "tile")
    anomaly_all = lax.all_gather(anomaly, "member", axis=0, tiled=True)

    kept, added = state_slots(layers, strip_width)
    smem, vmem = pl.BlockSpec(memory_space=pltpu.SMEM), pl.BlockSpec(memory_space=pltpu.VMEM)

    def f32(*shape):
        return jax.ShapeDtypeStruct(shape, jnp.float32)

    def whole(array):
        return pl.BlockSpec(array.shape, lambda g: (0,) * array.ndim)

    block = pl.BlockSpec((GROUP * rows * (strip_depth // LANES), LANES), lambda g: (g, 0))
    state_specs = [
        pl.BlockSpec((count, GROUP, strip_depth), lambda g: (0, g, 0))
        for count in [*map(len, kept.values()), 3]
    ]
    shared_scratch = pltpu.VMEM((len(FIELD_NAMES) * rows, 8, strip_depth), jnp.float32)
    cells, wells, press = perf_cell[None], perf_well[None], well_press[None]
    cost = pl.CostEstimate(flops=10**10, bytes_accessed=24 * flat_perm.size, transcendentals=0)
    state = pl.pallas_call(
        functools.partial(inner_kernel, (layers, strip_width)),
        grid=(local_count // GROUP,),
        in_specs=[block] + [whole(array) for array in fields] + [whole(cells)],
        out_specs=state_specs,
        out_shape=[
            f32(count, local_count, strip_depth) for count in map(len, kept.values())
        ]
        + [f32(3, local_count, slots)],
        scratch_shapes=[shared_scratch]
        + [pltpu.VMEM((rows, GROUP, strip_depth), jnp.float32)] * len(WORK),
        compiler_params=params,
        cost_estimate=cost,
    )(flat_perm, *fields, cells)
    flat_press, flat_sat, partial_rates = pl.pallas_call(
        functools.partial(edge_kernel, (local_count, layers, strip_width, tile_count)),
        grid=(local_count // GROUP,),
        in_specs=[smem, whole(low_rows), whole(high_rows)]
        + [whole(array) for array in fields]
        + [smem, whole(cells), whole(wells), whole(press)]
        + state_specs,
        out_specs=[
            block, block, pl.BlockSpec((local_count, well_count), lambda g: (0, 0))
        ],
        out_shape=[
            f32(*flat_perm.shape), f32(*flat_perm.shape), f32(local_count, well_count)
        ],
        scratch_shapes=[
            pltpu.VMEM((sum(map(len, added.values())), GROUP, strip_depth), jnp.float32),
            pltpu.VMEM((3, local_count, slots), jnp.float32),
            shared_scratch,
        ],
        compiler_params=params,
        cost_estimate=cost,
    )(
        tile_rank[None], low_rows, high_rows, *fields, perf_count, cells, wells, press, *state
    )
    own_rates = sum_over(partial_rates, "tile")
    well_rates = lax.dynamic_slice_in_dim(own_rates, tile_rank * well_share, well_share, 1)
    rates_all = lax.all_gather(own_rates, "member", axis=0, tiled=True)
    new_flat = pl.pallas_call(
        functools.partial(update_kernel, (local_count, layers, strip_width)),
        out_shape=jax.ShapeDtypeStruct(flat_perm.shape, jnp.float32),
        in_specs=[vmem] * 5 + [in_hbm] * 2,
        out_specs=vmem,
        scratch_shapes=[
            pltpu.VMEM(anomaly_all.shape, jnp.bfloat16),
            pltpu.VMEM(flat_perm.shape, jnp.float32),
            pltpu.SemaphoreType.DMA((2,)),
        ],
        compiler_params=pltpu.CompilerParams(vmem_limit_bytes=60 * 2**20),
        cost_estimate=pl.CostEstimate(
            flops=12 * members**3, bytes_accessed=16 * flat_perm.size, transcendentals=0
        ),
    )(rates_all, own_rates, obs_noise, observed[None], obs_var[None], anomaly_all, flat_perm)
    new_log_perm = unfold(new_flat, log_perm.shape)
    pressure = unfold(flat_press, log_perm.shape)
    saturation = unfold(flat_sat, log_perm.shape)
    return (new_log_perm, pressure, saturation, well_rates)


def solution(mesh):
    return jax.shard_map(
        per_device,
        mesh=mesh,
        in_specs=(
            P("member", None, "tile", None),
            P(None, "tile", None),
            P(None, "tile", None),
            P(None, "tile", None),
            P(None, "tile", None),
            P(),
            P("tile"),
            P("tile"),
            P("tile"),
            P(),
            P(),
            P("member", None),
        ),
        out_specs=(
            P("member", None, "tile", None),
            P("member", None, "tile", None),
            P("member", None, "tile", None),
            P("member", "tile"),
        ),
        check_vma=False,
    )
```

```python
import functools

import jax
import jax.numpy as jnp
from jax import lax
from jax.experimental import pallas as pl
from jax.experimental.pallas import tpu as pltpu
from jax.sharding import PartitionSpec as P

SWEEPS = 2
RIM = SWEEPS + 1


VERTICAL = 0.5
VISCOSITY_RATIO = 2.0
STEP_COEF = 0.1
INFLATION = 4.0
PANEL = 8
GROUP = 16
LANES = 128


def fold(array):
    members, layers, width, depth = array.shape
    array = array.reshape(members, layers, width, depth // LANES, LANES)
    return array.transpose(0, 1, 3, 2, 4).reshape(-1, LANES)


def unfold(rows, shape):
    members, layers, width, depth = shape
    array = rows.reshape(members, layers, depth // LANES, width, LANES)
    return array.transpose(0, 1, 3, 2, 4).reshape(shape)


def turn(tiles):
    row = lax.broadcasted_iota(jnp.int32, tiles[0].shape, 0)
    for step in (4, 2, 1):
        stays = (row & step) == 0
        turned = list(tiles)
        for i in range(8):
            if i & step == 0:
                first, second = tiles[i], tiles[i + step]
                turned[i] = jnp.where(stays, first, pltpu.roll(second, step, 0))
                turned[i + step] = jnp.where(stays, pltpu.roll(first, 8 - step, 0), second)
        tiles = turned
    return tiles


def tile_rows(member, layer, half, layers, halves):
    return pl.ds(((member * layers + layer) * halves + half) * 8, 8)


def members_down(ref, layer, half, first, count, layers, halves):
    octets = [
        turn([ref[tile_rows(m + i, layer, half, layers, halves), :] for i in range(8)])
        for m in range(first, first + count, 8)
    ]
    return [jnp.concatenate([octet[x] for octet in octets], axis=0) for x in range(8)]


def members_apart(rows_of_x, layer, half, layers, halves):
    for m in range(0, rows_of_x[0].shape[0], 8):
        for i, tile in enumerate(turn([rows[m : m + 8] for rows in rows_of_x])):
            yield tile_rows(m + i, layer, half, layers, halves), tile


def send_both(up_rows, down_rows, axis):
    count = lax.axis_size(axis)
    forward = [(i, i + 1) for i in range(count - 1)]
    backward = [(target, source) for source, target in forward]
    return lax.ppermute(up_rows, axis, forward), lax.ppermute(down_rows, axis, backward)


def sum_over(array, axis):
    count = lax.axis_size(axis)
    stride = count
    while stride > 1:
        radix = 2
        stride //= radix
        groups = [
            [base + low + i * stride for i in range(radix)]
            for base in range(0, count, stride * radix)
            for low in range(stride)
        ]
        array = jnp.sum(lax.all_gather(array, axis, axis_index_groups=groups), 0)
    return array


def reciprocal(values_in):
    guess = pl.reciprocal(values_in, approx=True)
    return guess * (2.0 - values_in * guess)


def pieces(values_in):
    parts = []
    for _ in range(3):
        parts.append(values_in.astype(jnp.bfloat16))
        values_in = values_in - parts[-1].astype(jnp.float32)
    return jnp.concatenate(parts, axis=0)


def water_frac(values_in):
    squared = values_in * values_in
    rest = 1.0 - values_in
    return squared * reciprocal(squared + VISCOSITY_RATIO * rest * rest)


def pack_kernel(
    dims, root, perm_ref, p0_ref, sat_ref, source_ref, storage_ref, up_ref, down_ref, anomaly_ref,
    up_rows, down_rows,
):
    local_count, layers, width = dims
    up_rows[...] = jnp.zeros_like(up_rows)
    down_rows[...] = jnp.zeros_like(down_rows)
    for f, fields_ref in enumerate((p0_ref, sat_ref, source_ref, storage_ref)):
        for layer in range(layers):
            at = f * GROUP + layer * RIM
            first = layer * width
            down_rows[at : at + RIM, :] = fields_ref[first : first + RIM, :]
            up_rows[at : at + RIM, :] = fields_ref[first + width - RIM : first + width, :]
    halves = anomaly_ref.shape[1] // LANES
    block = RIM * layers * local_count
    up_ref[block:, :] = up_rows[...].astype(jnp.bfloat16)
    down_ref[block:, :] = down_rows[...].astype(jnp.bfloat16)
    for layer in range(layers):
        for half in range(halves):
            lanes = slice(half * LANES, (half + 1) * LANES)
            for m in range(0, local_count, GROUP):
                values_of_x = members_down(perm_ref, layer, half, m, GROUP, layers, halves)
                for x, values in enumerate(values_of_x):
                    at = (layer * width + x) * local_count + m
                    anomaly_ref[at : at + GROUP, lanes] = (values / root).astype(jnp.bfloat16)
                    low_values = values.astype(jnp.bfloat16)
                    if x < RIM:
                        at = (x * layers + layer) * local_count + m
                        down_ref[at : at + GROUP, lanes] = low_values
                    if x >= width - RIM:
                        at = ((x - width + RIM) * layers + layer) * local_count + m
                        up_ref[at : at + GROUP, lanes] = low_values


WORK = ("half", "face_x", "face_y", "face_z", "inverse", "first", "last")
FIELD_NAMES = ("p0", "sat", "storage", "base", "ahead", "behind", "frac", "frac_ahead")


def state_slots(layers, width):
    kept, added = {}, {}
    rim = list(range(-RIM, 0)) + list(range(width, width + RIM))
    near = [-2, -1, width, width + 1]

    def place(where, kind, rows, count=layers):
        where[kind] = {}
        for r in rows:
            for layer in range(count):
                where[kind][r, layer] = len(where[kind])

    place(kept, "half", (0, width - 1))
    place(kept, "face_x", [0, 1, 2, width - 4, width - 3, width - 2])
    outer = [0, 1, 2, width - 3, width - 2, width - 1]
    place(kept, "face_y", outer)
    place(kept, "face_z", outer, layers - 1)
    place(kept, "inverse", [0, 1, width - 2, width - 1])
    place(kept, "first", outer)
    place(kept, "last", range(2, width - 2))
    place(kept, "sat", range(3, width - 3))
    place(added, "half", rim)
    place(added, "face_x", [-3, -2, -1, width - 1, width, width + 1])
    place(added, "face_y", near)
    place(added, "face_z", near, layers - 1)
    place(added, "inverse", near + [0, width - 1])
    place(added, "first", near + [0, width - 1])
    place(added, "last", [-1, 0, 1, width - 2, width - 1, width])
    first = 0
    for places in added.values():
        for key in places:
            places[key], first = first, first + 1
    return kept, added


def ahead(values_in):
    return pltpu.roll(values_in, values_in.shape[1] - 1, 1)


def behind(values_in):
    return pltpu.roll(values_in, 1, 1)


def derived_fields(p0, sat, source, storage):
    frac = water_frac(sat)
    return dict(
        p0=p0, sat=sat, storage=storage, base=source + storage * p0,
        ahead=ahead(p0), behind=behind(p0), frac=frac, frac_ahead=ahead(frac),
    )


def cell_faces(load, store, field, r, layer, layers, sides):
    here = load("half", r, layer)
    lane = lax.broadcasted_iota(jnp.int32, here.shape, 1)
    up_y = jnp.where(lane < here.shape[1] - 1, reciprocal(here + ahead(here)), 0.0)
    low_y = behind(up_y)
    store("face_y", r, layer, up_y)
    flow = up_y * field("ahead", r, layer) + low_y * field("behind", r, layer)
    weight = up_y + low_y
    for face, towards in sides:
        flow = flow + face * field("p0", towards, layer)
        weight = weight + face
    if layer + 1 < layers:
        up_z = VERTICAL * reciprocal(here + load("half", r, layer + 1))
        store("face_z", r, layer, up_z)
        flow = flow + up_z * field("p0", r, layer + 1)
        weight = weight + up_z
    if layer > 0:
        low_z = load("face_z", r, layer - 1)
        flow = flow + low_z * field("p0", r, layer - 1)
        weight = weight + low_z
    return field("base", r, layer) + flow, field("storage", r, layer) + weight


def second_sweep(load, store, field, r, layers):
    for layer in range(layers):
        here = load("first", r, layer)
        up_y = load("face_y", r, layer)
        flow = (
            load("face_x", r - 1, layer) * load("first", r - 1, layer)
            + load("face_x", r, layer) * load("first", r + 1, layer)
            + up_y * ahead(here)
            + behind(up_y * here)
        )
        if layer + 1 < layers:
            flow = flow + load("face_z", r, layer) * load("first", r, layer + 1)
        if layer > 0:
            flow = flow + load("face_z", r, layer - 1) * load("first", r, layer - 1)
        store("last", r, layer, (field("base", r, layer) + flow) * load("inverse", r, layer))


def carried(face, low_press, up_press, low_frac, up_frac):
    velocity = face * (low_press - up_press)
    return velocity * jnp.where(velocity > 0, low_frac, up_frac)


def transported(load, field, first_row, last_row, layers):
    def side(r, layer):
        return carried(
            load("face_x", r, layer), load("last", r, layer), load("last", r + 1, layer),
            field("frac", r, layer), field("frac", r + 1, layer),
        )

    low_x = [side(first_row - 1, layer) for layer in range(layers)]
    for r in range(first_row, last_row + 1):
        low_z = None
        for layer in range(layers):
            here = load("last", r, layer)
            frac = field("frac", r, layer)
            up_x = side(r, layer)
            up_y = carried(
                load("face_y", r, layer), here, ahead(here), frac, field("frac_ahead", r, layer)
            )
            change = (low_x[layer] - up_x) + (behind(up_y) - up_y)
            low_x[layer] = up_x
            if low_z is not None:
                change = change + low_z
            if layer + 1 < layers:
                low_z = carried(
                    load("face_z", r, layer), here, load("last", r, layer + 1), frac,
                    field("frac", r, layer + 1),
                )
                change = change - low_z
            yield r, layer, field("sat", r, layer) + STEP_COEF * change


def pick(picked, values_in, row, lane_of, row_of):
    halves = values_in.shape[1] // LANES
    for half in range(halves):
        part = values_in[:, half * LANES : (half + 1) * LANES]
        for p in range(len(picked)):
            found = jnp.take_along_axis(part, lane_of[p], axis=1, mode="promise_in_bounds")
            picked[p] = jnp.where(row_of[p] == row * halves + half, found, picked[p])


def slot_parts(array):
    parts = [array[:, p * LANES : (p + 1) * LANES] for p in range(array.shape[1] // LANES)]
    return [jnp.concatenate([part] * (GROUP // part.shape[0]), axis=0) for part in parts]


def put_fields(dest_ref, field_refs):
    fields = derived_fields(*(ref[...] for ref in field_refs))
    rows, depth = field_refs[0].shape
    for n, name in enumerate(FIELD_NAMES):
        for row in range(rows):
            dest_ref[n * rows + row] = jnp.broadcast_to(fields[name][row : row + 1, :], (8, depth))


def cell_places(cell_ref):
    cells = jnp.broadcast_to(cell_ref[...], (GROUP, cell_ref.shape[1]))
    return slot_parts(cells % LANES), slot_parts(cells // LANES)


def inner_kernel(dims, perm_ref, *refs):
    layers, width = dims
    rows = layers * width
    kept, _ = state_slots(layers, width)
    field_refs, cell_ref, refs = refs[:4], refs[4], refs[5:]
    states, refs = dict(zip(kept, refs)), refs[len(kept) :]
    perf_ref, shared_ref, work_refs = refs[0], refs[1], dict(zip(WORK, refs[2:]))
    slots = cell_ref.shape[1]
    depth = field_refs[0].shape[1]
    halves = depth // LANES

    @pl.when(pl.program_id(0) == 0)
    def _():
        put_fields(shared_ref, field_refs)

    def field(name, r, layer):
        tile = shared_ref[FIELD_NAMES.index(name) * rows + layer * width + r]
        return jnp.concatenate([tile] * (GROUP // 8), axis=0)

    lane_of, row_of = cell_places(cell_ref)
    zeros = [jnp.zeros((GROUP, LANES), jnp.float32)] * (slots // LANES)
    picked = [list(zeros) for _ in range(3)]

    def load(kind, r, layer):
        return work_refs[kind][layer * width + r]

    def store(kind, r, layer, values_in):
        if kind in work_refs:
            work_refs[kind][layer * width + r] = values_in
        if (r, layer) in kept[kind]:
            states[kind][kept[kind][r, layer]] = values_in

    for layer in range(layers):
        lane_tiles = [
            members_down(perm_ref, layer, h, 0, GROUP, layers, halves) for h in range(halves)
        ]
        for r in range(width):
            values = jnp.concatenate([tiles[r] for tiles in lane_tiles], axis=1)
            half = 0.5 * jnp.exp(-values)
            store("half", r, layer, half)
            pick(picked[0], half, layer * width + r, lane_of, row_of)
    for r in range(width - 1):
        for layer in range(layers):
            store(
                "face_x", r, layer,
                reciprocal(load("half", r, layer) + load("half", r + 1, layer)),
            )
    for r in range(width):
        for layer in range(layers):
            sides = []
            if r > 0:
                sides.append((load("face_x", r - 1, layer), r - 1))
            if r < width - 1:
                sides.append((load("face_x", r, layer), r + 1))
            top, bottom = cell_faces(load, store, field, r, layer, layers, sides)
            if 0 < r < width - 1:
                bottom = reciprocal(bottom)
                top = top * bottom
            store("first", r, layer, top)
            store("inverse", r, layer, bottom)
    for r in range(2, width - 2):
        second_sweep(load, store, field, r, layers)
        for layer in range(layers):
            pick(picked[1], load("last", r, layer), layer * width + r, lane_of, row_of)
    for r, layer, saturation in transported(load, field, 3, width - 4, layers):
        store("sat", r, layer, saturation)
        pick(picked[2], saturation, layer * width + r, lane_of, row_of)
    for n in range(3):
        perf_ref[n] = jnp.concatenate(picked[n], axis=1)


def edge_kernel(dims, rank_ref, low_ref, high_ref, *refs):
    local_count, layers, width, tile_count = dims
    rows = layers * width
    depth = low_ref.shape[1]
    halves = depth // LANES
    group = pl.program_id(0)
    kept, added = state_slots(layers, width)
    field_refs, count_ref, cell_ref, well_ref, bhp_ref = refs[:4], refs[4], refs[5], refs[6], refs[7]
    refs = refs[8:]
    states, refs = dict(zip(kept, refs)), refs[len(kept) :]
    perf_ref, press_ref, sat_ref, rates_ref = refs[:4]
    added_ref, gathered_ref, shared_ref, moved_ref = refs[4:]
    rim_rows = RIM * layers * local_count
    has_low = (rank_ref[0] > 0).astype(jnp.float32)
    has_high = (rank_ref[0] < tile_count - 1).astype(jnp.float32)
    rims = [
        derived_fields(
            *(
                ref[rim_rows + f * GROUP : rim_rows + (f + 1) * GROUP, :].astype(jnp.float32)
                for f in range(4)
            )
        )
        for ref in (low_ref, high_ref)
    ]
    slots, wells = cell_ref.shape[1], bhp_ref.shape[1]

    @pl.when(group == 0)
    def _():
        put_fields(shared_ref, field_refs)

    def field(name, r, layer):
        if 0 <= r < width:
            tile = shared_ref[FIELD_NAMES.index(name) * rows + layer * width + r]
            return jnp.concatenate([tile] * (GROUP // 8), axis=0)
        part, at = (rims[0], r + RIM) if r < 0 else (rims[1], r - width)
        at = layer * RIM + at
        return part[name][at : at + 1, :]

    lane_of, row_of = cell_places(cell_ref)
    parts = slots // LANES
    picked = [
        [perf_ref[n, :, p * LANES : (p + 1) * LANES] for p in range(parts)]
        for n in range(3)
    ]

    def load(kind, r, layer):
        if (r, layer) in added.get(kind, {}):
            return added_ref[added[kind][r, layer]]
        return states[kind][kept[kind][r, layer]]

    def store(kind, r, layer, values_in):
        added_ref[added[kind][r, layer]] = values_in

    for r in list(range(-RIM, 0)) + list(range(width, width + RIM)):
        ref, i = (low_ref, r + RIM) if r < 0 else (high_ref, r - width)
        for layer in range(layers):
            at = (i * layers + layer) * local_count + group * GROUP
            values = ref[pl.ds(pl.multiple_of(at, GROUP), GROUP), :].astype(jnp.float32)
            store("half", r, layer, 0.5 * jnp.exp(-values))
    for r in (-3, -2, -1, width - 1, width, width + 1):
        for layer in range(layers):
            face = reciprocal(load("half", r, layer) + load("half", r + 1, layer))
            if r == -1:
                face = face * has_low
            if r == width - 1:
                face = face * has_high
            store("face_x", r, layer, face)
    for r in (-2, -1, width, width + 1):
        for layer in range(layers):
            sides = [
                (load("face_x", r - 1, layer), r - 1), (load("face_x", r, layer), r + 1)
            ]
            top, bottom = cell_faces(load, store, field, r, layer, layers, sides)
            bottom = reciprocal(bottom)
            store("first", r, layer, top * bottom)
            store("inverse", r, layer, bottom)
    for r, face_row, towards in ((0, -1, -1), (width - 1, width - 1, width)):
        for layer in range(layers):
            face = load("face_x", face_row, layer)
            top = states["first"][kept["first"][r, layer]]
            bottom = states["inverse"][kept["inverse"][r, layer]]
            bottom = reciprocal(bottom + face)
            store("first", r, layer, (top + face * field("p0", towards, layer)) * bottom)
            store("inverse", r, layer, bottom)
    for r in (-1, 0, 1, width - 2, width - 1, width):
        second_sweep(load, store, field, r, layers)

    def put(ref, rows_of, layer):
        for h in range(halves):
            rows_of_x = [rows_of(r)[:, h * LANES : (h + 1) * LANES] for r in range(width)]
            for where_tile, tile in members_apart(rows_of_x, layer, h, layers, halves):
                ref[where_tile, :] = tile

    for r in (0, 1, width - 2, width - 1):
        for layer in range(layers):
            pick(picked[1], load("last", r, layer), layer * width + r, lane_of, row_of)
    for first_row, last_row in ((0, 2), (width - 3, width - 1)):
        for r, layer, saturation in transported(load, field, first_row, last_row, layers):
            moved_ref[layer * width + r] = saturation
            pick(picked[2], saturation, layer * width + r, lane_of, row_of)

    def saturation_of(r, layer):
        if (r, layer) in kept["sat"]:
            return load("sat", r, layer)
        return moved_ref[layer * width + r]

    for layer in range(layers):
        put(press_ref, lambda r: load("last", r, layer), layer)
        put(sat_ref, lambda r: saturation_of(r, layer), layer)
    for n in range(3):
        gathered_ref[n, pl.ds(pl.multiple_of(group * GROUP, GROUP), GROUP), :] = jnp.concatenate(picked[n], axis=1)

    @pl.when(group == local_count // GROUP - 1)
    def _():
        chosen = (
            (lax.broadcasted_iota(jnp.int32, (wells, slots), 0) == well_ref[...])
            .astype(jnp.float32)
            .astype(jnp.bfloat16)
        )
        bhp = pieces(jnp.broadcast_to(bhp_ref[...], (GROUP, wells)))
        bhp = jnp.dot(bhp, chosen, preferred_element_type=jnp.float32)
        perf_bhp = (bhp[:1] + bhp[GROUP : GROUP + 1]) + bhp[2 * GROUP : 2 * GROUP + 1]
        live = (lax.broadcasted_iota(jnp.int32, (1, slots), 1) < count_ref[0]).astype(jnp.float32)
        mobility = water_frac(gathered_ref[2]) * reciprocal(2.0 * gathered_ref[0])
        terms = mobility * (gathered_ref[1] - perf_bhp) * live
        sums = lax.dot_general(
            pieces(terms), chosen, (((1,), (1,)), ((), ())), preferred_element_type=jnp.float32
        )
        rates_ref[...] = (sums[:local_count] + sums[local_count : 2 * local_count]) + sums[
            2 * local_count :
        ]


def invert_panel(columns):
    row = lax.broadcasted_iota(jnp.int32, columns[0].shape, 0)
    columns = list(columns)
    for k in range(PANEL):
        inverse = 1.0 / columns[k][k : k + 1]
        pivot = columns[k]
        for j in range(PANEL):
            if j != k:
                factor = columns[j][k : k + 1] * inverse
                columns[j] = jnp.where(row == k, factor, columns[j] - pivot * factor)
        columns[k] = jnp.where(row == k, inverse, -pivot * inverse)
    return columns


def solve_blocks(gram_matrix, cross_matrix):
    size = gram_matrix.shape[0]
    count = size // PANEL
    row = lax.broadcasted_iota(jnp.int32, gram_matrix.shape, 0)
    lane = lax.broadcasted_iota(jnp.int32, gram_matrix.shape, 1)
    full = gram_matrix + (row == lane).astype(jnp.float32)
    left = [full[i * PANEL : (i + 1) * PANEL] for i in range(count)]
    right = [cross_matrix[i * PANEL : (i + 1) * PANEL] for i in range(count)]
    width = cross_matrix.shape[1]
    for p in range(count):
        columns = [
            [
                jnp.broadcast_to(left[i][:, p * PANEL + j : p * PANEL + j + 1], (PANEL, size))
                for j in range(PANEL)
            ]
            for i in range(count)
        ]
        inverse = invert_panel(columns[p])
        new_left = sum(inverse[j] * left[p][j : j + 1] for j in range(PANEL))
        new_right = sum(inverse[j][:, :width] * right[p][j : j + 1] for j in range(PANEL))
        for i in range(count):
            if i != p:
                for j in range(PANEL):
                    if p + 1 < count:
                        left[i] = left[i] - columns[i][j] * new_left[j : j + 1]
                    right[i] = right[i] - columns[i][j][:, :width] * new_right[j : j + 1]
        left[p], right[p] = new_left, new_right
    return jnp.concatenate(right, axis=0)


def update_kernel(
    dims, rates_ref, own_ref, noise_ref, observed_ref, var_ref, anomaly_ref, perm_ref, out_ref,
    anomaly_buf, perm_buf, sems,
):
    local_count, layers, width = dims
    rows = layers * width
    halves = anomaly_ref.shape[1] // LANES
    copies = [
        pltpu.make_async_copy(anomaly_ref, anomaly_buf, sems.at[0]),
        pltpu.make_async_copy(perm_ref, perm_buf, sems.at[1]),
    ]
    for copy in copies:
        copy.start()
    rates = rates_ref[...]
    members = rates.shape[0]
    spread = jnp.sqrt(INFLATION * var_ref[...])
    mean_rate = jnp.sum(rates, 0, keepdims=True) / members
    scaled = (rates - mean_rate) / (spread * (members - 1) ** 0.5)
    innovation = (observed_ref[...] - own_ref[...]) / spread + noise_ref[...]
    contract = (((1,), (1,)), ((), ()))
    gram_matrix, cross_matrix = (
        lax.dot_general(
            scaled, other, contract, precision=lax.Precision.HIGHEST,
            preferred_element_type=jnp.float32,
        )
        for other in (scaled, innovation)
    )
    weights = solve_blocks(gram_matrix, cross_matrix).T.astype(jnp.bfloat16)
    for copy in copies:
        copy.wait()
    for layer in range(layers):
        updates = []
        for x in range(width):
            at = (layer * width + x) * local_count
            every = jnp.concatenate(
                [
                    anomaly_buf[first + at : first + at + local_count, :]
                    for first in range(0, members * rows, rows * local_count)
                ],
                axis=0,
            )
            updates.append(jnp.dot(weights, every, preferred_element_type=jnp.float32))
        for h in range(halves):
            rows_of_x = [update[:, h * LANES : (h + 1) * LANES] for update in updates]
            for where_tile, tile in members_apart(rows_of_x, layer, h, layers, halves):
                out_ref[where_tile, :] = perm_buf[where_tile, :] + tile


def per_device(
    log_perm,
    start_pressure,
    start_sat,
    source,
    storage,
    well_press,
    perf_cell,
    perf_well,
    perf_count,
    observed,
    obs_var,
    obs_noise,
):
    local_count, layers, strip_width, strip_depth = log_perm.shape
    tile_count = lax.axis_size("tile")
    members = local_count * lax.axis_size("member")
    well_count = well_press.shape[0]
    well_share = well_count // tile_count
    tile_rank = lax.axis_index("tile")
    rows = layers * strip_width
    slots = perf_cell.shape[0]
    flat_perm = fold(log_perm)
    fields = [
        array.reshape(rows, strip_depth) for array in (start_pressure, start_sat, source, storage)
    ]
    in_hbm = pl.BlockSpec(memory_space=pltpu.HBM)
    rim_shape = (RIM * layers * local_count + 4 * GROUP, strip_depth)
    field_scratch = pltpu.VMEM((4 * GROUP, strip_depth), jnp.float32)
    params = pltpu.CompilerParams(vmem_limit_bytes=60 * 2**20)
    up_rows, down_rows, anomaly = pl.pallas_call(
        functools.partial(
            pack_kernel, (local_count, layers, strip_width), (members - 1) ** 0.5
        ),
        out_shape=(
            jax.ShapeDtypeStruct(rim_shape, jnp.bfloat16),
            jax.ShapeDtypeStruct(rim_shape, jnp.bfloat16),
            jax.ShapeDtypeStruct((local_count * rows, strip_depth), jnp.bfloat16),
        ),
        scratch_shapes=[field_scratch, field_scratch],
        compiler_params=params,
        cost_estimate=pl.CostEstimate(
            flops=4 * flat_perm.size, bytes_accessed=8 * flat_perm.size, transcendentals=0
        ),
    )(flat_perm, *fields)
    low_rows, high_rows = send_both(up_rows, down_rows, "tile")
    anomaly_all = lax.all_gather(anomaly, "member", axis=0, tiled=True)

    kept, added = state_slots(layers, strip_width)
    smem, vmem = pl.BlockSpec(memory_space=pltpu.SMEM), pl.BlockSpec(memory_space=pltpu.VMEM)

    def f32(*shape):
        return jax.ShapeDtypeStruct(shape, jnp.float32)

    def whole(array):
        return pl.BlockSpec(array.shape, lambda g: (0,) * array.ndim)

    block = pl.BlockSpec((GROUP * rows * (strip_depth // LANES), LANES), lambda g: (g, 0))
    state_specs = [
        pl.BlockSpec((count, GROUP, strip_depth), lambda g: (0, g, 0))
        for count in [*map(len, kept.values()), 3]
    ]
    shared_scratch = pltpu.VMEM((len(FIELD_NAMES) * rows, 8, strip_depth), jnp.float32)
    cells, wells, press = perf_cell[None], perf_well[None], well_press[None]
    cost = pl.CostEstimate(flops=10**10, bytes_accessed=24 * flat_perm.size, transcendentals=0)
    state = pl.pallas_call(
        functools.partial(inner_kernel, (layers, strip_width)),
        grid=(local_count // GROUP,),
        in_specs=[block] + [whole(array) for array in fields] + [whole(cells)],
        out_specs=state_specs,
        out_shape=[
            f32(count, local_count, strip_depth) for count in map(len, kept.values())
        ]
        + [f32(3, local_count, slots)],
        scratch_shapes=[shared_scratch]
        + [pltpu.VMEM((rows, GROUP, strip_depth), jnp.float32)] * len(WORK),
        compiler_params=params,
        cost_estimate=cost,
    )(flat_perm, *fields, cells)
    flat_press, flat_sat, partial_rates = pl.pallas_call(
        functools.partial(edge_kernel, (local_count, layers, strip_width, tile_count)),
        grid=(local_count // GROUP,),
        in_specs=[smem, whole(low_rows), whole(high_rows)]
        + [whole(array) for array in fields]
        + [smem, whole(cells), whole(wells), whole(press)]
        + state_specs,
        out_specs=[
            block, block, pl.BlockSpec((local_count, well_count), lambda g: (0, 0))
        ],
        out_shape=[
            f32(*flat_perm.shape), f32(*flat_perm.shape), f32(local_count, well_count)
        ],
        scratch_shapes=[
            pltpu.VMEM((sum(map(len, added.values())), GROUP, strip_depth), jnp.float32),
            pltpu.VMEM((3, local_count, slots), jnp.float32),
            shared_scratch,
            pltpu.VMEM((rows, GROUP, strip_depth), jnp.float32),
        ],
        compiler_params=params,
        cost_estimate=cost,
    )(
        tile_rank[None], low_rows, high_rows, *fields, perf_count, cells, wells, press, *state
    )
    own_rates = sum_over(partial_rates, "tile")
    well_rates = lax.dynamic_slice_in_dim(own_rates, tile_rank * well_share, well_share, 1)
    rates_all = lax.all_gather(own_rates, "member", axis=0, tiled=True)
    new_flat = pl.pallas_call(
        functools.partial(update_kernel, (local_count, layers, strip_width)),
        out_shape=jax.ShapeDtypeStruct(flat_perm.shape, jnp.float32),
        in_specs=[vmem] * 5 + [in_hbm] * 2,
        out_specs=vmem,
        scratch_shapes=[
            pltpu.VMEM(anomaly_all.shape, jnp.bfloat16),
            pltpu.VMEM(flat_perm.shape, jnp.float32),
            pltpu.SemaphoreType.DMA((2,)),
        ],
        compiler_params=pltpu.CompilerParams(vmem_limit_bytes=60 * 2**20),
        cost_estimate=pl.CostEstimate(
            flops=12 * members**3, bytes_accessed=16 * flat_perm.size, transcendentals=0
        ),
    )(rates_all, own_rates, obs_noise, observed[None], obs_var[None], anomaly_all, flat_perm)
    new_log_perm = unfold(new_flat, log_perm.shape)
    pressure = unfold(flat_press, log_perm.shape)
    saturation = unfold(flat_sat, log_perm.shape)
    return (new_log_perm, pressure, saturation, well_rates)


def solution(mesh):
    return jax.shard_map(
        per_device,
        mesh=mesh,
        in_specs=(
            P("member", None, "tile", None),
            P(None, "tile", None),
            P(None, "tile", None),
            P(None, "tile", None),
            P(None, "tile", None),
            P(),
            P("tile"),
            P("tile"),
            P("tile"),
            P(),
            P(),
            P("member", None),
        ),
        out_specs=(
            P("member", None, "tile", None),
            P("member", None, "tile", None),
            P("member", None, "tile", None),
            P("member", "tile"),
        ),
        check_vma=False,
    )
```

```python
import functools

import jax
import jax.numpy as jnp
from jax import lax
from jax.experimental import pallas as pl
from jax.experimental.pallas import tpu as pltpu
from jax.sharding import PartitionSpec as P

SWEEPS = 2
RIM = SWEEPS + 1


VERTICAL = 0.5
VISCOSITY_RATIO = 2.0
STEP_COEF = 0.1
INFLATION = 4.0
PANEL = 8
GROUP = 16
LANES = 128


def fold(array):
    members, layers, width, depth = array.shape
    array = array.reshape(members, layers, width, depth // LANES, LANES)
    return array.transpose(0, 1, 3, 2, 4).reshape(-1, LANES)


def unfold(rows, shape):
    members, layers, width, depth = shape
    array = rows.reshape(members, layers, depth // LANES, width, LANES)
    return array.transpose(0, 1, 3, 2, 4).reshape(shape)


def turn(tiles):
    row = lax.broadcasted_iota(jnp.int32, tiles[0].shape, 0)
    for step in (4, 2, 1):
        stays = (row & step) == 0
        turned = list(tiles)
        for i in range(8):
            if i & step == 0:
                first, second = tiles[i], tiles[i + step]
                turned[i] = jnp.where(stays, first, pltpu.roll(second, step, 0))
                turned[i + step] = jnp.where(stays, pltpu.roll(first, 8 - step, 0), second)
        tiles = turned
    return tiles


def tile_rows(member, layer, half, layers, halves):
    return pl.ds(((member * layers + layer) * halves + half) * 8, 8)


def members_down(ref, layer, half, first, count, layers, halves):
    octets = [
        turn([ref[tile_rows(m + i, layer, half, layers, halves), :] for i in range(8)])
        for m in range(first, first + count, 8)
    ]
    return [jnp.concatenate([octet[x] for octet in octets], axis=0) for x in range(8)]


def members_apart(rows_of_x, layer, half, layers, halves):
    for m in range(0, rows_of_x[0].shape[0], 8):
        for i, tile in enumerate(turn([rows[m : m + 8] for rows in rows_of_x])):
            yield tile_rows(m + i, layer, half, layers, halves), tile


def send_both(up_rows, down_rows, axis):
    count = lax.axis_size(axis)
    forward = [(i, i + 1) for i in range(count - 1)]
    backward = [(target, source) for source, target in forward]
    return lax.ppermute(up_rows, axis, forward), lax.ppermute(down_rows, axis, backward)


def sum_over(array, axis):
    count = lax.axis_size(axis)
    stride = count
    while stride > 1:
        radix = 2
        stride //= radix
        groups = [
            [base + low + i * stride for i in range(radix)]
            for base in range(0, count, stride * radix)
            for low in range(stride)
        ]
        array = jnp.sum(lax.all_gather(array, axis, axis_index_groups=groups), 0)
    return array


def reciprocal(values_in):
    guess = pl.reciprocal(values_in, approx=True)
    return guess * (2.0 - values_in * guess)


def pieces(values_in):
    parts = []
    for _ in range(3):
        parts.append(values_in.astype(jnp.bfloat16))
        values_in = values_in - parts[-1].astype(jnp.float32)
    return jnp.concatenate(parts, axis=0)


def water_frac(values_in):
    squared = values_in * values_in
    rest = 1.0 - values_in
    return squared * reciprocal(squared + VISCOSITY_RATIO * rest * rest)


def pack_kernel(
    dims, root, perm_ref, p0_ref, sat_ref, source_ref, storage_ref, up_ref, down_ref, anomaly_ref,
    up_rows, down_rows,
):
    local_count, layers, width = dims
    up_rows[...] = jnp.zeros_like(up_rows)
    down_rows[...] = jnp.zeros_like(down_rows)
    for f, fields_ref in enumerate((p0_ref, sat_ref, source_ref, storage_ref)):
        for layer in range(layers):
            at = f * GROUP + layer * RIM
            first = layer * width
            down_rows[at : at + RIM, :] = fields_ref[first : first + RIM, :]
            up_rows[at : at + RIM, :] = fields_ref[first + width - RIM : first + width, :]
    halves = anomaly_ref.shape[1] // LANES
    block = RIM * layers * local_count
    up_ref[block:, :] = up_rows[...].astype(jnp.bfloat16)
    down_ref[block:, :] = down_rows[...].astype(jnp.bfloat16)
    for layer in range(layers):
        for half in range(halves):
            lanes = slice(half * LANES, (half + 1) * LANES)
            for m in range(0, local_count, GROUP):
                values_of_x = members_down(perm_ref, layer, half, m, GROUP, layers, halves)
                for x, values in enumerate(values_of_x):
                    at = (layer * width + x) * local_count + m
                    anomaly_ref[at : at + GROUP, lanes] = (values / root).astype(jnp.bfloat16)
                    low_values = values.astype(jnp.bfloat16)
                    if x < RIM:
                        at = (x * layers + layer) * local_count + m
                        down_ref[at : at + GROUP, lanes] = low_values
                    if x >= width - RIM:
                        at = ((x - width + RIM) * layers + layer) * local_count + m
                        up_ref[at : at + GROUP, lanes] = low_values


WORK = ("half", "face_x", "face_y", "face_z", "inverse", "first", "last")
FIELD_NAMES = ("p0", "sat", "storage", "base", "ahead", "behind", "frac", "frac_ahead")


def state_slots(layers, width):
    kept, added = {}, {}
    rim = list(range(-RIM, 0)) + list(range(width, width + RIM))
    near = [-2, -1, width, width + 1]

    def place(where, kind, rows, count=layers):
        where[kind] = {}
        for r in rows:
            for layer in range(count):
                where[kind][r, layer] = len(where[kind])

    place(kept, "half", (0, width - 1))
    place(kept, "face_x", [0, 1, 2, width - 4, width - 3, width - 2])
    outer = [0, 1, 2, width - 3, width - 2, width - 1]
    place(kept, "face_y", outer)
    place(kept, "face_z", outer, layers - 1)
    place(kept, "inverse", [0, 1, width - 2, width - 1])
    place(kept, "first", outer)
    place(kept, "last", range(2, width - 2))
    place(kept, "sat", range(3, width - 3))
    place(added, "half", rim)
    place(added, "face_x", [-3, -2, -1, width - 1, width, width + 1])
    place(added, "face_y", near)
    place(added, "face_z", near, layers - 1)
    place(added, "inverse", near + [0, width - 1])
    place(added, "first", near + [0, width - 1])
    place(added, "last", [-1, 0, 1, width - 2, width - 1, width])
    first = 0
    for places in added.values():
        for key in places:
            places[key], first = first, first + 1
    return kept, added


def ahead(values_in):
    return pltpu.roll(values_in, values_in.shape[1] - 1, 1)


def behind(values_in):
    return pltpu.roll(values_in, 1, 1)


def derived_fields(p0, sat, source, storage):
    frac = water_frac(sat)
    return dict(
        p0=p0, sat=sat, storage=storage, base=source + storage * p0,
        ahead=ahead(p0), behind=behind(p0), frac=frac, frac_ahead=ahead(frac),
    )


def cell_faces(load, store, field, r, layer, layers, sides):
    here = load("half", r, layer)
    lane = lax.broadcasted_iota(jnp.int32, here.shape, 1)
    up_y = jnp.where(lane < here.shape[1] - 1, reciprocal(here + ahead(here)), 0.0)
    low_y = behind(up_y)
    store("face_y", r, layer, up_y)
    flow = up_y * field("ahead", r, layer) + low_y * field("behind", r, layer)
    weight = up_y + low_y
    for face, towards in sides:
        flow = flow + face * field("p0", towards, layer)
        weight = weight + face
    if layer + 1 < layers:
        up_z = VERTICAL * reciprocal(here + load("half", r, layer + 1))
        store("face_z", r, layer, up_z)
        flow = flow + up_z * field("p0", r, layer + 1)
        weight = weight + up_z
    if layer > 0:
        low_z = load("face_z", r, layer - 1)
        flow = flow + low_z * field("p0", r, layer - 1)
        weight = weight + low_z
    return field("base", r, layer) + flow, field("storage", r, layer) + weight


def second_sweep(load, store, field, r, layers):
    for layer in range(layers):
        here = load("first", r, layer)
        up_y = load("face_y", r, layer)
        flow = (
            load("face_x", r - 1, layer) * load("first", r - 1, layer)
            + load("face_x", r, layer) * load("first", r + 1, layer)
            + up_y * ahead(here)
            + behind(up_y * here)
        )
        if layer + 1 < layers:
            flow = flow + load("face_z", r, layer) * load("first", r, layer + 1)
        if layer > 0:
            flow = flow + load("face_z", r, layer - 1) * load("first", r, layer - 1)
        store("last", r, layer, (field("base", r, layer) + flow) * load("inverse", r, layer))


def carried(face, low_press, up_press, low_frac, up_frac):
    velocity = face * (low_press - up_press)
    return velocity * jnp.where(velocity > 0, low_frac, up_frac)


def transported(load, field, first_row, last_row, layers):
    def side(r, layer):
        return carried(
            load("face_x", r, layer), load("last", r, layer), load("last", r + 1, layer),
            field("frac", r, layer), field("frac", r + 1, layer),
        )

    low_x = [side(first_row - 1, layer) for layer in range(layers)]
    for r in range(first_row, last_row + 1):
        low_z = None
        for layer in range(layers):
            here = load("last", r, layer)
            frac = field("frac", r, layer)
            up_x = side(r, layer)
            up_y = carried(
                load("face_y", r, layer), here, ahead(here), frac, field("frac_ahead", r, layer)
            )
            change = (low_x[layer] - up_x) + (behind(up_y) - up_y)
            low_x[layer] = up_x
            if low_z is not None:
                change = change + low_z
            if layer + 1 < layers:
                low_z = carried(
                    load("face_z", r, layer), here, load("last", r, layer + 1), frac,
                    field("frac", r, layer + 1),
                )
                change = change - low_z
            yield r, layer, field("sat", r, layer) + STEP_COEF * change


def put_places(dest_ref, cell_ref, cell_rows, depth):
    at = lax.broadcasted_iota(jnp.int32, (depth, cell_ref.shape[1]), 0)
    for i, row in enumerate(cell_rows):
        found = at + row * depth == cell_ref[...]
        dest_ref[i * depth : (i + 1) * depth, :] = found.astype(jnp.float32).astype(jnp.bfloat16)


def find(found, values_of, place):
    every = jnp.concatenate([pieces(values) for _, values in values_of], axis=0)
    sums = jnp.dot(every, place, preferred_element_type=jnp.float32)
    for i, (n, _) in enumerate(values_of):
        part = sums[i * 3 * GROUP : (i + 1) * 3 * GROUP]
        found[n] = part if found[n] is None else found[n] + part


def joined(part):
    return (part[:GROUP] + part[GROUP : 2 * GROUP]) + part[2 * GROUP :]


def put_fields(dest_ref, field_refs):
    fields = derived_fields(*(ref[...] for ref in field_refs))
    rows, depth = field_refs[0].shape
    for n, name in enumerate(FIELD_NAMES):
        for row in range(rows):
            dest_ref[n * rows + row] = jnp.broadcast_to(fields[name][row : row + 1, :], (8, depth))


def inner_kernel(dims, perm_ref, *refs):
    layers, width = dims
    rows = layers * width
    kept, _ = state_slots(layers, width)
    field_refs, cell_ref, refs = refs[:4], refs[4], refs[5:]
    states, refs = dict(zip(kept, refs)), refs[len(kept) :]
    perf_ref, shared_ref, place_ref = refs[:3]
    work_refs = dict(zip(WORK, refs[3:]))
    depth = field_refs[0].shape[1]
    halves = depth // LANES

    @pl.when(pl.program_id(0) == 0)
    def _():
        put_fields(shared_ref, field_refs)
        put_places(place_ref, cell_ref, range(rows), depth)

    def field(name, r, layer):
        tile = shared_ref[FIELD_NAMES.index(name) * rows + layer * width + r]
        return jnp.concatenate([tile] * (GROUP // 8), axis=0)

    found = [None] * 3

    def load(kind, r, layer):
        return work_refs[kind][layer * width + r]

    def store(kind, r, layer, values_in):
        if kind in work_refs:
            work_refs[kind][layer * width + r] = values_in
        if (r, layer) in kept[kind]:
            states[kind][kept[kind][r, layer]] = values_in

    for layer in range(layers):
        lane_tiles = [
            members_down(perm_ref, layer, h, 0, GROUP, layers, halves) for h in range(halves)
        ]
        for r in range(width):
            values = jnp.concatenate([tiles[r] for tiles in lane_tiles], axis=1)
            half = 0.5 * jnp.exp(-values)
            store("half", r, layer, half)
    for r in range(width - 1):
        for layer in range(layers):
            store(
                "face_x", r, layer,
                reciprocal(load("half", r, layer) + load("half", r + 1, layer)),
            )
    for r in range(width):
        for layer in range(layers):
            sides = []
            if r > 0:
                sides.append((load("face_x", r - 1, layer), r - 1))
            if r < width - 1:
                sides.append((load("face_x", r, layer), r + 1))
            top, bottom = cell_faces(load, store, field, r, layer, layers, sides)
            if 0 < r < width - 1:
                bottom = reciprocal(bottom)
                top = top * bottom
            store("first", r, layer, top)
            store("inverse", r, layer, bottom)
    for r in range(2, width - 2):
        second_sweep(load, store, field, r, layers)
    for r, layer, saturation in transported(load, field, 3, width - 4, layers):
        store("sat", r, layer, saturation)
    for r in range(width):
        for layer in range(layers):
            values_of = [(0, load("half", r, layer))]
            if (r, layer) in kept["last"]:
                values_of.append((1, load("last", r, layer)))
            if (r, layer) in kept["sat"]:
                values_of.append((2, states["sat"][kept["sat"][r, layer]]))
            first = (layer * width + r) * depth
            find(found, values_of, place_ref[first : first + depth, :])
    for n in range(3):
        perf_ref[n] = joined(found[n])


def edge_kernel(dims, rank_ref, low_ref, high_ref, *refs):
    local_count, layers, width, tile_count = dims
    rows = layers * width
    depth = low_ref.shape[1]
    halves = depth // LANES
    group = pl.program_id(0)
    kept, added = state_slots(layers, width)
    field_refs, count_ref, cell_ref, well_ref, bhp_ref = refs[:4], refs[4], refs[5], refs[6], refs[7]
    refs = refs[8:]
    states, refs = dict(zip(kept, refs)), refs[len(kept) :]
    perf_ref, press_ref, sat_ref, rates_ref = refs[:4]
    added_ref, gathered_ref, shared_ref, moved_ref, place_ref = refs[4:]
    rim_rows = RIM * layers * local_count
    has_low = (rank_ref[0] > 0).astype(jnp.float32)
    has_high = (rank_ref[0] < tile_count - 1).astype(jnp.float32)
    rims = [
        derived_fields(
            *(
                ref[rim_rows + f * GROUP : rim_rows + (f + 1) * GROUP, :].astype(jnp.float32)
                for f in range(4)
            )
        )
        for ref in (low_ref, high_ref)
    ]
    slots, wells = cell_ref.shape[1], bhp_ref.shape[1]

    moved = [layer * width + r for layer in range(layers) for r in range(width)]
    moved = [row for row in moved if (row % width, row // width) not in kept["sat"]]

    @pl.when(group == 0)
    def _():
        put_fields(shared_ref, field_refs)
        put_places(place_ref, cell_ref, moved, depth)

    def field(name, r, layer):
        if 0 <= r < width:
            tile = shared_ref[FIELD_NAMES.index(name) * rows + layer * width + r]
            return jnp.concatenate([tile] * (GROUP // 8), axis=0)
        part, at = (rims[0], r + RIM) if r < 0 else (rims[1], r - width)
        at = layer * RIM + at
        return part[name][at : at + 1, :]

    found = [None] * 3

    def load(kind, r, layer):
        if (r, layer) in added.get(kind, {}):
            return added_ref[added[kind][r, layer]]
        return states[kind][kept[kind][r, layer]]

    def store(kind, r, layer, values_in):
        added_ref[added[kind][r, layer]] = values_in

    for r in list(range(-RIM, 0)) + list(range(width, width + RIM)):
        ref, i = (low_ref, r + RIM) if r < 0 else (high_ref, r - width)
        for layer in range(layers):
            at = (i * layers + layer) * local_count + group * GROUP
            values = ref[pl.ds(pl.multiple_of(at, GROUP), GROUP), :].astype(jnp.float32)
            store("half", r, layer, 0.5 * jnp.exp(-values))
    for r in (-3, -2, -1, width - 1, width, width + 1):
        for layer in range(layers):
            face = reciprocal(load("half", r, layer) + load("half", r + 1, layer))
            if r == -1:
                face = face * has_low
            if r == width - 1:
                face = face * has_high
            store("face_x", r, layer, face)
    for r in (-2, -1, width, width + 1):
        for layer in range(layers):
            sides = [
                (load("face_x", r - 1, layer), r - 1), (load("face_x", r, layer), r + 1)
            ]
            top, bottom = cell_faces(load, store, field, r, layer, layers, sides)
            bottom = reciprocal(bottom)
            store("first", r, layer, top * bottom)
            store("inverse", r, layer, bottom)
    for r, face_row, towards in ((0, -1, -1), (width - 1, width - 1, width)):
        for layer in range(layers):
            face = load("face_x", face_row, layer)
            top = states["first"][kept["first"][r, layer]]
            bottom = states["inverse"][kept["inverse"][r, layer]]
            bottom = reciprocal(bottom + face)
            store("first", r, layer, (top + face * field("p0", towards, layer)) * bottom)
            store("inverse", r, layer, bottom)
    for r in (-1, 0, 1, width - 2, width - 1, width):
        second_sweep(load, store, field, r, layers)

    def put(ref, rows_of, layer):
        for h in range(halves):
            rows_of_x = [rows_of(r)[:, h * LANES : (h + 1) * LANES] for r in range(width)]
            for where_tile, tile in members_apart(rows_of_x, layer, h, layers, halves):
                ref[where_tile, :] = tile

    for first_row, last_row in ((0, 2), (width - 3, width - 1)):
        for r, layer, saturation in transported(load, field, first_row, last_row, layers):
            moved_ref[layer * width + r] = saturation

    def saturation_of(r, layer):
        if (r, layer) in kept["sat"]:
            return load("sat", r, layer)
        return moved_ref[layer * width + r]

    for layer in range(layers):
        put(press_ref, lambda r: load("last", r, layer), layer)
        put(sat_ref, lambda r: saturation_of(r, layer), layer)
    for i, row in enumerate(moved):
        r, layer = row % width, row // width
        values_of = [(2, moved_ref[row])]
        if (r, layer) in added["last"]:
            values_of.append((1, load("last", r, layer)))
        find(found, values_of, place_ref[i * depth : (i + 1) * depth, :])
    for n in range(3):
        total = perf_ref[n] if found[n] is None else perf_ref[n] + joined(found[n])
        gathered_ref[n, pl.ds(pl.multiple_of(group * GROUP, GROUP), GROUP), :] = total

    @pl.when(group == local_count // GROUP - 1)
    def _():
        chosen = (
            (lax.broadcasted_iota(jnp.int32, (wells, slots), 0) == well_ref[...])
            .astype(jnp.float32)
            .astype(jnp.bfloat16)
        )
        bhp = pieces(jnp.broadcast_to(bhp_ref[...], (GROUP, wells)))
        bhp = jnp.dot(bhp, chosen, preferred_element_type=jnp.float32)
        perf_bhp = (bhp[:1] + bhp[GROUP : GROUP + 1]) + bhp[2 * GROUP : 2 * GROUP + 1]
        live = (lax.broadcasted_iota(jnp.int32, (1, slots), 1) < count_ref[0]).astype(jnp.float32)
        mobility = water_frac(gathered_ref[2]) * reciprocal(2.0 * gathered_ref[0])
        terms = mobility * (gathered_ref[1] - perf_bhp) * live
        sums = lax.dot_general(
            pieces(terms), chosen, (((1,), (1,)), ((), ())), preferred_element_type=jnp.float32
        )
        rates_ref[...] = (sums[:local_count] + sums[local_count : 2 * local_count]) + sums[
            2 * local_count :
        ]


def invert_panel(columns):
    row = lax.broadcasted_iota(jnp.int32, columns[0].shape, 0)
    columns = list(columns)
    for k in range(PANEL):
        inverse = 1.0 / columns[k][k : k + 1]
        pivot = columns[k]
        for j in range(PANEL):
            if j != k:
                factor = columns[j][k : k + 1] * inverse
                columns[j] = jnp.where(row == k, factor, columns[j] - pivot * factor)
        columns[k] = jnp.where(row == k, inverse, -pivot * inverse)
    return columns


def solve_blocks(gram_matrix, cross_matrix):
    size = gram_matrix.shape[0]
    count = size // PANEL
    row = lax.broadcasted_iota(jnp.int32, gram_matrix.shape, 0)
    lane = lax.broadcasted_iota(jnp.int32, gram_matrix.shape, 1)
    full = gram_matrix + (row == lane).astype(jnp.float32)
    left = [full[i * PANEL : (i + 1) * PANEL] for i in range(count)]
    right = [cross_matrix[i * PANEL : (i + 1) * PANEL] for i in range(count)]
    width = cross_matrix.shape[1]
    for p in range(count):
        columns = [
            [
                jnp.broadcast_to(left[i][:, p * PANEL + j : p * PANEL + j + 1], (PANEL, size))
                for j in range(PANEL)
            ]
            for i in range(count)
        ]
        inverse = invert_panel(columns[p])
        new_left = sum(inverse[j] * left[p][j : j + 1] for j in range(PANEL))
        new_right = sum(inverse[j][:, :width] * right[p][j : j + 1] for j in range(PANEL))
        for i in range(count):
            if i != p:
                for j in range(PANEL):
                    if p + 1 < count:
                        left[i] = left[i] - columns[i][j] * new_left[j : j + 1]
                    right[i] = right[i] - columns[i][j][:, :width] * new_right[j : j + 1]
        left[p], right[p] = new_left, new_right
    return jnp.concatenate(right, axis=0)


def update_kernel(
    dims, rank_ref, rates_ref, own_ref, noise_ref, observed_ref, var_ref, anomaly_ref, perm_ref,
    out_ref, held_ref, anomaly_buf, perm_buf, sems,
):
    local_count, layers, width = dims
    rows = layers * width
    halves = anomaly_ref.shape[1] // LANES
    copies = [
        pltpu.make_async_copy(anomaly_ref, anomaly_buf, sems.at[0]),
        pltpu.make_async_copy(perm_ref, perm_buf, sems.at[1]),
    ]
    for copy in copies:
        copy.start()
    wells, share = own_ref.shape[1], held_ref.shape[1]
    held_ref[...] = pltpu.roll(
        own_ref[...], lax.rem(wells - rank_ref[0] * share, wells), 1
    )[:, :share]
    rates = rates_ref[...]
    members = rates.shape[0]
    spread = jnp.sqrt(INFLATION * var_ref[...])
    mean_rate = jnp.sum(rates, 0, keepdims=True) / members
    scaled = (rates - mean_rate) / (spread * (members - 1) ** 0.5)
    innovation = (observed_ref[...] - own_ref[...]) / spread + noise_ref[...]
    contract = (((1,), (1,)), ((), ()))
    gram_matrix, cross_matrix = (
        lax.dot_general(
            scaled, other, contract, precision=lax.Precision.HIGHEST,
            preferred_element_type=jnp.float32,
        )
        for other in (scaled, innovation)
    )
    weights = solve_blocks(gram_matrix, cross_matrix).T.astype(jnp.bfloat16)
    for copy in copies:
        copy.wait()
    for layer in range(layers):
        updates = []
        for x in range(width):
            at = (layer * width + x) * local_count
            every = jnp.concatenate(
                [
                    anomaly_buf[first + at : first + at + local_count, :]
                    for first in range(0, members * rows, rows * local_count)
                ],
                axis=0,
            )
            updates.append(jnp.dot(weights, every, preferred_element_type=jnp.float32))
        for h in range(halves):
            rows_of_x = [update[:, h * LANES : (h + 1) * LANES] for update in updates]
            for where_tile, tile in members_apart(rows_of_x, layer, h, layers, halves):
                out_ref[where_tile, :] = perm_buf[where_tile, :] + tile


def per_device(
    log_perm,
    start_pressure,
    start_sat,
    source,
    storage,
    well_press,
    perf_cell,
    perf_well,
    perf_count,
    observed,
    obs_var,
    obs_noise,
):
    local_count, layers, strip_width, strip_depth = log_perm.shape
    tile_count = lax.axis_size("tile")
    members = local_count * lax.axis_size("member")
    well_count = well_press.shape[0]
    well_share = well_count // tile_count
    tile_rank = lax.axis_index("tile")
    rows = layers * strip_width
    slots = perf_cell.shape[0]
    flat_perm = fold(log_perm)
    fields = [
        array.reshape(rows, strip_depth) for array in (start_pressure, start_sat, source, storage)
    ]
    in_hbm = pl.BlockSpec(memory_space=pltpu.HBM)
    rim_shape = (RIM * layers * local_count + 4 * GROUP, strip_depth)
    field_scratch = pltpu.VMEM((4 * GROUP, strip_depth), jnp.float32)
    params = pltpu.CompilerParams(vmem_limit_bytes=60 * 2**20)
    up_rows, down_rows, anomaly = pl.pallas_call(
        functools.partial(
            pack_kernel, (local_count, layers, strip_width), (members - 1) ** 0.5
        ),
        out_shape=(
            jax.ShapeDtypeStruct(rim_shape, jnp.bfloat16),
            jax.ShapeDtypeStruct(rim_shape, jnp.bfloat16),
            jax.ShapeDtypeStruct((local_count * rows, strip_depth), jnp.bfloat16),
        ),
        scratch_shapes=[field_scratch, field_scratch],
        compiler_params=params,
        cost_estimate=pl.CostEstimate(
            flops=4 * flat_perm.size, bytes_accessed=8 * flat_perm.size, transcendentals=0
        ),
    )(flat_perm, *fields)
    low_rows, high_rows = send_both(up_rows, down_rows, "tile")
    anomaly_all = lax.all_gather(anomaly, "member", axis=0, tiled=True)

    kept, added = state_slots(layers, strip_width)
    smem, vmem = pl.BlockSpec(memory_space=pltpu.SMEM), pl.BlockSpec(memory_space=pltpu.VMEM)

    def f32(*shape):
        return jax.ShapeDtypeStruct(shape, jnp.float32)

    def whole(array):
        return pl.BlockSpec(array.shape, lambda g: (0,) * array.ndim)

    block = pl.BlockSpec((GROUP * rows * (strip_depth // LANES), LANES), lambda g: (g, 0))
    state_specs = [
        pl.BlockSpec((count, GROUP, strip_depth), lambda g: (0, g, 0))
        for count in [*map(len, kept.values()), 3]
    ]
    shared_scratch = pltpu.VMEM((len(FIELD_NAMES) * rows, 8, strip_depth), jnp.float32)
    place_scratch = pltpu.VMEM((rows * strip_depth, slots), jnp.bfloat16)
    cells, wells, press = perf_cell[None], perf_well[None], well_press[None]
    cost = pl.CostEstimate(flops=10**10, bytes_accessed=24 * flat_perm.size, transcendentals=0)
    state = pl.pallas_call(
        functools.partial(inner_kernel, (layers, strip_width)),
        grid=(local_count // GROUP,),
        in_specs=[block] + [whole(array) for array in fields] + [whole(cells)],
        out_specs=state_specs,
        out_shape=[
            f32(count, local_count, strip_depth) for count in map(len, kept.values())
        ]
        + [f32(3, local_count, slots)],
        scratch_shapes=[shared_scratch, place_scratch]
        + [pltpu.VMEM((rows, GROUP, strip_depth), jnp.float32)] * len(WORK),
        compiler_params=params,
        cost_estimate=cost,
    )(flat_perm, *fields, cells)
    flat_press, flat_sat, partial_rates = pl.pallas_call(
        functools.partial(edge_kernel, (local_count, layers, strip_width, tile_count)),
        grid=(local_count // GROUP,),
        in_specs=[smem, whole(low_rows), whole(high_rows)]
        + [whole(array) for array in fields]
        + [smem, whole(cells), whole(wells), whole(press)]
        + state_specs,
        out_specs=[
            block, block, pl.BlockSpec((local_count, well_count), lambda g: (0, 0))
        ],
        out_shape=[
            f32(*flat_perm.shape), f32(*flat_perm.shape), f32(local_count, well_count)
        ],
        scratch_shapes=[
            pltpu.VMEM((sum(map(len, added.values())), GROUP, strip_depth), jnp.float32),
            pltpu.VMEM((3, local_count, slots), jnp.float32),
            shared_scratch,
            pltpu.VMEM((rows, GROUP, strip_depth), jnp.float32),
            place_scratch,
        ],
        compiler_params=params,
        cost_estimate=cost,
    )(
        tile_rank[None], low_rows, high_rows, *fields, perf_count, cells, wells, press, *state
    )
    own_rates = sum_over(partial_rates, "tile")
    rates_all = lax.all_gather(own_rates, "member", axis=0, tiled=True)
    new_flat, well_rates = pl.pallas_call(
        functools.partial(update_kernel, (local_count, layers, strip_width)),
        out_shape=(f32(*flat_perm.shape), f32(local_count, well_share)),
        in_specs=[smem] + [vmem] * 5 + [in_hbm] * 2,
        out_specs=(vmem, vmem),
        scratch_shapes=[
            pltpu.VMEM(anomaly_all.shape, jnp.bfloat16),
            pltpu.VMEM(flat_perm.shape, jnp.float32),
            pltpu.SemaphoreType.DMA((2,)),
        ],
        compiler_params=pltpu.CompilerParams(vmem_limit_bytes=60 * 2**20),
        cost_estimate=pl.CostEstimate(
            flops=12 * members**3, bytes_accessed=16 * flat_perm.size, transcendentals=0
        ),
    )(tile_rank[None], rates_all, own_rates, obs_noise, observed[None], obs_var[None], anomaly_all, flat_perm)
    new_log_perm = unfold(new_flat, log_perm.shape)
    pressure = unfold(flat_press, log_perm.shape)
    saturation = unfold(flat_sat, log_perm.shape)
    return (new_log_perm, pressure, saturation, well_rates)


def solution(mesh):
    return jax.shard_map(
        per_device,
        mesh=mesh,
        in_specs=(
            P("member", None, "tile", None),
            P(None, "tile", None),
            P(None, "tile", None),
            P(None, "tile", None),
            P(None, "tile", None),
            P(),
            P("tile"),
            P("tile"),
            P("tile"),
            P(),
            P(),
            P("member", None),
        ),
        out_specs=(
            P("member", None, "tile", None),
            P("member", None, "tile", None),
            P("member", None, "tile", None),
            P("member", "tile"),
        ),
        check_vma=False,
    )
```

```python
import functools

import jax
import jax.numpy as jnp
from jax import lax
from jax.experimental import pallas as pl
from jax.experimental.pallas import tpu as pltpu
from jax.sharding import PartitionSpec as P

SWEEPS = 2
RIM = SWEEPS + 1


VERTICAL = 0.5
VISCOSITY_RATIO = 2.0
STEP_COEF = 0.1
INFLATION = 4.0
PANEL = 8
GROUP = 16
INNER_GRANT = 121 * 2**19
UPDATE_GRANT = 598 * 2**20 // 10
LANES = 128


def fold(array):
    members, layers, width, depth = array.shape
    array = array.reshape(members, layers, width, depth // LANES, LANES)
    return array.transpose(0, 1, 3, 2, 4).reshape(-1, LANES)


def unfold(rows, shape):
    members, layers, width, depth = shape
    array = rows.reshape(members, layers, depth // LANES, width, LANES)
    return array.transpose(0, 1, 3, 2, 4).reshape(shape)


def turn(tiles):
    row = lax.broadcasted_iota(jnp.int32, tiles[0].shape, 0)
    for step in (4, 2, 1):
        stays = (row & step) == 0
        turned = list(tiles)
        for i in range(8):
            if i & step == 0:
                first, second = tiles[i], tiles[i + step]
                turned[i] = jnp.where(stays, first, pltpu.roll(second, step, 0))
                turned[i + step] = jnp.where(stays, pltpu.roll(first, 8 - step, 0), second)
        tiles = turned
    return tiles


def tile_rows(member, layer, half, layers, halves):
    return pl.ds(((member * layers + layer) * halves + half) * 8, 8)


def members_down(ref, layer, half, first, count, layers, halves):
    octets = [
        turn([ref[tile_rows(m + i, layer, half, layers, halves), :] for i in range(8)])
        for m in range(first, first + count, 8)
    ]
    return [jnp.concatenate([octet[x] for octet in octets], axis=0) for x in range(8)]


def members_apart(rows_of_x, layer, half, layers, halves):
    for m in range(0, rows_of_x[0].shape[0], 8):
        for i, tile in enumerate(turn([rows[m : m + 8] for rows in rows_of_x])):
            yield tile_rows(m + i, layer, half, layers, halves), tile


def send_both(up_rows, down_rows, axis):
    count = lax.axis_size(axis)
    forward = [(i, i + 1) for i in range(count - 1)]
    backward = [(target, source) for source, target in forward]
    return lax.ppermute(up_rows, axis, forward), lax.ppermute(down_rows, axis, backward)


def sum_over(array, axis):
    count = lax.axis_size(axis)
    stride = count
    while stride > 1:
        radix = 2
        stride //= radix
        groups = [
            [base + low + i * stride for i in range(radix)]
            for base in range(0, count, stride * radix)
            for low in range(stride)
        ]
        array = jnp.sum(lax.all_gather(array, axis, axis_index_groups=groups), 0)
    return array


def reciprocal(values_in):
    guess = pl.reciprocal(values_in, approx=True)
    return guess * (2.0 - values_in * guess)


def pieces(values_in):
    parts = []
    for _ in range(3):
        parts.append(values_in.astype(jnp.bfloat16))
        values_in = values_in - parts[-1].astype(jnp.float32)
    return jnp.concatenate(parts, axis=0)


def water_frac(values_in):
    squared = values_in * values_in
    rest = 1.0 - values_in
    return squared * reciprocal(squared + VISCOSITY_RATIO * rest * rest)


def pack_kernel(
    dims, scale, perm_ref, p0_ref, sat_ref, source_ref, storage_ref, up_ref, down_ref, anomaly_ref,
    up_rows, down_rows,
):
    layers, width = dims
    halves = anomaly_ref.shape[2] // LANES
    block = RIM * layers

    @pl.when(pl.program_id(0) == 0)
    def _():
        up_rows[...] = jnp.zeros_like(up_rows)
        down_rows[...] = jnp.zeros_like(down_rows)
        for f, fields_ref in enumerate((p0_ref, sat_ref, source_ref, storage_ref)):
            for layer in range(layers):
                at = layer * RIM
                first = layer * width
                down_rows[f, at : at + RIM, :] = fields_ref[first : first + RIM, :]
                up_rows[f, at : at + RIM, :] = fields_ref[first + width - RIM : first + width, :]

    for i in range(2):
        f = 2 * i + pl.program_id(0)
        up_ref[block + i] = up_rows[f].astype(jnp.bfloat16)
        down_ref[block + i] = down_rows[f].astype(jnp.bfloat16)
    for layer in range(layers):
        for half in range(halves):
            lanes = slice(half * LANES, (half + 1) * LANES)
            values_of_x = members_down(perm_ref, layer, half, 0, GROUP, layers, halves)
            for x, values in enumerate(values_of_x):
                anomaly_ref[layer * width + x, :, lanes] = (values * scale).astype(jnp.bfloat16)
                low_values = values.astype(jnp.bfloat16)
                if x < RIM:
                    down_ref[x * layers + layer, :, lanes] = low_values
                if x >= width - RIM:
                    up_ref[(x - width + RIM) * layers + layer, :, lanes] = low_values


WORK = ("half", "face_x", "face_y", "face_z", "inverse", "first", "last")
FIELD_NAMES = ("p0", "sat", "storage", "base", "ahead", "behind", "frac", "frac_ahead")


def state_slots(layers, width):
    kept, added = {}, {}
    rim = list(range(-RIM, 0)) + list(range(width, width + RIM))
    near = [-2, -1, width, width + 1]

    def place(where, kind, rows, count=layers):
        where[kind] = {}
        for r in rows:
            for layer in range(count):
                where[kind][r, layer] = len(where[kind])

    place(kept, "half", (0, width - 1))
    place(kept, "face_x", [0, 1, 2, width - 4, width - 3, width - 2])
    outer = [0, 1, 2, width - 3, width - 2, width - 1]
    place(kept, "face_y", outer)
    place(kept, "face_z", outer, layers - 1)
    place(kept, "inverse", [0, 1, width - 2, width - 1])
    place(kept, "first", outer)
    place(kept, "last", range(2, width - 2))
    place(kept, "sat", range(3, width - 3))
    place(added, "half", rim)
    place(added, "face_x", [-3, -2, -1, width - 1, width, width + 1])
    place(added, "face_y", near)
    place(added, "face_z", near, layers - 1)
    place(added, "inverse", near + [0, width - 1])
    place(added, "first", near + [0, width - 1])
    place(added, "last", [-1, 0, 1, width - 2, width - 1, width])
    first = 0
    for places in added.values():
        for key in places:
            places[key], first = first, first + 1
    return kept, added


def ahead(values_in):
    return pltpu.roll(values_in, values_in.shape[1] - 1, 1)


def behind(values_in):
    return pltpu.roll(values_in, 1, 1)


def derived_fields(p0, sat, source, storage):
    frac = water_frac(sat)
    return dict(
        p0=p0, sat=sat, storage=storage, base=source + storage * p0,
        ahead=ahead(p0), behind=behind(p0), frac=frac, frac_ahead=ahead(frac),
    )


def cell_faces(load, store, field, r, layer, layers, sides):
    here = load("half", r, layer)
    lane = lax.broadcasted_iota(jnp.int32, here.shape, 1)
    up_y = jnp.where(lane < here.shape[1] - 1, reciprocal(here + ahead(here)), 0.0)
    low_y = behind(up_y)
    store("face_y", r, layer, up_y)
    flow = up_y * field("ahead", r, layer) + low_y * field("behind", r, layer)
    weight = up_y + low_y
    for face, towards in sides:
        flow = flow + face * field("p0", towards, layer)
        weight = weight + face
    if layer + 1 < layers:
        up_z = VERTICAL * reciprocal(here + load("half", r, layer + 1))
        store("face_z", r, layer, up_z)
        flow = flow + up_z * field("p0", r, layer + 1)
        weight = weight + up_z
    if layer > 0:
        low_z = load("face_z", r, layer - 1)
        flow = flow + low_z * field("p0", r, layer - 1)
        weight = weight + low_z
    return field("base", r, layer) + flow, field("storage", r, layer) + weight


def second_sweep(load, store, field, r, layers):
    for layer in range(layers):
        here = load("first", r, layer)
        up_y = load("face_y", r, layer)
        flow = (
            load("face_x", r - 1, layer) * load("first", r - 1, layer)
            + load("face_x", r, layer) * load("first", r + 1, layer)
            + up_y * ahead(here)
            + behind(up_y * here)
        )
        if layer + 1 < layers:
            flow = flow + load("face_z", r, layer) * load("first", r, layer + 1)
        if layer > 0:
            flow = flow + load("face_z", r, layer - 1) * load("first", r, layer - 1)
        store("last", r, layer, (field("base", r, layer) + flow) * load("inverse", r, layer))


def carried(face, low_press, up_press, low_frac, up_frac):
    velocity = face * (low_press - up_press)
    return velocity * jnp.where(velocity > 0, low_frac, up_frac)


def transported(load, field, first_row, last_row, layers):
    def side(r, layer):
        return carried(
            load("face_x", r, layer), load("last", r, layer), load("last", r + 1, layer),
            field("frac", r, layer), field("frac", r + 1, layer),
        )

    low_x = [side(first_row - 1, layer) for layer in range(layers)]
    for r in range(first_row, last_row + 1):
        low_z = None
        for layer in range(layers):
            here = load("last", r, layer)
            frac = field("frac", r, layer)
            up_x = side(r, layer)
            up_y = carried(
                load("face_y", r, layer), here, ahead(here), frac, field("frac_ahead", r, layer)
            )
            change = (low_x[layer] - up_x) + (behind(up_y) - up_y)
            low_x[layer] = up_x
            if low_z is not None:
                change = change + low_z
            if layer + 1 < layers:
                low_z = carried(
                    load("face_z", r, layer), here, load("last", r, layer + 1), frac,
                    field("frac", r, layer + 1),
                )
                change = change - low_z
            yield r, layer, field("sat", r, layer) + STEP_COEF * change


def put_places(dest_ref, cell_ref, cell_rows, depth):
    at = lax.broadcasted_iota(jnp.int32, (depth, cell_ref.shape[1]), 0)
    for i, row in enumerate(cell_rows):
        found = at + row * depth == cell_ref[...]
        dest_ref[i * depth : (i + 1) * depth, :] = found.astype(jnp.float32).astype(jnp.bfloat16)


def find(found, values_of, place):
    every = jnp.concatenate([pieces(values) for _, values in values_of], axis=0)
    sums = jnp.dot(every, place, preferred_element_type=jnp.float32)
    for i, (n, _) in enumerate(values_of):
        part = sums[i * 3 * GROUP : (i + 1) * 3 * GROUP]
        found[n] = part if found[n] is None else found[n] + part


def joined(part):
    return (part[:GROUP] + part[GROUP : 2 * GROUP]) + part[2 * GROUP :]


def put_fields(dest_ref, field_refs):
    fields = derived_fields(*(ref[...] for ref in field_refs))
    rows, depth = field_refs[0].shape
    for n, name in enumerate(FIELD_NAMES):
        for row in range(rows):
            dest_ref[n * rows + row] = jnp.broadcast_to(fields[name][row : row + 1, :], (8, depth))


def inner_kernel(dims, rank_ref, count_ref, perm_ref, *refs):
    layers, width = dims
    rows = layers * width
    kept, _ = state_slots(layers, width)
    field_refs, cell_ref, refs = refs[:4], refs[4], refs[5:]
    states, refs = dict(zip(kept, refs)), refs[len(kept) :]
    perf_ref, shared_ref, place_ref = refs[:3]
    work_refs = dict(zip(WORK, refs[3:]))
    depth = field_refs[0].shape[1]
    halves = depth // LANES

    @pl.when(pl.program_id(0) == 0)
    def _():
        put_fields(shared_ref, field_refs)
        put_places(place_ref, cell_ref, range(rows), depth)

    def field(name, r, layer):
        tile = shared_ref[FIELD_NAMES.index(name) * rows + layer * width + r]
        return jnp.concatenate([tile] * (GROUP // 8), axis=0)

    found = [None] * 3

    def load(kind, r, layer):
        return work_refs[kind][layer * width + r]

    def store(kind, r, layer, values_in):
        if kind in work_refs:
            work_refs[kind][layer * width + r] = values_in
        if (r, layer) in kept[kind]:
            states[kind][kept[kind][r, layer]] = values_in

    for layer in range(layers):
        lane_tiles = [
            members_down(perm_ref, layer, h, 0, GROUP, layers, halves) for h in range(halves)
        ]
        for r in range(width):
            values = jnp.concatenate([tiles[r] for tiles in lane_tiles], axis=1)
            half = 0.5 * jnp.exp(-values)
            store("half", r, layer, half)
    for r in range(width - 1):
        for layer in range(layers):
            store(
                "face_x", r, layer,
                reciprocal(load("half", r, layer) + load("half", r + 1, layer)),
            )
    for r in range(width):
        for layer in range(layers):
            sides = []
            if r > 0:
                sides.append((load("face_x", r - 1, layer), r - 1))
            if r < width - 1:
                sides.append((load("face_x", r, layer), r + 1))
            top, bottom = cell_faces(load, store, field, r, layer, layers, sides)
            if 0 < r < width - 1:
                bottom = reciprocal(bottom)
                top = top * bottom
            store("first", r, layer, top)
            store("inverse", r, layer, bottom)
    for r in range(2, width - 2):
        second_sweep(load, store, field, r, layers)
    for r, layer, saturation in transported(load, field, 3, width - 4, layers):
        store("sat", r, layer, saturation)
    for r in range(width):
        for layer in range(layers):
            values_of = [(0, load("half", r, layer))]
            if (r, layer) in kept["last"]:
                values_of.append((1, load("last", r, layer)))
            if (r, layer) in kept["sat"]:
                values_of.append((2, states["sat"][kept["sat"][r, layer]]))
            first = (layer * width + r) * depth
            find(found, values_of, place_ref[first : first + depth, :])
    for n in range(3):
        perf_ref[n] = joined(found[n])


def edge_kernel(dims, rank_ref, low_ref, high_ref, *refs):
    local_count, layers, width, tile_count = dims
    rows = layers * width
    depth = low_ref.shape[1]
    halves = depth // LANES
    group = pl.program_id(0)
    kept, added = state_slots(layers, width)
    field_refs, count_ref, cell_ref, well_ref, bhp_ref = refs[:4], refs[4], refs[5], refs[6], refs[7]
    refs = refs[8:]
    states, refs = dict(zip(kept, refs)), refs[len(kept) :]
    perf_ref, press_ref, sat_ref, rates_ref = refs[:4]
    added_ref, gathered_ref, shared_ref, moved_ref, place_ref = refs[4:]
    rim_rows = RIM * layers * local_count
    has_low = (rank_ref[0] > 0).astype(jnp.float32)
    has_high = (rank_ref[0] < tile_count - 1).astype(jnp.float32)
    rims = [
        derived_fields(
            *(
                ref[rim_rows + f * GROUP : rim_rows + (f + 1) * GROUP, :].astype(jnp.float32)
                for f in range(4)
            )
        )
        for ref in (low_ref, high_ref)
    ]
    slots, wells = cell_ref.shape[1], bhp_ref.shape[1]

    moved = [layer * width + r for layer in range(layers) for r in range(width)]
    moved = [row for row in moved if (row % width, row // width) not in kept["sat"]]

    @pl.when(group == 0)
    def _():
        put_fields(shared_ref, field_refs)
        put_places(place_ref, cell_ref, moved, depth)

    def field(name, r, layer):
        if 0 <= r < width:
            tile = shared_ref[FIELD_NAMES.index(name) * rows + layer * width + r]
            return jnp.concatenate([tile] * (GROUP // 8), axis=0)
        part, at = (rims[0], r + RIM) if r < 0 else (rims[1], r - width)
        at = layer * RIM + at
        return part[name][at : at + 1, :]

    found = [None] * 3

    def load(kind, r, layer):
        if (r, layer) in added.get(kind, {}):
            return added_ref[added[kind][r, layer]]
        return states[kind][kept[kind][r, layer]]

    def store(kind, r, layer, values_in):
        added_ref[added[kind][r, layer]] = values_in

    for r in list(range(-RIM, 0)) + list(range(width, width + RIM)):
        ref, i = (low_ref, r + RIM) if r < 0 else (high_ref, r - width)
        for layer in range(layers):
            at = (i * layers + layer) * local_count + group * GROUP
            values = ref[pl.ds(pl.multiple_of(at, GROUP), GROUP), :].astype(jnp.float32)
            store("half", r, layer, 0.5 * jnp.exp(-values))
    for r in (-3, -2, -1, width - 1, width, width + 1):
        for layer in range(layers):
            face = reciprocal(load("half", r, layer) + load("half", r + 1, layer))
            if r == -1:
                face = face * has_low
            if r == width - 1:
                face = face * has_high
            store("face_x", r, layer, face)
    for r in (-2, -1, width, width + 1):
        for layer in range(layers):
            sides = [
                (load("face_x", r - 1, layer), r - 1), (load("face_x", r, layer), r + 1)
            ]
            top, bottom = cell_faces(load, store, field, r, layer, layers, sides)
            bottom = reciprocal(bottom)
            store("first", r, layer, top * bottom)
            store("inverse", r, layer, bottom)
    for r, face_row, towards in ((0, -1, -1), (width - 1, width - 1, width)):
        for layer in range(layers):
            face = load("face_x", face_row, layer)
            top = states["first"][kept["first"][r, layer]]
            bottom = states["inverse"][kept["inverse"][r, layer]]
            bottom = reciprocal(bottom + face)
            store("first", r, layer, (top + face * field("p0", towards, layer)) * bottom)
            store("inverse", r, layer, bottom)
    for r in (-1, 0, 1, width - 2, width - 1, width):
        second_sweep(load, store, field, r, layers)

    def put(ref, rows_of, layer):
        for h in range(halves):
            rows_of_x = [rows_of(r)[:, h * LANES : (h + 1) * LANES] for r in range(width)]
            for where_tile, tile in members_apart(rows_of_x, layer, h, layers, halves):
                ref[where_tile, :] = tile

    for first_row, last_row in ((0, 2), (width - 3, width - 1)):
        for r, layer, saturation in transported(load, field, first_row, last_row, layers):
            moved_ref[layer * width + r] = saturation

    def saturation_of(r, layer):
        if (r, layer) in kept["sat"]:
            return load("sat", r, layer)
        return moved_ref[layer * width + r]

    for layer in range(layers):
        put(press_ref, lambda r: load("last", r, layer), layer)
        put(sat_ref, lambda r: saturation_of(r, layer), layer)
    for i, row in enumerate(moved):
        r, layer = row % width, row // width
        values_of = [(2, moved_ref[row])]
        if (r, layer) in added["last"]:
            values_of.append((1, load("last", r, layer)))
        find(found, values_of, place_ref[i * depth : (i + 1) * depth, :])
    for n in range(3):
        total = perf_ref[n] if found[n] is None else perf_ref[n] + joined(found[n])
        gathered_ref[n, pl.ds(pl.multiple_of(group * GROUP, GROUP), GROUP), :] = total

    @pl.when(group == local_count // GROUP - 1)
    def _():
        chosen = (
            (lax.broadcasted_iota(jnp.int32, (wells, slots), 0) == well_ref[...])
            .astype(jnp.float32)
            .astype(jnp.bfloat16)
        )
        bhp = pieces(jnp.broadcast_to(bhp_ref[...], (GROUP, wells)))
        bhp = jnp.dot(bhp, chosen, preferred_element_type=jnp.float32)
        perf_bhp = (bhp[:1] + bhp[GROUP : GROUP + 1]) + bhp[2 * GROUP : 2 * GROUP + 1]
        live = (lax.broadcasted_iota(jnp.int32, (1, slots), 1) < count_ref[0]).astype(jnp.float32)
        mobility = water_frac(gathered_ref[2]) * reciprocal(2.0 * gathered_ref[0])
        terms = mobility * (gathered_ref[1] - perf_bhp) * live
        sums = lax.dot_general(
            pieces(terms), chosen, (((1,), (1,)), ((), ())), preferred_element_type=jnp.float32
        )
        rates_ref[...] = (sums[:local_count] + sums[local_count : 2 * local_count]) + sums[
            2 * local_count :
        ]


def invert_panel(columns):
    row = lax.broadcasted_iota(jnp.int32, columns[0].shape, 0)
    columns = list(columns)
    for k in range(PANEL):
        inverse = reciprocal(columns[k][k : k + 1])
        pivot = columns[k]
        for j in range(PANEL):
            if j != k:
                factor = columns[j][k : k + 1] * inverse
                columns[j] = jnp.where(row == k, factor, columns[j] - pivot * factor)
        columns[k] = jnp.where(row == k, inverse, -pivot * inverse)
    return columns


def solve_blocks(gram_matrix, cross_matrix):
    size = gram_matrix.shape[0]
    count = size // PANEL
    row = lax.broadcasted_iota(jnp.int32, gram_matrix.shape, 0)
    lane = lax.broadcasted_iota(jnp.int32, gram_matrix.shape, 1)
    full = gram_matrix + (row == lane).astype(jnp.float32)
    left = [full[i * PANEL : (i + 1) * PANEL] for i in range(count)]
    right = [cross_matrix[i * PANEL : (i + 1) * PANEL] for i in range(count)]
    width = cross_matrix.shape[1]
    for p in range(count):
        columns = [
            [
                jnp.broadcast_to(left[i][:, p * PANEL + j : p * PANEL + j + 1], (PANEL, size))
                for j in range(PANEL)
            ]
            for i in range(count)
        ]
        inverse = invert_panel(columns[p])
        new_left = sum(inverse[j] * left[p][j : j + 1] for j in range(PANEL))
        new_right = sum(inverse[j][:, :width] * right[p][j : j + 1] for j in range(PANEL))
        for i in range(count):
            if i != p:
                for j in range(PANEL):
                    if p + 1 < count:
                        left[i] = left[i] - columns[i][j] * new_left[j : j + 1]
                    right[i] = right[i] - columns[i][j][:, :width] * new_right[j : j + 1]
        left[p], right[p] = new_left, new_right
    return jnp.concatenate(right, axis=0)


def update_kernel(
    dims, rank_ref, rates_ref, own_ref, noise_ref, observed_ref, var_ref, anomaly_ref, perm_ref,
    out_ref, held_ref, anomaly_buf, perm_buf, sems,
):
    local_count, layers, width = dims
    rows = layers * width
    halves = anomaly_ref.shape[1] // LANES
    copies = [
        pltpu.make_async_copy(anomaly_ref, anomaly_buf, sems.at[0]),
        pltpu.make_async_copy(perm_ref, perm_buf, sems.at[1]),
    ]
    for copy in copies:
        copy.start()
    wells, share = own_ref.shape[1], held_ref.shape[1]
    held_ref[...] = pltpu.roll(
        own_ref[...], lax.rem(wells - rank_ref[0] * share, wells), 1
    )[:, :share]
    rates = rates_ref[...]
    members = rates.shape[0]
    spread = jnp.sqrt(INFLATION * var_ref[...])
    mean_rate = jnp.sum(rates, 0, keepdims=True) / members
    scaled = (rates - mean_rate) / (spread * (members - 1) ** 0.5)
    innovation = (observed_ref[...] - own_ref[...]) / spread + noise_ref[...]
    contract = (((1,), (1,)), ((), ()))
    gram_matrix, cross_matrix = (
        lax.dot_general(
            scaled, other, contract, precision=lax.Precision.HIGHEST,
            preferred_element_type=jnp.float32,
        )
        for other in (scaled, innovation)
    )
    weights = solve_blocks(gram_matrix, cross_matrix).T.astype(jnp.bfloat16)
    for copy in copies:
        copy.wait()
    for layer in range(layers):
        updates = []
        for x in range(width):
            at = (layer * width + x) * local_count
            every = jnp.concatenate(
                [
                    anomaly_buf[first + at : first + at + local_count, :]
                    for first in range(0, members * rows, rows * local_count)
                ],
                axis=0,
            )
            updates.append(jnp.dot(weights, every, preferred_element_type=jnp.float32))
        for h in range(halves):
            rows_of_x = [update[:, h * LANES : (h + 1) * LANES] for update in updates]
            for where_tile, tile in members_apart(rows_of_x, layer, h, layers, halves):
                out_ref[where_tile, :] = perm_buf[where_tile, :] + tile


def per_device(
    log_perm,
    start_pressure,
    start_sat,
    source,
    storage,
    well_press,
    perf_cell,
    perf_well,
    perf_count,
    observed,
    obs_var,
    obs_noise,
):
    local_count, layers, strip_width, strip_depth = log_perm.shape
    tile_count = lax.axis_size("tile")
    members = local_count * lax.axis_size("member")
    well_count = well_press.shape[0]
    well_share = well_count // tile_count
    tile_rank = lax.axis_index("tile")
    rows = layers * strip_width
    slots = perf_cell.shape[0]
    flat_perm = fold(log_perm)
    fields = [
        array.reshape(rows, strip_depth) for array in (start_pressure, start_sat, source, storage)
    ]
    in_hbm = pl.BlockSpec(memory_space=pltpu.HBM)
    rim_blocks = RIM * layers + 2
    field_scratch = pltpu.VMEM((4, GROUP, strip_depth), jnp.float32)
    params = pltpu.CompilerParams(vmem_limit_bytes=INNER_GRANT)

    def whole(array):
        return pl.BlockSpec(array.shape, lambda g: (0,) * array.ndim)

    def stacked(count):
        return pl.BlockSpec((count, GROUP, strip_depth), lambda g: (0, g, 0))

    block = pl.BlockSpec((GROUP * rows * (strip_depth // LANES), LANES), lambda g: (g, 0))
    up_rows, down_rows, anomaly = (
        array.reshape(-1, strip_depth)
        for array in pl.pallas_call(
            functools.partial(pack_kernel, (layers, strip_width), (members - 1) ** -0.5),
            grid=(local_count // GROUP,),
            in_specs=[block] + [whole(array) for array in fields],
            out_specs=[stacked(rim_blocks), stacked(rim_blocks), stacked(rows)],
            out_shape=[
                jax.ShapeDtypeStruct((count, local_count, strip_depth), jnp.bfloat16)
                for count in (rim_blocks, rim_blocks, rows)
            ],
            scratch_shapes=[field_scratch, field_scratch],
            compiler_params=params,
            cost_estimate=pl.CostEstimate(
                flops=4 * flat_perm.size, bytes_accessed=8 * flat_perm.size, transcendentals=0
            ),
        )(flat_perm, *fields)
    )
    low_rows, high_rows = send_both(up_rows, down_rows, "tile")
    anomaly_all = lax.all_gather(anomaly, "member", axis=0, tiled=True)

    kept, added = state_slots(layers, strip_width)
    smem, vmem = pl.BlockSpec(memory_space=pltpu.SMEM), pl.BlockSpec(memory_space=pltpu.VMEM)

    def f32(*shape):
        return jax.ShapeDtypeStruct(shape, jnp.float32)

    state_specs = [stacked(count) for count in [*map(len, kept.values()), 3]]
    shared_scratch = pltpu.VMEM((len(FIELD_NAMES) * rows, 8, strip_depth), jnp.float32)
    place_scratch = pltpu.VMEM((rows * strip_depth, slots), jnp.bfloat16)
    cells, wells, press = perf_cell[None], perf_well[None], well_press[None]
    cost = pl.CostEstimate(flops=10**10, bytes_accessed=24 * flat_perm.size, transcendentals=0)
    state = pl.pallas_call(
        functools.partial(inner_kernel, (layers, strip_width)),
        grid=(local_count // GROUP,),
        in_specs=[smem, smem, block] + [whole(array) for array in fields] + [whole(cells)],
        out_specs=state_specs,
        out_shape=[
            f32(count, local_count, strip_depth) for count in map(len, kept.values())
        ]
        + [f32(3, local_count, slots)],
        scratch_shapes=[shared_scratch, place_scratch]
        + [pltpu.VMEM((rows, GROUP, strip_depth), jnp.float32)] * len(WORK),
        compiler_params=params,
        cost_estimate=cost,
    )(tile_rank[None], perf_count, flat_perm, *fields, cells)
    flat_press, flat_sat, partial_rates = pl.pallas_call(
        functools.partial(edge_kernel, (local_count, layers, strip_width, tile_count)),
        grid=(local_count // GROUP,),
        in_specs=[smem, whole(low_rows), whole(high_rows)]
        + [whole(array) for array in fields]
        + [smem, whole(cells), whole(wells), whole(press)]
        + state_specs,
        out_specs=[
            block, block, pl.BlockSpec((local_count, well_count), lambda g: (0, 0))
        ],
        out_shape=[
            f32(*flat_perm.shape), f32(*flat_perm.shape), f32(local_count, well_count)
        ],
        scratch_shapes=[
            pltpu.VMEM((sum(map(len, added.values())), GROUP, strip_depth), jnp.float32),
            pltpu.VMEM((3, local_count, slots), jnp.float32),
            shared_scratch,
            pltpu.VMEM((rows, GROUP, strip_depth), jnp.float32),
            place_scratch,
        ],
        compiler_params=params,
        cost_estimate=cost,
    )(
        tile_rank[None], low_rows, high_rows, *fields, perf_count, cells, wells, press, *state
    )
    own_rates = sum_over(partial_rates, "tile")
    rates_all = lax.all_gather(own_rates, "member", axis=0, tiled=True)
    new_flat, well_rates = pl.pallas_call(
        functools.partial(update_kernel, (local_count, layers, strip_width)),
        out_shape=(f32(*flat_perm.shape), f32(local_count, well_share)),
        in_specs=[smem] + [vmem] * 5 + [in_hbm] * 2,
        out_specs=(vmem, vmem),
        scratch_shapes=[
            pltpu.VMEM(anomaly_all.shape, jnp.bfloat16),
            pltpu.VMEM(flat_perm.shape, jnp.float32),
            pltpu.SemaphoreType.DMA((2,)),
        ],
        compiler_params=pltpu.CompilerParams(vmem_limit_bytes=UPDATE_GRANT),
        cost_estimate=pl.CostEstimate(
            flops=12 * members**3, bytes_accessed=16 * flat_perm.size, transcendentals=0
        ),
    )(tile_rank[None], rates_all, own_rates, obs_noise, observed[None], obs_var[None], anomaly_all, flat_perm)
    new_log_perm = unfold(new_flat, log_perm.shape)
    pressure = unfold(flat_press, log_perm.shape)
    saturation = unfold(flat_sat, log_perm.shape)
    return (new_log_perm, pressure, saturation, well_rates)


def solution(mesh):
    return jax.shard_map(
        per_device,
        mesh=mesh,
        in_specs=(
            P("member", None, "tile", None),
            P(None, "tile", None),
            P(None, "tile", None),
            P(None, "tile", None),
            P(None, "tile", None),
            P(),
            P("tile"),
            P("tile"),
            P("tile"),
            P(),
            P(),
            P("member", None),
        ),
        out_specs=(
            P("member", None, "tile", None),
            P("member", None, "tile", None),
            P("member", None, "tile", None),
            P("member", "tile"),
        ),
        check_vma=False,
    )
```

```python
import functools

import jax
import jax.numpy as jnp
from jax import lax
from jax.experimental import pallas as pl
from jax.experimental.pallas import tpu as pltpu
from jax.sharding import PartitionSpec as P

SWEEPS = 2
RIM = SWEEPS + 1


VERTICAL = 0.5
VISCOSITY_RATIO = 2.0
STEP_COEF = 0.1
INFLATION = 4.0
PANEL = 8
GROUP = 16
LANES = 128


def fold(array):
    members, layers, width, depth = array.shape
    array = array.reshape(members, layers, width, depth // LANES, LANES)
    return array.transpose(0, 1, 3, 2, 4).reshape(-1, LANES)


def unfold(rows, shape):
    members, layers, width, depth = shape
    array = rows.reshape(members, layers, depth // LANES, width, LANES)
    return array.transpose(0, 1, 3, 2, 4).reshape(shape)


def turn(tiles):
    row = lax.broadcasted_iota(jnp.int32, tiles[0].shape, 0)
    for step in (4, 2, 1):
        stays = (row & step) == 0
        turned = list(tiles)
        for i in range(8):
            if i & step == 0:
                first, second = tiles[i], tiles[i + step]
                turned[i] = jnp.where(stays, first, pltpu.roll(second, step, 0))
                turned[i + step] = jnp.where(stays, pltpu.roll(first, 8 - step, 0), second)
        tiles = turned
    return tiles


def tile_rows(member, layer, half, layers, halves):
    return pl.ds(((member * layers + layer) * halves + half) * 8, 8)


def members_down(ref, layer, half, first, count, layers, halves):
    octets = [
        turn([ref[tile_rows(m + i, layer, half, layers, halves), :] for i in range(8)])
        for m in range(first, first + count, 8)
    ]
    return [jnp.concatenate([octet[x] for octet in octets], axis=0) for x in range(8)]


def members_apart(rows_of_x, layer, half, layers, halves):
    for m in range(0, rows_of_x[0].shape[0], 8):
        for i, tile in enumerate(turn([rows[m : m + 8] for rows in rows_of_x])):
            yield tile_rows(m + i, layer, half, layers, halves), tile


def send_both(up_rows, down_rows, axis):
    count = lax.axis_size(axis)
    forward = [(i, i + 1) for i in range(count - 1)]
    backward = [(target, source) for source, target in forward]
    return lax.ppermute(up_rows, axis, forward), lax.ppermute(down_rows, axis, backward)


def reciprocal(values_in):
    guess = pl.reciprocal(values_in, approx=True)
    return guess * (2.0 - values_in * guess)


def pieces(values_in):
    parts = []
    for _ in range(3):
        parts.append(values_in.astype(jnp.bfloat16))
        values_in = values_in - parts[-1].astype(jnp.float32)
    return jnp.concatenate(parts, axis=0)


def water_frac(values_in):
    squared = values_in * values_in
    rest = 1.0 - values_in
    return squared * reciprocal(squared + VISCOSITY_RATIO * rest * rest)


def pack_kernel(
    dims, scale, perm_ref, p0_ref, sat_ref, source_ref, storage_ref, up_ref, down_ref, anomaly_ref,
    up_rows, down_rows,
):
    layers, width = dims
    halves = anomaly_ref.shape[2] // LANES
    block = RIM * layers

    @pl.when(pl.program_id(0) == 0)
    def _():
        up_rows[...] = jnp.zeros_like(up_rows)
        down_rows[...] = jnp.zeros_like(down_rows)
        for f, fields_ref in enumerate((p0_ref, sat_ref, source_ref, storage_ref)):
            for layer in range(layers):
                at = layer * RIM
                first = layer * width
                down_rows[f, at : at + RIM, :] = fields_ref[first : first + RIM, :]
                up_rows[f, at : at + RIM, :] = fields_ref[first + width - RIM : first + width, :]

    for i in range(2):
        f = 2 * i + pl.program_id(0)
        up_ref[block + i] = up_rows[f].astype(jnp.bfloat16)
        down_ref[block + i] = down_rows[f].astype(jnp.bfloat16)
    for layer in range(layers):
        for half in range(halves):
            lanes = slice(half * LANES, (half + 1) * LANES)
            values_of_x = members_down(perm_ref, layer, half, 0, GROUP, layers, halves)
            for x, values in enumerate(values_of_x):
                anomaly_ref[layer * width + x, :, lanes] = (values * scale).astype(jnp.bfloat16)
                low_values = values.astype(jnp.bfloat16)
                if x < RIM:
                    down_ref[x * layers + layer, :, lanes] = low_values
                if x >= width - RIM:
                    up_ref[(x - width + RIM) * layers + layer, :, lanes] = low_values


WORK = ("half", "face_x", "face_y", "face_z", "inverse", "first", "last")
FIELD_NAMES = ("p0", "sat", "storage", "base", "ahead", "behind", "frac", "frac_ahead")


def state_slots(layers, width):
    kept, added = {}, {}
    rim = list(range(-RIM, 0)) + list(range(width, width + RIM))
    near = [-2, -1, width, width + 1]

    def place(where, kind, rows, count=layers):
        where[kind] = {}
        for r in rows:
            for layer in range(count):
                where[kind][r, layer] = len(where[kind])

    place(kept, "half", (0, width - 1))
    place(kept, "face_x", [0, 1, 2, width - 4, width - 3, width - 2])
    outer = [0, 1, 2, width - 3, width - 2, width - 1]
    place(kept, "face_y", outer)
    place(kept, "face_z", outer, layers - 1)
    place(kept, "inverse", [0, 1, width - 2, width - 1])
    place(kept, "first", outer)
    place(kept, "last", range(2, width - 2))
    place(kept, "sat", range(3, width - 3))
    place(added, "half", rim)
    place(added, "face_x", [-3, -2, -1, width - 1, width, width + 1])
    place(added, "face_y", near)
    place(added, "face_z", near, layers - 1)
    place(added, "inverse", near + [0, width - 1])
    place(added, "first", near + [0, width - 1])
    place(added, "last", [-1, 0, 1, width - 2, width - 1, width])
    first = 0
    for places in added.values():
        for key in places:
            places[key], first = first, first + 1
    return kept, added


def ahead(values_in):
    return pltpu.roll(values_in, values_in.shape[1] - 1, 1)


def behind(values_in):
    return pltpu.roll(values_in, 1, 1)


def derived_fields(p0, sat, source, storage):
    frac = water_frac(sat)
    return dict(
        p0=p0, sat=sat, storage=storage, base=source + storage * p0,
        ahead=ahead(p0), behind=behind(p0), frac=frac, frac_ahead=ahead(frac),
    )


def cell_faces(load, store, field, r, layer, layers, sides):
    here = load("half", r, layer)
    lane = lax.broadcasted_iota(jnp.int32, here.shape, 1)
    up_y = jnp.where(lane < here.shape[1] - 1, reciprocal(here + ahead(here)), 0.0)
    low_y = behind(up_y)
    store("face_y", r, layer, up_y)
    flow = up_y * field("ahead", r, layer) + low_y * field("behind", r, layer)
    weight = up_y + low_y
    for face, towards in sides:
        flow = flow + face * field("p0", towards, layer)
        weight = weight + face
    if layer + 1 < layers:
        up_z = VERTICAL * reciprocal(here + load("half", r, layer + 1))
        store("face_z", r, layer, up_z)
        flow = flow + up_z * field("p0", r, layer + 1)
        weight = weight + up_z
    if layer > 0:
        low_z = load("face_z", r, layer - 1)
        flow = flow + low_z * field("p0", r, layer - 1)
        weight = weight + low_z
    return field("base", r, layer) + flow, field("storage", r, layer) + weight


def second_sweep(load, store, field, r, layers):
    for layer in range(layers):
        here = load("first", r, layer)
        up_y = load("face_y", r, layer)
        flow = (
            load("face_x", r - 1, layer) * load("first", r - 1, layer)
            + load("face_x", r, layer) * load("first", r + 1, layer)
            + up_y * ahead(here)
            + behind(up_y * here)
        )
        if layer + 1 < layers:
            flow = flow + load("face_z", r, layer) * load("first", r, layer + 1)
        if layer > 0:
            flow = flow + load("face_z", r, layer - 1) * load("first", r, layer - 1)
        store("last", r, layer, (field("base", r, layer) + flow) * load("inverse", r, layer))


def carried(face, low_press, up_press, low_frac, up_frac):
    velocity = face * (low_press - up_press)
    return velocity * jnp.where(velocity > 0, low_frac, up_frac)


def transported(load, field, first_row, last_row, layers):
    def side(r, layer):
        return carried(
            load("face_x", r, layer), load("last", r, layer), load("last", r + 1, layer),
            field("frac", r, layer), field("frac", r + 1, layer),
        )

    low_x = [side(first_row - 1, layer) for layer in range(layers)]
    for r in range(first_row, last_row + 1):
        low_z = None
        for layer in range(layers):
            here = load("last", r, layer)
            frac = field("frac", r, layer)
            up_x = side(r, layer)
            up_y = carried(
                load("face_y", r, layer), here, ahead(here), frac, field("frac_ahead", r, layer)
            )
            change = (low_x[layer] - up_x) + (behind(up_y) - up_y)
            low_x[layer] = up_x
            if low_z is not None:
                change = change + low_z
            if layer + 1 < layers:
                low_z = carried(
                    load("face_z", r, layer), here, load("last", r, layer + 1), frac,
                    field("frac", r, layer + 1),
                )
                change = change - low_z
            yield r, layer, field("sat", r, layer) + STEP_COEF * change


def put_places(dest_ref, cell_ref, cell_rows, depth):
    at = lax.broadcasted_iota(jnp.int32, (depth, cell_ref.shape[1]), 0)
    for i, row in enumerate(cell_rows):
        found = at + row * depth == cell_ref[...]
        dest_ref[i * depth : (i + 1) * depth, :] = found.astype(jnp.float32).astype(jnp.bfloat16)


def find(found, values_of, place):
    every = jnp.concatenate([pieces(values) for _, values in values_of], axis=0)
    sums = jnp.dot(every, place, preferred_element_type=jnp.float32)
    for i, (n, _) in enumerate(values_of):
        part = sums[i * 3 * GROUP : (i + 1) * 3 * GROUP]
        found[n] = part if found[n] is None else found[n] + part


def joined(part):
    return (part[:GROUP] + part[GROUP : 2 * GROUP]) + part[2 * GROUP :]


def put_fields(dest_ref, field_refs):
    fields = derived_fields(*(ref[...] for ref in field_refs))
    rows, depth = field_refs[0].shape
    for n, name in enumerate(FIELD_NAMES):
        for row in range(rows):
            dest_ref[n * rows + row] = jnp.broadcast_to(fields[name][row : row + 1, :], (8, depth))


def inner_kernel(dims, rank_ref, count_ref, perm_ref, *refs):
    layers, width = dims
    rows = layers * width
    kept, _ = state_slots(layers, width)
    field_refs, cell_ref, refs = refs[:4], refs[4], refs[5:]
    states, refs = dict(zip(kept, refs)), refs[len(kept) :]
    perf_ref, shared_ref, place_ref = refs[:3]
    work_refs = dict(zip(WORK, refs[3:]))
    depth = field_refs[0].shape[1]
    halves = depth // LANES

    @pl.when(pl.program_id(0) == 0)
    def _():
        put_fields(shared_ref, field_refs)
        put_places(place_ref, cell_ref, range(rows), depth)

    def field(name, r, layer):
        tile = shared_ref[FIELD_NAMES.index(name) * rows + layer * width + r]
        return jnp.concatenate([tile] * (GROUP // 8), axis=0)

    found = [None] * 3

    def load(kind, r, layer):
        return work_refs[kind][layer * width + r]

    def store(kind, r, layer, values_in):
        if kind in work_refs:
            work_refs[kind][layer * width + r] = values_in
        if (r, layer) in kept[kind]:
            states[kind][kept[kind][r, layer]] = values_in

    for layer in range(layers):
        lane_tiles = [
            members_down(perm_ref, layer, h, 0, GROUP, layers, halves) for h in range(halves)
        ]
        for r in range(width):
            values = jnp.concatenate([tiles[r] for tiles in lane_tiles], axis=1)
            half = 0.5 * jnp.exp(-values)
            store("half", r, layer, half)
    for r in range(width - 1):
        for layer in range(layers):
            store(
                "face_x", r, layer,
                reciprocal(load("half", r, layer) + load("half", r + 1, layer)),
            )
    for r in range(width):
        for layer in range(layers):
            sides = []
            if r > 0:
                sides.append((load("face_x", r - 1, layer), r - 1))
            if r < width - 1:
                sides.append((load("face_x", r, layer), r + 1))
            top, bottom = cell_faces(load, store, field, r, layer, layers, sides)
            if 0 < r < width - 1:
                bottom = reciprocal(bottom)
                top = top * bottom
            store("first", r, layer, top)
            store("inverse", r, layer, bottom)
    for r in range(2, width - 2):
        second_sweep(load, store, field, r, layers)
    for r, layer, saturation in transported(load, field, 3, width - 4, layers):
        store("sat", r, layer, saturation)
    for r in range(width):
        for layer in range(layers):
            values_of = [(0, load("half", r, layer))]
            if (r, layer) in kept["last"]:
                values_of.append((1, load("last", r, layer)))
            if (r, layer) in kept["sat"]:
                values_of.append((2, states["sat"][kept["sat"][r, layer]]))
            first = (layer * width + r) * depth
            find(found, values_of, place_ref[first : first + depth, :])
    for n in range(3):
        perf_ref[n] = joined(found[n])


def edge_kernel(dims, rank_ref, low_ref, high_ref, *refs):
    local_count, layers, width, tile_count = dims
    rows = layers * width
    depth = low_ref.shape[1]
    halves = depth // LANES
    group = pl.program_id(0)
    kept, added = state_slots(layers, width)
    field_refs, count_ref, cell_ref, well_ref, bhp_ref = refs[:4], refs[4], refs[5], refs[6], refs[7]
    refs = refs[8:]
    states, refs = dict(zip(kept, refs)), refs[len(kept) :]
    perf_ref, press_ref, moved_ref, rates_ref = refs[:4]
    added_ref, gathered_ref, shared_ref, place_ref = refs[4:]
    rim_rows = RIM * layers * local_count
    has_low = (rank_ref[0] > 0).astype(jnp.float32)
    has_high = (rank_ref[0] < tile_count - 1).astype(jnp.float32)
    rims = [
        derived_fields(
            *(
                ref[rim_rows + f * GROUP : rim_rows + (f + 1) * GROUP, :].astype(jnp.float32)
                for f in range(4)
            )
        )
        for ref in (low_ref, high_ref)
    ]
    slots, wells = cell_ref.shape[1], bhp_ref.shape[1]

    moved = [layer * width + r for layer in range(layers) for r in range(width)]
    moved = [row for row in moved if (row % width, row // width) not in kept["sat"]]

    @pl.when(group == 0)
    def _():
        put_fields(shared_ref, field_refs)
        put_places(place_ref, cell_ref, moved, depth)

    def field(name, r, layer):
        if 0 <= r < width:
            tile = shared_ref[FIELD_NAMES.index(name) * rows + layer * width + r]
            return jnp.concatenate([tile] * (GROUP // 8), axis=0)
        part, at = (rims[0], r + RIM) if r < 0 else (rims[1], r - width)
        at = layer * RIM + at
        return part[name][at : at + 1, :]

    found = [None] * 3

    def load(kind, r, layer):
        if (r, layer) in added.get(kind, {}):
            return added_ref[added[kind][r, layer]]
        return states[kind][kept[kind][r, layer]]

    def store(kind, r, layer, values_in):
        added_ref[added[kind][r, layer]] = values_in

    for r in list(range(-RIM, 0)) + list(range(width, width + RIM)):
        ref, i = (low_ref, r + RIM) if r < 0 else (high_ref, r - width)
        for layer in range(layers):
            at = (i * layers + layer) * local_count + group * GROUP
            values = ref[pl.ds(pl.multiple_of(at, GROUP), GROUP), :].astype(jnp.float32)
            store("half", r, layer, 0.5 * jnp.exp(-values))
    for r in (-3, -2, -1, width - 1, width, width + 1):
        for layer in range(layers):
            face = reciprocal(load("half", r, layer) + load("half", r + 1, layer))
            if r == -1:
                face = face * has_low
            if r == width - 1:
                face = face * has_high
            store("face_x", r, layer, face)
    for r in (-2, -1, width, width + 1):
        for layer in range(layers):
            sides = [
                (load("face_x", r - 1, layer), r - 1), (load("face_x", r, layer), r + 1)
            ]
            top, bottom = cell_faces(load, store, field, r, layer, layers, sides)
            bottom = reciprocal(bottom)
            store("first", r, layer, top * bottom)
            store("inverse", r, layer, bottom)
    for r, face_row, towards in ((0, -1, -1), (width - 1, width - 1, width)):
        for layer in range(layers):
            face = load("face_x", face_row, layer)
            top = states["first"][kept["first"][r, layer]]
            bottom = states["inverse"][kept["inverse"][r, layer]]
            bottom = reciprocal(bottom + face)
            store("first", r, layer, (top + face * field("p0", towards, layer)) * bottom)
            store("inverse", r, layer, bottom)
    for r in (-1, 0, 1, width - 2, width - 1, width):
        second_sweep(load, store, field, r, layers)

    for first_row, last_row in ((0, 2), (width - 3, width - 1)):
        for r, layer, saturation in transported(load, field, first_row, last_row, layers):
            moved_ref[layer * width + r] = saturation

    for layer in range(layers):
        for r in range(width):
            press_ref[layer * width + r] = load("last", r, layer)
            if (r, layer) in kept["sat"]:
                moved_ref[layer * width + r] = load("sat", r, layer)

    for i, row in enumerate(moved):
        r, layer = row % width, row // width
        values_of = [(2, moved_ref[row])]
        if (r, layer) in added["last"]:
            values_of.append((1, load("last", r, layer)))
        find(found, values_of, place_ref[i * depth : (i + 1) * depth, :])
    for n in range(3):
        total = perf_ref[n] if found[n] is None else perf_ref[n] + joined(found[n])
        gathered_ref[n, pl.ds(pl.multiple_of(group * GROUP, GROUP), GROUP), :] = total

    @pl.when(group == local_count // GROUP - 1)
    def _():
        chosen = (
            (lax.broadcasted_iota(jnp.int32, (wells, slots), 0) == well_ref[...])
            .astype(jnp.float32)
            .astype(jnp.bfloat16)
        )
        bhp = pieces(jnp.broadcast_to(bhp_ref[...], (GROUP, wells)))
        bhp = jnp.dot(bhp, chosen, preferred_element_type=jnp.float32)
        perf_bhp = (bhp[:1] + bhp[GROUP : GROUP + 1]) + bhp[2 * GROUP : 2 * GROUP + 1]
        live = (lax.broadcasted_iota(jnp.int32, (1, slots), 1) < count_ref[0]).astype(jnp.float32)
        mobility = water_frac(gathered_ref[2]) * reciprocal(2.0 * gathered_ref[0])
        terms = mobility * (gathered_ref[1] - perf_bhp) * live
        sums = lax.dot_general(
            pieces(terms), chosen, (((1,), (1,)), ((), ())), preferred_element_type=jnp.float32
        )
        partial_rates = (sums[:local_count] + sums[local_count : 2 * local_count]) + sums[
            2 * local_count :
        ]
        rates_ref[...] = jnp.broadcast_to(partial_rates[None], rates_ref.shape)


def output_kernel(layers, width, *refs):
    halves = refs[0].shape[2] // LANES
    for source_ref, out_ref in zip(refs[:2], refs[2:]):
        for layer in range(layers):
            for h in range(halves):
                rows_of_x = [
                    source_ref[layer * width + x, :, h * LANES : (h + 1) * LANES]
                    for x in range(width)
                ]
                for where_tile, tile in members_apart(rows_of_x, layer, h, layers, halves):
                    out_ref[where_tile, :] = tile


def invert_panel(columns):
    row = lax.broadcasted_iota(jnp.int32, columns[0].shape, 0)
    columns = list(columns)
    for k in range(PANEL):
        inverse = 1.0 / columns[k][k : k + 1]
        pivot = columns[k]
        for j in range(PANEL):
            if j != k:
                factor = columns[j][k : k + 1] * inverse
                columns[j] = jnp.where(row == k, factor, columns[j] - pivot * factor)
        columns[k] = jnp.where(row == k, inverse, -pivot * inverse)
    return columns


def solve_blocks(gram_matrix, cross_matrix):
    size = gram_matrix.shape[0]
    count = size // PANEL
    row = lax.broadcasted_iota(jnp.int32, gram_matrix.shape, 0)
    lane = lax.broadcasted_iota(jnp.int32, gram_matrix.shape, 1)
    full = gram_matrix + (row == lane).astype(jnp.float32)
    left = [full[i * PANEL : (i + 1) * PANEL] for i in range(count)]
    right = [cross_matrix[i * PANEL : (i + 1) * PANEL] for i in range(count)]
    width = cross_matrix.shape[1]
    for p in range(count):
        columns = [
            [
                jnp.broadcast_to(left[i][:, p * PANEL + j : p * PANEL + j + 1], (PANEL, size))
                for j in range(PANEL)
            ]
            for i in range(count)
        ]
        inverse = invert_panel(columns[p])
        new_left = sum(inverse[j] * left[p][j : j + 1] for j in range(PANEL))
        new_right = sum(inverse[j][:, :width] * right[p][j : j + 1] for j in range(PANEL))
        for i in range(count):
            if i != p:
                for j in range(PANEL):
                    if p + 1 < count:
                        left[i] = left[i] - columns[i][j] * new_left[j : j + 1]
                    right[i] = right[i] - columns[i][j][:, :width] * new_right[j : j + 1]
        left[p], right[p] = new_left, new_right
    return jnp.concatenate(right, axis=0)


def update_kernel(
    dims, rank_ref, rates_ref, own_ref, noise_ref, observed_ref, var_ref, anomaly_ref, perm_ref,
    out_ref, held_ref, anomaly_buf, perm_buf, sems,
):
    local_count, layers, width = dims
    rows = layers * width
    halves = anomaly_ref.shape[1] // LANES
    copies = [
        pltpu.make_async_copy(anomaly_ref, anomaly_buf, sems.at[0]),
        pltpu.make_async_copy(perm_ref, perm_buf, sems.at[1]),
    ]
    for copy in copies:
        copy.start()
    wells, share = own_ref.shape[1], held_ref.shape[1]
    held_ref[...] = pltpu.roll(
        own_ref[...], lax.rem(wells - rank_ref[0] * share, wells), 1
    )[:, :share]
    rates = rates_ref[...]
    members = rates.shape[0]
    spread = jnp.sqrt(INFLATION * var_ref[...])
    mean_rate = jnp.sum(rates, 0, keepdims=True) / members
    scaled = (rates - mean_rate) / (spread * (members - 1) ** 0.5)
    innovation = (observed_ref[...] - own_ref[...]) / spread + noise_ref[...]
    contract = (((1,), (1,)), ((), ()))
    gram_matrix, cross_matrix = (
        lax.dot_general(
            scaled, other, contract, precision=lax.Precision.HIGHEST,
            preferred_element_type=jnp.float32,
        )
        for other in (scaled, innovation)
    )
    weights = solve_blocks(gram_matrix, cross_matrix).T.astype(jnp.bfloat16)
    for copy in copies:
        copy.wait()
    for layer in range(layers):
        updates = []
        for x in range(width):
            at = (layer * width + x) * local_count
            every = jnp.concatenate(
                [
                    anomaly_buf[first + at : first + at + local_count, :]
                    for first in range(0, members * rows, rows * local_count)
                ],
                axis=0,
            )
            updates.append(jnp.dot(weights, every, preferred_element_type=jnp.float32))
        for h in range(halves):
            rows_of_x = [update[:, h * LANES : (h + 1) * LANES] for update in updates]
            for where_tile, tile in members_apart(rows_of_x, layer, h, layers, halves):
                out_ref[where_tile, :] = perm_buf[where_tile, :] + tile


def per_device(
    log_perm,
    start_pressure,
    start_sat,
    source,
    storage,
    well_press,
    perf_cell,
    perf_well,
    perf_count,
    observed,
    obs_var,
    obs_noise,
):
    local_count, layers, strip_width, strip_depth = log_perm.shape
    tile_count = lax.axis_size("tile")
    members = local_count * lax.axis_size("member")
    well_count = well_press.shape[0]
    well_share = well_count // tile_count
    tile_rank = lax.axis_index("tile")
    rows = layers * strip_width
    slots = perf_cell.shape[0]
    flat_perm = fold(log_perm)
    fields = [
        array.reshape(rows, strip_depth) for array in (start_pressure, start_sat, source, storage)
    ]
    in_hbm = pl.BlockSpec(memory_space=pltpu.HBM)
    rim_blocks = RIM * layers + 2
    field_scratch = pltpu.VMEM((4, GROUP, strip_depth), jnp.float32)
    params = pltpu.CompilerParams(vmem_limit_bytes=60 * 2**20)

    def whole(array):
        return pl.BlockSpec(array.shape, lambda g: (0,) * array.ndim)

    def stacked(count):
        return pl.BlockSpec((count, GROUP, strip_depth), lambda g: (0, g, 0))

    block = pl.BlockSpec((GROUP * rows * (strip_depth // LANES), LANES), lambda g: (g, 0))
    up_rows, down_rows, anomaly = (
        array.reshape(-1, strip_depth)
        for array in pl.pallas_call(
            functools.partial(pack_kernel, (layers, strip_width), (members - 1) ** -0.5),
            grid=(local_count // GROUP,),
            in_specs=[block] + [whole(array) for array in fields],
            out_specs=[stacked(rim_blocks), stacked(rim_blocks), stacked(rows)],
            out_shape=[
                jax.ShapeDtypeStruct((count, local_count, strip_depth), jnp.bfloat16)
                for count in (rim_blocks, rim_blocks, rows)
            ],
            scratch_shapes=[field_scratch, field_scratch],
            compiler_params=params,
            cost_estimate=pl.CostEstimate(
                flops=4 * flat_perm.size, bytes_accessed=8 * flat_perm.size, transcendentals=0
            ),
        )(flat_perm, *fields)
    )
    low_rows, high_rows = send_both(up_rows, down_rows, "tile")
    anomaly_all = lax.all_gather(anomaly, "member", axis=0, tiled=True)

    kept, added = state_slots(layers, strip_width)
    smem, vmem = pl.BlockSpec(memory_space=pltpu.SMEM), pl.BlockSpec(memory_space=pltpu.VMEM)

    def f32(*shape):
        return jax.ShapeDtypeStruct(shape, jnp.float32)

    state_specs = [stacked(count) for count in [*map(len, kept.values()), 3]]
    shared_scratch = pltpu.VMEM((len(FIELD_NAMES) * rows, 8, strip_depth), jnp.float32)
    place_scratch = pltpu.VMEM((rows * strip_depth, slots), jnp.bfloat16)
    cells, wells, press = perf_cell[None], perf_well[None], well_press[None]
    cost = pl.CostEstimate(flops=10**10, bytes_accessed=24 * flat_perm.size, transcendentals=0)
    state = pl.pallas_call(
        functools.partial(inner_kernel, (layers, strip_width)),
        grid=(local_count // GROUP,),
        in_specs=[smem, smem, block] + [whole(array) for array in fields] + [whole(cells)],
        out_specs=state_specs,
        out_shape=[
            f32(count, local_count, strip_depth) for count in map(len, kept.values())
        ]
        + [f32(3, local_count, slots)],
        scratch_shapes=[shared_scratch, place_scratch]
        + [pltpu.VMEM((rows, GROUP, strip_depth), jnp.float32)] * len(WORK),
        compiler_params=params,
        cost_estimate=cost,
    )(tile_rank[None], perf_count, flat_perm, *fields, cells)
    press_rows, sat_rows, partial_rates = pl.pallas_call(
        functools.partial(edge_kernel, (local_count, layers, strip_width, tile_count)),
        grid=(local_count // GROUP,),
        in_specs=[smem, whole(low_rows), whole(high_rows)]
        + [whole(array) for array in fields]
        + [smem, whole(cells), whole(wells), whole(press)]
        + state_specs,
        out_specs=[
            stacked(rows), stacked(rows),
            pl.BlockSpec((tile_count, local_count, well_count), lambda g: (0, 0, 0)),
        ],
        out_shape=[
            f32(rows, local_count, strip_depth), f32(rows, local_count, strip_depth),
            f32(tile_count, local_count, well_count),
        ],
        scratch_shapes=[
            pltpu.VMEM((sum(map(len, added.values())), GROUP, strip_depth), jnp.float32),
            pltpu.VMEM((3, local_count, slots), jnp.float32),
            shared_scratch,
            place_scratch,
        ],
        compiler_params=params,
        cost_estimate=cost,
    )(
        tile_rank[None], low_rows, high_rows, *fields, perf_count, cells, wells, press, *state
    )
    flat_press, flat_sat = pl.pallas_call(
        functools.partial(output_kernel, layers, strip_width),
        grid=(local_count // GROUP,),
        in_specs=[stacked(rows)] * 2,
        out_specs=[block] * 2,
        out_shape=[f32(*flat_perm.shape)] * 2,
        compiler_params=params,
        cost_estimate=pl.CostEstimate(
            flops=10**9, bytes_accessed=16 * flat_perm.size, transcendentals=0
        ),
    )(press_rows, sat_rows)
    own_rates = jnp.sum(lax.all_to_all(partial_rates, "tile", 0, 0), 0)
    rates_all = lax.all_gather(own_rates, "member", axis=0, tiled=True)
    new_flat, well_rates = pl.pallas_call(
        functools.partial(update_kernel, (local_count, layers, strip_width)),
        out_shape=(f32(*flat_perm.shape), f32(local_count, well_share)),
        in_specs=[smem] + [vmem] * 5 + [in_hbm] * 2,
        out_specs=(vmem, vmem),
        scratch_shapes=[
            pltpu.VMEM(anomaly_all.shape, jnp.bfloat16),
            pltpu.VMEM(flat_perm.shape, jnp.float32),
            pltpu.SemaphoreType.DMA((2,)),
        ],
        compiler_params=pltpu.CompilerParams(vmem_limit_bytes=60 * 2**20),
        cost_estimate=pl.CostEstimate(
            flops=12 * members**3, bytes_accessed=16 * flat_perm.size, transcendentals=0
        ),
    )(tile_rank[None], rates_all, own_rates, obs_noise, observed[None], obs_var[None], anomaly_all, flat_perm)
    new_log_perm = unfold(new_flat, log_perm.shape)
    pressure = unfold(flat_press, log_perm.shape)
    saturation = unfold(flat_sat, log_perm.shape)
    return (new_log_perm, pressure, saturation, well_rates)


def solution(mesh):
    return jax.shard_map(
        per_device,
        mesh=mesh,
        in_specs=(
            P("member", None, "tile", None),
            P(None, "tile", None),
            P(None, "tile", None),
            P(None, "tile", None),
            P(None, "tile", None),
            P(),
            P("tile"),
            P("tile"),
            P("tile"),
            P(),
            P(),
            P("member", None),
        ),
        out_specs=(
            P("member", None, "tile", None),
            P("member", None, "tile", None),
            P("member", None, "tile", None),
            P("member", "tile"),
        ),
        check_vma=False,
    )
```

```python
import functools

import jax
import jax.numpy as jnp
from jax import lax
from jax.experimental import pallas as pl
from jax.experimental.pallas import tpu as pltpu
from jax.sharding import PartitionSpec as P

SWEEPS = 2
RIM = SWEEPS + 1


VERTICAL = 0.5
VISCOSITY_RATIO = 2.0
STEP_COEF = 0.1
INFLATION = 4.0
PANEL = 8
GROUP = 16
LANES = 128


def fold(array):
    members, layers, width, depth = array.shape
    array = array.reshape(members, layers, width, depth // LANES, LANES)
    return array.transpose(0, 1, 3, 2, 4).reshape(-1, LANES)


def unfold(rows, shape):
    members, layers, width, depth = shape
    array = rows.reshape(members, layers, depth // LANES, width, LANES)
    return array.transpose(0, 1, 3, 2, 4).reshape(shape)


def turn(tiles):
    row = lax.broadcasted_iota(jnp.int32, tiles[0].shape, 0)
    for step in (4, 2, 1):
        stays = (row & step) == 0
        turned = list(tiles)
        for i in range(8):
            if i & step == 0:
                first, second = tiles[i], tiles[i + step]
                turned[i] = jnp.where(stays, first, pltpu.roll(second, step, 0))
                turned[i + step] = jnp.where(stays, pltpu.roll(first, 8 - step, 0), second)
        tiles = turned
    return tiles


def tile_rows(member, layer, half, layers, halves):
    return pl.ds(((member * layers + layer) * halves + half) * 8, 8)


def members_down(ref, layer, half, first, count, layers, halves):
    octets = [
        turn([ref[tile_rows(m + i, layer, half, layers, halves), :] for i in range(8)])
        for m in range(first, first + count, 8)
    ]
    return [jnp.concatenate([octet[x] for octet in octets], axis=0) for x in range(8)]


def members_apart(rows_of_x, layer, half, layers, halves):
    for m in range(0, rows_of_x[0].shape[0], 8):
        for i, tile in enumerate(turn([rows[m : m + 8] for rows in rows_of_x])):
            yield tile_rows(m + i, layer, half, layers, halves), tile


def send_both(up_rows, down_rows, axis):
    count = lax.axis_size(axis)
    forward = [(i, i + 1) for i in range(count - 1)]
    backward = [(target, source) for source, target in forward]
    return lax.ppermute(up_rows, axis, forward), lax.ppermute(down_rows, axis, backward)


def reciprocal(values_in):
    guess = pl.reciprocal(values_in, approx=True)
    return guess * (2.0 - values_in * guess)


def pieces(values_in):
    parts = []
    for _ in range(3):
        parts.append(values_in.astype(jnp.bfloat16))
        values_in = values_in - parts[-1].astype(jnp.float32)
    return jnp.concatenate(parts, axis=0)


def water_frac(values_in):
    squared = values_in * values_in
    rest = 1.0 - values_in
    return squared * reciprocal(squared + VISCOSITY_RATIO * rest * rest)


def pack_kernel(
    dims, scale, perm_ref, p0_ref, sat_ref, source_ref, storage_ref, up_ref, down_ref, anomaly_ref,
    up_rows, down_rows,
):
    layers, width = dims
    halves = anomaly_ref.shape[2] // LANES
    block = RIM * layers

    @pl.when(pl.program_id(0) == 0)
    def _():
        up_rows[...] = jnp.zeros_like(up_rows)
        down_rows[...] = jnp.zeros_like(down_rows)
        for f, fields_ref in enumerate((p0_ref, sat_ref, source_ref, storage_ref)):
            for layer in range(layers):
                at = layer * RIM
                first = layer * width
                down_rows[f, at : at + RIM, :] = fields_ref[first : first + RIM, :]
                up_rows[f, at : at + RIM, :] = fields_ref[first + width - RIM : first + width, :]

    for i in range(2):
        f = 2 * i + pl.program_id(0)
        up_ref[block + i] = up_rows[f].astype(jnp.bfloat16)
        down_ref[block + i] = down_rows[f].astype(jnp.bfloat16)
    for layer in range(layers):
        for half in range(halves):
            lanes = slice(half * LANES, (half + 1) * LANES)
            values_of_x = members_down(perm_ref, layer, half, 0, GROUP, layers, halves)
            for x, values in enumerate(values_of_x):
                anomaly_ref[layer * width + x, :, lanes] = (values * scale).astype(jnp.bfloat16)
                low_values = values.astype(jnp.bfloat16)
                if x < RIM:
                    down_ref[x * layers + layer, :, lanes] = low_values
                if x >= width - RIM:
                    up_ref[(x - width + RIM) * layers + layer, :, lanes] = low_values


WORK = ("half", "face_x", "face_y", "face_z", "inverse", "first", "last")
EDGE_NAMES = ("p0", "base", "sat", "frac", "frac_ahead")
FIELD_NAMES = ("p0", "sat", "storage", "base", "ahead", "behind", "frac", "frac_ahead")


def state_slots(layers, width):
    kept, added = {}, {}
    rim = list(range(-RIM, 0)) + list(range(width, width + RIM))
    near = [-2, -1, width, width + 1]

    def place(where, kind, rows, count=layers):
        where[kind] = {}
        for r in rows:
            for layer in range(count):
                where[kind][r, layer] = len(where[kind])

    place(kept, "half", (0, width - 1))
    place(kept, "face_x", [0, 1, 2, width - 4, width - 3, width - 2])
    outer = [0, 1, 2, width - 3, width - 2, width - 1]
    place(kept, "face_y", outer)
    place(kept, "face_z", outer, layers - 1)
    place(kept, "inverse", [0, 1, width - 2, width - 1])
    place(kept, "first", outer)
    place(kept, "last", range(2, width - 2))
    place(kept, "sat", range(3, width - 3))
    place(added, "half", rim)
    place(added, "face_x", [-3, -2, -1, width - 1, width, width + 1])
    place(added, "face_y", near)
    place(added, "face_z", near, layers - 1)
    place(added, "inverse", near + [0, width - 1])
    place(added, "first", near + [0, width - 1])
    place(added, "last", [-1, 0, 1, width - 2, width - 1, width])
    first = 0
    for places in added.values():
        for key in places:
            places[key], first = first, first + 1
    return kept, added


def ahead(values_in):
    return pltpu.roll(values_in, values_in.shape[1] - 1, 1)


def behind(values_in):
    return pltpu.roll(values_in, 1, 1)


def derived_fields(p0, sat, source, storage):
    frac = water_frac(sat)
    return dict(
        p0=p0, sat=sat, storage=storage, base=source + storage * p0,
        ahead=ahead(p0), behind=behind(p0), frac=frac, frac_ahead=ahead(frac),
    )


def cell_faces(load, store, field, r, layer, layers, sides):
    here = load("half", r, layer)
    lane = lax.broadcasted_iota(jnp.int32, here.shape, 1)
    up_y = jnp.where(lane < here.shape[1] - 1, reciprocal(here + ahead(here)), 0.0)
    low_y = behind(up_y)
    store("face_y", r, layer, up_y)
    flow = up_y * field("ahead", r, layer) + low_y * field("behind", r, layer)
    weight = up_y + low_y
    for face, towards in sides:
        flow = flow + face * field("p0", towards, layer)
        weight = weight + face
    if layer + 1 < layers:
        up_z = VERTICAL * reciprocal(here + load("half", r, layer + 1))
        store("face_z", r, layer, up_z)
        flow = flow + up_z * field("p0", r, layer + 1)
        weight = weight + up_z
    if layer > 0:
        low_z = load("face_z", r, layer - 1)
        flow = flow + low_z * field("p0", r, layer - 1)
        weight = weight + low_z
    return field("base", r, layer) + flow, field("storage", r, layer) + weight


def second_sweep(load, store, field, r, layers):
    for layer in range(layers):
        here = load("first", r, layer)
        up_y = load("face_y", r, layer)
        flow = (
            load("face_x", r - 1, layer) * load("first", r - 1, layer)
            + load("face_x", r, layer) * load("first", r + 1, layer)
            + up_y * ahead(here)
            + behind(up_y * here)
        )
        if layer + 1 < layers:
            flow = flow + load("face_z", r, layer) * load("first", r, layer + 1)
        if layer > 0:
            flow = flow + load("face_z", r, layer - 1) * load("first", r, layer - 1)
        store("last", r, layer, (field("base", r, layer) + flow) * load("inverse", r, layer))


def carried(face, low_press, up_press, low_frac, up_frac):
    velocity = face * (low_press - up_press)
    return velocity * jnp.where(velocity > 0, low_frac, up_frac)


def transported(load, field, first_row, last_row, layers):
    def side(r, layer):
        return carried(
            load("face_x", r, layer), load("last", r, layer), load("last", r + 1, layer),
            field("frac", r, layer), field("frac", r + 1, layer),
        )

    low_x = [side(first_row - 1, layer) for layer in range(layers)]
    for r in range(first_row, last_row + 1):
        low_z = None
        for layer in range(layers):
            here = load("last", r, layer)
            frac = field("frac", r, layer)
            up_x = side(r, layer)
            up_y = carried(
                load("face_y", r, layer), here, ahead(here), frac, field("frac_ahead", r, layer)
            )
            change = (low_x[layer] - up_x) + (behind(up_y) - up_y)
            low_x[layer] = up_x
            if low_z is not None:
                change = change + low_z
            if layer + 1 < layers:
                low_z = carried(
                    load("face_z", r, layer), here, load("last", r, layer + 1), frac,
                    field("frac", r, layer + 1),
                )
                change = change - low_z
            yield r, layer, field("sat", r, layer) + STEP_COEF * change


def put_places(dest_ref, cell_ref, cell_rows, depth):
    at = lax.broadcasted_iota(jnp.int32, (depth, cell_ref.shape[1]), 0)
    for i, row in enumerate(cell_rows):
        found = at + row * depth == cell_ref[...]
        dest_ref[i * depth : (i + 1) * depth, :] = found.astype(jnp.float32).astype(jnp.bfloat16)


def find(found, values_of, place):
    every = jnp.concatenate([pieces(values) for _, values in values_of], axis=0)
    sums = jnp.dot(every, place, preferred_element_type=jnp.float32)
    for i, (n, _) in enumerate(values_of):
        part = sums[i * 3 * GROUP : (i + 1) * 3 * GROUP]
        found[n] = part if found[n] is None else found[n] + part


def joined(part):
    return (part[:GROUP] + part[GROUP : 2 * GROUP]) + part[2 * GROUP :]


def put_fields(dest_ref, field_refs, names):
    fields = derived_fields(*(ref[...] for ref in field_refs))
    rows, depth = field_refs[0].shape
    for n, name in enumerate(names):
        for row in range(rows):
            dest_ref[n * rows + row] = jnp.broadcast_to(fields[name][row : row + 1, :], (8, depth))


def inner_kernel(dims, rank_ref, count_ref, perm_ref, *refs):
    layers, width = dims
    rows = layers * width
    kept, _ = state_slots(layers, width)
    field_refs, cell_ref, refs = refs[:4], refs[4], refs[5:]
    states, refs = dict(zip(kept, refs)), refs[len(kept) :]
    perf_ref, shared_ref, place_ref = refs[:3]
    work_refs = dict(zip(WORK, refs[3:]))
    depth = field_refs[0].shape[1]
    halves = depth // LANES

    @pl.when(pl.program_id(0) == 0)
    def _():
        put_fields(shared_ref, field_refs, FIELD_NAMES)
        put_places(place_ref, cell_ref, range(rows), depth)

    def field(name, r, layer):
        tile = shared_ref[FIELD_NAMES.index(name) * rows + layer * width + r]
        return jnp.concatenate([tile] * (GROUP // 8), axis=0)

    found = [None] * 3

    def load(kind, r, layer):
        return work_refs[kind][layer * width + r]

    def store(kind, r, layer, values_in):
        if kind in work_refs:
            work_refs[kind][layer * width + r] = values_in
        if (r, layer) in kept[kind]:
            states[kind][kept[kind][r, layer]] = values_in

    for layer in range(layers):
        lane_tiles = [
            members_down(perm_ref, layer, h, 0, GROUP, layers, halves) for h in range(halves)
        ]
        for r in range(width):
            values = jnp.concatenate([tiles[r] for tiles in lane_tiles], axis=1)
            half = 0.5 * jnp.exp(-values)
            store("half", r, layer, half)
    for r in range(width - 1):
        for layer in range(layers):
            store(
                "face_x", r, layer,
                reciprocal(load("half", r, layer) + load("half", r + 1, layer)),
            )
    for r in range(width):
        for layer in range(layers):
            sides = []
            if r > 0:
                sides.append((load("face_x", r - 1, layer), r - 1))
            if r < width - 1:
                sides.append((load("face_x", r, layer), r + 1))
            top, bottom = cell_faces(load, store, field, r, layer, layers, sides)
            if 0 < r < width - 1:
                bottom = reciprocal(bottom)
                top = top * bottom
            store("first", r, layer, top)
            store("inverse", r, layer, bottom)
    for r in range(2, width - 2):
        second_sweep(load, store, field, r, layers)
    for r, layer, saturation in transported(load, field, 3, width - 4, layers):
        store("sat", r, layer, saturation)
    for r in range(width):
        for layer in range(layers):
            values_of = [(0, load("half", r, layer))]
            if (r, layer) in kept["last"]:
                values_of.append((1, load("last", r, layer)))
            if (r, layer) in kept["sat"]:
                values_of.append((2, states["sat"][kept["sat"][r, layer]]))
            first = (layer * width + r) * depth
            find(found, values_of, place_ref[first : first + depth, :])
    for n in range(3):
        perf_ref[n] = joined(found[n])


def edge_kernel(dims, rank_ref, low_ref, high_ref, *refs):
    local_count, layers, width, tile_count = dims
    rows = layers * width
    depth = low_ref.shape[1]
    halves = depth // LANES
    group = pl.program_id(0)
    kept, added = state_slots(layers, width)
    field_refs, count_ref, cell_ref, well_ref, bhp_ref = refs[:4], refs[4], refs[5], refs[6], refs[7]
    refs = refs[8:]
    states, refs = dict(zip(kept, refs)), refs[len(kept) :]
    perf_ref, press_ref, moved_ref, rates_ref = refs[:4]
    added_ref, gathered_ref, shared_ref, place_ref = refs[4:]
    rim_rows = RIM * layers * local_count
    has_low = (rank_ref[0] > 0).astype(jnp.float32)
    has_high = (rank_ref[0] < tile_count - 1).astype(jnp.float32)
    rims = [
        derived_fields(
            *(
                ref[rim_rows + f * GROUP : rim_rows + (f + 1) * GROUP, :].astype(jnp.float32)
                for f in range(4)
            )
        )
        for ref in (low_ref, high_ref)
    ]
    slots, wells = cell_ref.shape[1], bhp_ref.shape[1]

    moved = [layer * width + r for layer in range(layers) for r in range(width)]
    moved = [row for row in moved if (row % width, row // width) not in kept["sat"]]

    @pl.when(group == 0)
    def _():
        put_fields(shared_ref, field_refs, EDGE_NAMES)
        put_places(place_ref, cell_ref, moved, depth)

    def field(name, r, layer):
        if 0 <= r < width:
            tile = shared_ref[EDGE_NAMES.index(name) * rows + layer * width + r]
            return jnp.concatenate([tile] * (GROUP // 8), axis=0)
        part, at = (rims[0], r + RIM) if r < 0 else (rims[1], r - width)
        at = layer * RIM + at
        return part[name][at : at + 1, :]

    found = [None] * 3

    def load(kind, r, layer):
        if (r, layer) in added.get(kind, {}):
            return added_ref[added[kind][r, layer]]
        return states[kind][kept[kind][r, layer]]

    def store(kind, r, layer, values_in):
        added_ref[added[kind][r, layer]] = values_in

    for r in list(range(-RIM, 0)) + list(range(width, width + RIM)):
        ref, i = (low_ref, r + RIM) if r < 0 else (high_ref, r - width)
        for layer in range(layers):
            at = (i * layers + layer) * local_count + group * GROUP
            values = ref[pl.ds(pl.multiple_of(at, GROUP), GROUP), :].astype(jnp.float32)
            store("half", r, layer, 0.5 * jnp.exp(-values))
    for r in (-3, -2, -1, width - 1, width, width + 1):
        for layer in range(layers):
            face = reciprocal(load("half", r, layer) + load("half", r + 1, layer))
            if r == -1:
                face = face * has_low
            if r == width - 1:
                face = face * has_high
            store("face_x", r, layer, face)
    for r in (-2, -1, width, width + 1):
        for layer in range(layers):
            sides = [
                (load("face_x", r - 1, layer), r - 1), (load("face_x", r, layer), r + 1)
            ]
            top, bottom = cell_faces(load, store, field, r, layer, layers, sides)
            bottom = reciprocal(bottom)
            store("first", r, layer, top * bottom)
            store("inverse", r, layer, bottom)
    for r, face_row, towards in ((0, -1, -1), (width - 1, width - 1, width)):
        for layer in range(layers):
            face = load("face_x", face_row, layer)
            top = states["first"][kept["first"][r, layer]]
            bottom = states["inverse"][kept["inverse"][r, layer]]
            bottom = reciprocal(bottom + face)
            store("first", r, layer, (top + face * field("p0", towards, layer)) * bottom)
            store("inverse", r, layer, bottom)
    for r in (-1, 0, 1, width - 2, width - 1, width):
        second_sweep(load, store, field, r, layers)

    for first_row, last_row in ((0, 2), (width - 3, width - 1)):
        for r, layer, saturation in transported(load, field, first_row, last_row, layers):
            moved_ref[layer * width + r] = saturation

    for layer in range(layers):
        for r in range(width):
            press_ref[layer * width + r] = load("last", r, layer)
            if (r, layer) in kept["sat"]:
                moved_ref[layer * width + r] = load("sat", r, layer)

    for i, row in enumerate(moved):
        r, layer = row % width, row // width
        values_of = [(2, moved_ref[row])]
        if (r, layer) in added["last"]:
            values_of.append((1, load("last", r, layer)))
        find(found, values_of, place_ref[i * depth : (i + 1) * depth, :])
    for n in range(3):
        total = perf_ref[n] if found[n] is None else perf_ref[n] + joined(found[n])
        gathered_ref[n, pl.ds(pl.multiple_of(group * GROUP, GROUP), GROUP), :] = total

    @pl.when(group == local_count // GROUP - 1)
    def _():
        chosen = (
            (lax.broadcasted_iota(jnp.int32, (wells, slots), 0) == well_ref[...])
            .astype(jnp.float32)
            .astype(jnp.bfloat16)
        )
        bhp = pieces(jnp.broadcast_to(bhp_ref[...], (GROUP, wells)))
        bhp = jnp.dot(bhp, chosen, preferred_element_type=jnp.float32)
        perf_bhp = (bhp[:1] + bhp[GROUP : GROUP + 1]) + bhp[2 * GROUP : 2 * GROUP + 1]
        live = (lax.broadcasted_iota(jnp.int32, (1, slots), 1) < count_ref[0]).astype(jnp.float32)
        mobility = water_frac(gathered_ref[2]) * reciprocal(2.0 * gathered_ref[0])
        terms = mobility * (gathered_ref[1] - perf_bhp) * live
        sums = lax.dot_general(
            pieces(terms), chosen, (((1,), (1,)), ((), ())), preferred_element_type=jnp.float32
        )
        partial_rates = (sums[:local_count] + sums[local_count : 2 * local_count]) + sums[
            2 * local_count :
        ]
        rates_ref[...] = jnp.broadcast_to(partial_rates[None], rates_ref.shape)


def output_kernel(layers, width, *refs):
    halves = refs[0].shape[2] // LANES
    for source_ref, out_ref in zip(refs[:2], refs[2:]):
        for layer in range(layers):
            for h in range(halves):
                rows_of_x = [
                    source_ref[layer * width + x, :, h * LANES : (h + 1) * LANES]
                    for x in range(width)
                ]
                for where_tile, tile in members_apart(rows_of_x, layer, h, layers, halves):
                    out_ref[where_tile, :] = tile


def invert_panel(columns):
    row = lax.broadcasted_iota(jnp.int32, columns[0].shape, 0)
    columns = list(columns)
    for k in range(PANEL):
        inverse = 1.0 / columns[k][k : k + 1]
        pivot = columns[k]
        for j in range(PANEL):
            if j != k:
                factor = columns[j][k : k + 1] * inverse
                columns[j] = jnp.where(row == k, factor, columns[j] - pivot * factor)
        columns[k] = jnp.where(row == k, inverse, -pivot * inverse)
    return columns


def solve_blocks(gram_matrix, cross_matrix):
    size = gram_matrix.shape[0]
    count = size // PANEL
    row = lax.broadcasted_iota(jnp.int32, gram_matrix.shape, 0)
    lane = lax.broadcasted_iota(jnp.int32, gram_matrix.shape, 1)
    full = gram_matrix + (row == lane).astype(jnp.float32)
    left = [full[i * PANEL : (i + 1) * PANEL] for i in range(count)]
    right = [cross_matrix[i * PANEL : (i + 1) * PANEL] for i in range(count)]
    width = cross_matrix.shape[1]
    for p in range(count):
        columns = [
            [
                jnp.broadcast_to(left[i][:, p * PANEL + j : p * PANEL + j + 1], (PANEL, size))
                for j in range(PANEL)
            ]
            for i in range(count)
        ]
        inverse = invert_panel(columns[p])
        new_left = sum(inverse[j] * left[p][j : j + 1] for j in range(PANEL))
        new_right = sum(inverse[j][:, :width] * right[p][j : j + 1] for j in range(PANEL))
        for i in range(count):
            if i != p:
                for j in range(PANEL):
                    if p + 1 < count:
                        left[i] = left[i] - columns[i][j] * new_left[j : j + 1]
                    right[i] = right[i] - columns[i][j][:, :width] * new_right[j : j + 1]
        left[p], right[p] = new_left, new_right
    return jnp.concatenate(right, axis=0)


def update_kernel(
    dims, rank_ref, rates_ref, own_ref, noise_ref, observed_ref, var_ref, anomaly_ref, perm_ref,
    out_ref, held_ref, anomaly_buf, perm_buf, out_buf, sems,
):
    local_count, layers, width = dims
    rows = layers * width
    halves = anomaly_ref.shape[1] // LANES
    copies = [
        pltpu.make_async_copy(anomaly_ref, anomaly_buf, sems.at[0]),
        pltpu.make_async_copy(perm_ref, perm_buf, sems.at[1]),
    ]
    for copy in copies:
        copy.start()
    wells, share = own_ref.shape[1], held_ref.shape[1]
    held_ref[...] = pltpu.roll(
        own_ref[...], lax.rem(wells - rank_ref[0] * share, wells), 1
    )[:, :share]
    rates = rates_ref[...]
    members = rates.shape[0]
    spread = jnp.sqrt(INFLATION * var_ref[...])
    mean_rate = jnp.sum(rates, 0, keepdims=True) / members
    scaled = (rates - mean_rate) / (spread * (members - 1) ** 0.5)
    innovation = (observed_ref[...] - own_ref[...]) / spread + noise_ref[...]
    contract = (((1,), (1,)), ((), ()))
    gram_matrix, cross_matrix = (
        lax.dot_general(
            scaled, other, contract, precision=lax.Precision.HIGHEST,
            preferred_element_type=jnp.float32,
        )
        for other in (scaled, innovation)
    )
    weights = solve_blocks(gram_matrix, cross_matrix).T.astype(jnp.bfloat16)
    for copy in copies:
        copy.wait()
    sent = []
    for layer in range(layers):
        updates = []
        for x in range(width):
            at = (layer * width + x) * local_count
            every = jnp.concatenate(
                [
                    anomaly_buf[first + at : first + at + local_count, :]
                    for first in range(0, members * rows, rows * local_count)
                ],
                axis=0,
            )
            updates.append(jnp.dot(weights, every, preferred_element_type=jnp.float32))
        for h in range(halves):
            rows_of_x = [update[:, h * LANES : (h + 1) * LANES] for update in updates]
            tiles = members_apart(rows_of_x, layer, h, layers, halves)
            for m, (where_tile, tile) in enumerate(tiles):
                out_buf[m, layer, h * 8 : (h + 1) * 8, :] = perm_buf[where_tile, :] + tile
        sent.append(
            pltpu.make_async_copy(
                out_buf.at[:, layer], out_ref.at[:, layer], sems.at[2 + layer]
            )
        )
        sent[-1].start()
    for copy in sent:
        copy.wait()


def per_device(
    log_perm,
    start_pressure,
    start_sat,
    source,
    storage,
    well_press,
    perf_cell,
    perf_well,
    perf_count,
    observed,
    obs_var,
    obs_noise,
):
    local_count, layers, strip_width, strip_depth = log_perm.shape
    tile_count = lax.axis_size("tile")
    members = local_count * lax.axis_size("member")
    well_count = well_press.shape[0]
    well_share = well_count // tile_count
    tile_rank = lax.axis_index("tile")
    rows = layers * strip_width
    slots = perf_cell.shape[0]
    flat_perm = fold(log_perm)
    fields = [
        array.reshape(rows, strip_depth) for array in (start_pressure, start_sat, source, storage)
    ]
    in_hbm = pl.BlockSpec(memory_space=pltpu.HBM)
    rim_blocks = RIM * layers + 2
    field_scratch = pltpu.VMEM((4, GROUP, strip_depth), jnp.float32)
    params = pltpu.CompilerParams(vmem_limit_bytes=60 * 2**20)

    def whole(array):
        return pl.BlockSpec(array.shape, lambda g: (0,) * array.ndim)

    def stacked(count):
        return pl.BlockSpec((count, GROUP, strip_depth), lambda g: (0, g, 0))

    block = pl.BlockSpec((GROUP * rows * (strip_depth // LANES), LANES), lambda g: (g, 0))
    up_rows, down_rows, anomaly = (
        array.reshape(-1, strip_depth)
        for array in pl.pallas_call(
            functools.partial(pack_kernel, (layers, strip_width), (members - 1) ** -0.5),
            grid=(local_count // GROUP,),
            in_specs=[block] + [whole(array) for array in fields],
            out_specs=[stacked(rim_blocks), stacked(rim_blocks), stacked(rows)],
            out_shape=[
                jax.ShapeDtypeStruct((count, local_count, strip_depth), jnp.bfloat16)
                for count in (rim_blocks, rim_blocks, rows)
            ],
            scratch_shapes=[field_scratch, field_scratch],
            compiler_params=params,
            cost_estimate=pl.CostEstimate(
                flops=4 * flat_perm.size, bytes_accessed=8 * flat_perm.size, transcendentals=0
            ),
        )(flat_perm, *fields)
    )
    low_rows, high_rows = send_both(up_rows, down_rows, "tile")
    anomaly_all = lax.all_gather(anomaly, "member", axis=0, tiled=True)

    kept, added = state_slots(layers, strip_width)
    smem, vmem = pl.BlockSpec(memory_space=pltpu.SMEM), pl.BlockSpec(memory_space=pltpu.VMEM)

    def f32(*shape):
        return jax.ShapeDtypeStruct(shape, jnp.float32)

    state_specs = [stacked(count) for count in [*map(len, kept.values()), 3]]
    shared_scratch = pltpu.VMEM((len(FIELD_NAMES) * rows, 8, strip_depth), jnp.float32)
    place_scratch = pltpu.VMEM((rows * strip_depth, slots), jnp.bfloat16)
    cells, wells, press = perf_cell[None], perf_well[None], well_press[None]
    cost = pl.CostEstimate(flops=10**10, bytes_accessed=24 * flat_perm.size, transcendentals=0)
    state = pl.pallas_call(
        functools.partial(inner_kernel, (layers, strip_width)),
        grid=(local_count // GROUP,),
        in_specs=[smem, smem, block] + [whole(array) for array in fields] + [whole(cells)],
        out_specs=state_specs,
        out_shape=[
            f32(count, local_count, strip_depth) for count in map(len, kept.values())
        ]
        + [f32(3, local_count, slots)],
        scratch_shapes=[shared_scratch, place_scratch]
        + [pltpu.VMEM((rows, GROUP, strip_depth), jnp.float32)] * len(WORK),
        compiler_params=params,
        cost_estimate=cost,
    )(tile_rank[None], perf_count, flat_perm, *fields, cells)
    press_rows, sat_rows, partial_rates = pl.pallas_call(
        functools.partial(edge_kernel, (local_count, layers, strip_width, tile_count)),
        grid=(local_count // GROUP,),
        in_specs=[smem, whole(low_rows), whole(high_rows)]
        + [whole(array) for array in fields]
        + [smem, whole(cells), whole(wells), whole(press)]
        + state_specs,
        out_specs=[
            stacked(rows), stacked(rows),
            pl.BlockSpec((tile_count, local_count, well_count), lambda g: (0, 0, 0)),
        ],
        out_shape=[
            f32(rows, local_count, strip_depth), f32(rows, local_count, strip_depth),
            f32(tile_count, local_count, well_count),
        ],
        scratch_shapes=[
            pltpu.VMEM((sum(map(len, added.values())), GROUP, strip_depth), jnp.float32),
            pltpu.VMEM((3, local_count, slots), jnp.float32),
            shared_scratch,
            place_scratch,
        ],
        compiler_params=params,
        cost_estimate=cost,
    )(
        tile_rank[None], low_rows, high_rows, *fields, perf_count, cells, wells, press, *state
    )
    flat_press, flat_sat = pl.pallas_call(
        functools.partial(output_kernel, layers, strip_width),
        grid=(local_count // GROUP,),
        in_specs=[stacked(rows)] * 2,
        out_specs=[block] * 2,
        out_shape=[f32(*flat_perm.shape)] * 2,
        compiler_params=params,
        cost_estimate=pl.CostEstimate(
            flops=10**9, bytes_accessed=16 * flat_perm.size, transcendentals=0
        ),
    )(press_rows, sat_rows)
    own_rates = jnp.sum(lax.all_to_all(partial_rates, "tile", 0, 0), 0)
    rates_all = lax.all_gather(own_rates, "member", axis=0, tiled=True)
    out_dims = (local_count, layers, rows * (strip_depth // LANES) // layers, LANES)
    new_flat, well_rates = pl.pallas_call(
        functools.partial(update_kernel, (local_count, layers, strip_width)),
        out_shape=(f32(*out_dims), f32(local_count, well_share)),
        in_specs=[smem] + [vmem] * 5 + [in_hbm] * 2,
        out_specs=(in_hbm, vmem),
        scratch_shapes=[
            pltpu.VMEM(anomaly_all.shape, jnp.bfloat16),
            pltpu.VMEM(flat_perm.shape, jnp.float32),
            pltpu.VMEM(out_dims, jnp.float32),
            pltpu.SemaphoreType.DMA((2 + layers,)),
        ],
        compiler_params=pltpu.CompilerParams(vmem_limit_bytes=60 * 2**20),
        cost_estimate=pl.CostEstimate(
            flops=12 * members**3, bytes_accessed=16 * flat_perm.size, transcendentals=0
        ),
    )(tile_rank[None], rates_all, own_rates, obs_noise, observed[None], obs_var[None], anomaly_all, flat_perm)
    new_log_perm = unfold(new_flat, log_perm.shape)
    pressure = unfold(flat_press, log_perm.shape)
    saturation = unfold(flat_sat, log_perm.shape)
    return (new_log_perm, pressure, saturation, well_rates)


def solution(mesh):
    return jax.shard_map(
        per_device,
        mesh=mesh,
        in_specs=(
            P("member", None, "tile", None),
            P(None, "tile", None),
            P(None, "tile", None),
            P(None, "tile", None),
            P(None, "tile", None),
            P(),
            P("tile"),
            P("tile"),
            P("tile"),
            P(),
            P(),
            P("member", None),
        ),
        out_specs=(
            P("member", None, "tile", None),
            P("member", None, "tile", None),
            P("member", None, "tile", None),
            P("member", "tile"),
        ),
        check_vma=False,
    )
```

```python
import functools

import jax
import jax.numpy as jnp
from jax import lax
from jax.experimental import pallas as pl
from jax.experimental.pallas import tpu as pltpu
from jax.sharding import PartitionSpec as P

SWEEPS = 2
RIM = SWEEPS + 1


VERTICAL = 0.5
VISCOSITY_RATIO = 2.0
STEP_COEF = 0.1
INFLATION = 4.0
PANEL = 8
GROUP = 16
LANES = 128


def fold(array):
    members, layers, width, depth = array.shape
    array = array.reshape(members, layers, width, depth // LANES, LANES)
    return array.transpose(0, 1, 3, 2, 4).reshape(-1, LANES)


def unfold(rows, shape):
    members, layers, width, depth = shape
    array = rows.reshape(members, layers, depth // LANES, width, LANES)
    return array.transpose(0, 1, 3, 2, 4).reshape(shape)


def turn(tiles):
    row = lax.broadcasted_iota(jnp.int32, tiles[0].shape, 0)
    for step in (4, 2, 1):
        stays = (row & step) == 0
        turned = list(tiles)
        for i in range(8):
            if i & step == 0:
                first, second = tiles[i], tiles[i + step]
                turned[i] = jnp.where(stays, first, pltpu.roll(second, step, 0))
                turned[i + step] = jnp.where(stays, pltpu.roll(first, 8 - step, 0), second)
        tiles = turned
    return tiles


def tile_rows(member, layer, half, layers, halves):
    return pl.ds(((member * layers + layer) * halves + half) * 8, 8)


def members_down(ref, layer, half, first, count, layers, halves):
    octets = [
        turn([ref[tile_rows(m + i, layer, half, layers, halves), :] for i in range(8)])
        for m in range(first, first + count, 8)
    ]
    return [jnp.concatenate([octet[x] for octet in octets], axis=0) for x in range(8)]


def members_apart(rows_of_x, layer, half, layers, halves):
    for m in range(0, rows_of_x[0].shape[0], 8):
        for i, tile in enumerate(turn([rows[m : m + 8] for rows in rows_of_x])):
            yield tile_rows(m + i, layer, half, layers, halves), tile


def send_both(up_rows, down_rows, axis):
    count = lax.axis_size(axis)
    forward = [(i, i + 1) for i in range(count - 1)]
    backward = [(target, source) for source, target in forward]
    return lax.ppermute(up_rows, axis, forward), lax.ppermute(down_rows, axis, backward)


def reciprocal(values_in):
    guess = pl.reciprocal(values_in, approx=True)
    return guess * (2.0 - values_in * guess)


def pieces(values_in):
    parts = []
    for _ in range(3):
        parts.append(values_in.astype(jnp.bfloat16))
        values_in = values_in - parts[-1].astype(jnp.float32)
    return jnp.concatenate(parts, axis=0)


def water_frac(values_in):
    squared = values_in * values_in
    rest = 1.0 - values_in
    return squared * reciprocal(squared + VISCOSITY_RATIO * rest * rest)


def pack_kernel(
    dims, scale, perm_ref, p0_ref, sat_ref, source_ref, storage_ref, up_ref, down_ref, anomaly_ref,
    up_rows, down_rows,
):
    layers, width = dims
    halves = anomaly_ref.shape[2] // LANES
    block = RIM * layers

    @pl.when(pl.program_id(0) == 0)
    def _():
        up_rows[...] = jnp.zeros_like(up_rows)
        down_rows[...] = jnp.zeros_like(down_rows)
        for f, fields_ref in enumerate((p0_ref, sat_ref, source_ref, storage_ref)):
            for layer in range(layers):
                at = layer * RIM
                first = layer * width
                down_rows[f, at : at + RIM, :] = fields_ref[first : first + RIM, :]
                up_rows[f, at : at + RIM, :] = fields_ref[first + width - RIM : first + width, :]

    for i in range(2):
        f = 2 * i + pl.program_id(0)
        up_ref[block + i] = up_rows[f].astype(jnp.bfloat16)
        down_ref[block + i] = down_rows[f].astype(jnp.bfloat16)
    for layer in range(layers):
        for half in range(halves):
            lanes = slice(half * LANES, (half + 1) * LANES)
            values_of_x = members_down(perm_ref, layer, half, 0, GROUP, layers, halves)
            for x, values in enumerate(values_of_x):
                anomaly_ref[layer * width + x, :, lanes] = (values * scale).astype(jnp.bfloat16)
                low_values = values.astype(jnp.bfloat16)
                if x < RIM:
                    down_ref[x * layers + layer, :, lanes] = low_values
                if x >= width - RIM:
                    up_ref[(x - width + RIM) * layers + layer, :, lanes] = low_values


WORK = ("half", "face_x", "face_y", "face_z", "inverse", "first", "last")
FIELD_NAMES = ("p0", "sat", "storage", "base", "ahead", "behind", "frac", "frac_ahead")


def state_slots(layers, width):
    kept, added = {}, {}
    rim = list(range(-RIM, 0)) + list(range(width, width + RIM))
    near = [-2, -1, width, width + 1]

    def place(where, kind, rows, count=layers):
        where[kind] = {}
        for r in rows:
            for layer in range(count):
                where[kind][r, layer] = len(where[kind])

    place(kept, "half", (0, width - 1))
    place(kept, "face_x", [0, 1, 2, width - 4, width - 3, width - 2])
    outer = [0, 1, 2, width - 3, width - 2, width - 1]
    place(kept, "face_y", outer)
    place(kept, "face_z", outer, layers - 1)
    place(kept, "inverse", [0, 1, width - 2, width - 1])
    place(kept, "first", outer)
    place(kept, "last", range(2, width - 2))
    place(kept, "sat", range(3, width - 3))
    place(added, "half", rim)
    place(added, "face_x", [-3, -2, -1, width - 1, width, width + 1])
    place(added, "face_y", near)
    place(added, "face_z", near, layers - 1)
    place(added, "inverse", near + [0, width - 1])
    place(added, "first", near + [0, width - 1])
    place(added, "last", [-1, 0, 1, width - 2, width - 1, width])
    first = 0
    for places in added.values():
        for key in places:
            places[key], first = first, first + 1
    return kept, added


def ahead(values_in):
    return pltpu.roll(values_in, values_in.shape[1] - 1, 1)


def behind(values_in):
    return pltpu.roll(values_in, 1, 1)


def derived_fields(p0, sat, source, storage):
    frac = water_frac(sat)
    return dict(
        p0=p0, sat=sat, storage=storage, base=source + storage * p0,
        ahead=ahead(p0), behind=behind(p0), frac=frac, frac_ahead=ahead(frac),
    )


def cell_faces(load, store, field, r, layer, layers, sides):
    here = load("half", r, layer)
    lane = lax.broadcasted_iota(jnp.int32, here.shape, 1)
    up_y = jnp.where(lane < here.shape[1] - 1, reciprocal(here + ahead(here)), 0.0)
    low_y = behind(up_y)
    store("face_y", r, layer, up_y)
    flow = up_y * field("ahead", r, layer) + low_y * field("behind", r, layer)
    weight = up_y + low_y
    for face, towards in sides:
        flow = flow + face * field("p0", towards, layer)
        weight = weight + face
    if layer + 1 < layers:
        up_z = VERTICAL * reciprocal(here + load("half", r, layer + 1))
        store("face_z", r, layer, up_z)
        flow = flow + up_z * field("p0", r, layer + 1)
        weight = weight + up_z
    if layer > 0:
        low_z = load("face_z", r, layer - 1)
        flow = flow + low_z * field("p0", r, layer - 1)
        weight = weight + low_z
    return field("base", r, layer) + flow, field("storage", r, layer) + weight


def second_sweep(load, store, field, r, layers):
    for layer in range(layers):
        here = load("first", r, layer)
        up_y = load("face_y", r, layer)
        flow = (
            load("face_x", r - 1, layer) * load("first", r - 1, layer)
            + load("face_x", r, layer) * load("first", r + 1, layer)
            + up_y * ahead(here)
            + behind(up_y * here)
        )
        if layer + 1 < layers:
            flow = flow + load("face_z", r, layer) * load("first", r, layer + 1)
        if layer > 0:
            flow = flow + load("face_z", r, layer - 1) * load("first", r, layer - 1)
        store("last", r, layer, (field("base", r, layer) + flow) * load("inverse", r, layer))


def carried(face, low_press, up_press, low_frac, up_frac):
    velocity = face * (low_press - up_press)
    return velocity * jnp.where(velocity > 0, low_frac, up_frac)


def transported(load, field, first_row, last_row, layers):
    def side(r, layer):
        return carried(
            load("face_x", r, layer), load("last", r, layer), load("last", r + 1, layer),
            field("frac", r, layer), field("frac", r + 1, layer),
        )

    low_x = [side(first_row - 1, layer) for layer in range(layers)]
    for r in range(first_row, last_row + 1):
        low_z = None
        for layer in range(layers):
            here = load("last", r, layer)
            frac = field("frac", r, layer)
            up_x = side(r, layer)
            up_y = carried(
                load("face_y", r, layer), here, ahead(here), frac, field("frac_ahead", r, layer)
            )
            change = (low_x[layer] - up_x) + (behind(up_y) - up_y)
            low_x[layer] = up_x
            if low_z is not None:
                change = change + low_z
            if layer + 1 < layers:
                low_z = carried(
                    load("face_z", r, layer), here, load("last", r, layer + 1), frac,
                    field("frac", r, layer + 1),
                )
                change = change - low_z
            yield r, layer, field("sat", r, layer) + STEP_COEF * change


def put_places(dest_ref, cell_ref, cell_rows, depth):
    at = lax.broadcasted_iota(jnp.int32, (depth, cell_ref.shape[1]), 0)
    for i, row in enumerate(cell_rows):
        found = at + row * depth == cell_ref[...]
        dest_ref[i * depth : (i + 1) * depth, :] = found.astype(jnp.float32).astype(jnp.bfloat16)


def find(found, values_of, place):
    every = jnp.concatenate([pieces(values) for _, values in values_of], axis=0)
    sums = jnp.dot(every, place, preferred_element_type=jnp.float32)
    for i, (n, _) in enumerate(values_of):
        part = sums[i * 3 * GROUP : (i + 1) * 3 * GROUP]
        found[n] = part if found[n] is None else found[n] + part


def joined(part):
    return (part[:GROUP] + part[GROUP : 2 * GROUP]) + part[2 * GROUP :]


def put_fields(dest_ref, field_refs):
    fields = derived_fields(*(ref[...] for ref in field_refs))
    rows, depth = field_refs[0].shape
    for n, name in enumerate(FIELD_NAMES):
        for row in range(rows):
            dest_ref[n * rows + row] = jnp.broadcast_to(fields[name][row : row + 1, :], (8, depth))


def inner_kernel(dims, rank_ref, count_ref, perm_ref, *refs):
    layers, width = dims
    rows = layers * width
    kept, _ = state_slots(layers, width)
    field_refs, cell_ref, refs = refs[:4], refs[4], refs[5:]
    states, refs = dict(zip(kept, refs)), refs[len(kept) :]
    perf_ref, shared_ref, place_ref = refs[:3]
    work_refs = dict(zip(WORK, refs[3:]))
    depth = field_refs[0].shape[1]
    halves = depth // LANES

    @pl.when(pl.program_id(0) == 0)
    def _():
        put_fields(shared_ref, field_refs)
        put_places(place_ref, cell_ref, range(rows), depth)

    def field(name, r, layer):
        tile = shared_ref[FIELD_NAMES.index(name) * rows + layer * width + r]
        return jnp.concatenate([tile] * (GROUP // 8), axis=0)

    found = [None] * 3

    def load(kind, r, layer):
        return work_refs[kind][layer * width + r]

    def store(kind, r, layer, values_in):
        if kind in work_refs:
            work_refs[kind][layer * width + r] = values_in
        if (r, layer) in kept[kind]:
            states[kind][kept[kind][r, layer]] = values_in

    for layer in range(layers):
        lane_tiles = [
            members_down(perm_ref, layer, h, 0, GROUP, layers, halves) for h in range(halves)
        ]
        for r in range(width):
            values = jnp.concatenate([tiles[r] for tiles in lane_tiles], axis=1)
            half = 0.5 * jnp.exp(-values)
            store("half", r, layer, half)
    for r in range(width - 1):
        for layer in range(layers):
            store(
                "face_x", r, layer,
                reciprocal(load("half", r, layer) + load("half", r + 1, layer)),
            )
    for r in range(width):
        for layer in range(layers):
            sides = []
            if r > 0:
                sides.append((load("face_x", r - 1, layer), r - 1))
            if r < width - 1:
                sides.append((load("face_x", r, layer), r + 1))
            top, bottom = cell_faces(load, store, field, r, layer, layers, sides)
            if 0 < r < width - 1:
                bottom = reciprocal(bottom)
                top = top * bottom
            store("first", r, layer, top)
            store("inverse", r, layer, bottom)
    for r in range(2, width - 2):
        second_sweep(load, store, field, r, layers)
    for r, layer, saturation in transported(load, field, 3, width - 4, layers):
        store("sat", r, layer, saturation)
    for r in range(width):
        for layer in range(layers):
            values_of = [(0, load("half", r, layer))]
            if (r, layer) in kept["last"]:
                values_of.append((1, load("last", r, layer)))
            if (r, layer) in kept["sat"]:
                values_of.append((2, states["sat"][kept["sat"][r, layer]]))
            first = (layer * width + r) * depth
            find(found, values_of, place_ref[first : first + depth, :])
    for n in range(3):
        perf_ref[n] = joined(found[n])


def edge_kernel(dims, rank_ref, low_ref, high_ref, *refs):
    local_count, layers, width, tile_count = dims
    rows = layers * width
    depth = low_ref.shape[1]
    halves = depth // LANES
    group = pl.program_id(0)
    kept, added = state_slots(layers, width)
    field_refs, count_ref, cell_ref, well_ref, bhp_ref = refs[:4], refs[4], refs[5], refs[6], refs[7]
    refs = refs[8:]
    sources, refs = refs[: len(kept) + 1], refs[len(kept) + 1 :]
    sems, buffers, refs = refs[-1], refs[-2 - len(kept) : -1], refs[: -2 - len(kept)]
    states = dict(zip(kept, buffers))
    copies = {
        kind: pltpu.make_async_copy(source, buffer, sems.at[n])
        for n, (kind, source, buffer) in enumerate(zip([*kept, "perf"], sources, buffers))
    }
    perf_ref, refs = buffers[-1], [None, *refs]
    at_group = pl.ds(pl.multiple_of(group * GROUP, GROUP), GROUP)

    @pl.when(group == 0)
    def _():
        for copy in copies.values():
            copy.start()

    def arrive(*kinds):
        @pl.when(group == 0)
        def _():
            for kind in kinds:
                copies[kind].wait()

    _, press_ref, moved_ref, rates_ref = refs[:4]
    added_ref, gathered_ref, shared_ref, place_ref = refs[4:]
    rim_rows = RIM * layers * local_count
    has_low = (rank_ref[0] > 0).astype(jnp.float32)
    has_high = (rank_ref[0] < tile_count - 1).astype(jnp.float32)
    rims = [
        derived_fields(
            *(
                ref[rim_rows + f * GROUP : rim_rows + (f + 1) * GROUP, :].astype(jnp.float32)
                for f in range(4)
            )
        )
        for ref in (low_ref, high_ref)
    ]
    slots, wells = cell_ref.shape[1], bhp_ref.shape[1]

    moved = [layer * width + r for layer in range(layers) for r in range(width)]
    moved = [row for row in moved if (row % width, row // width) not in kept["sat"]]

    @pl.when(group == 0)
    def _():
        put_fields(shared_ref, field_refs)
        put_places(place_ref, cell_ref, moved, depth)

    def field(name, r, layer):
        if 0 <= r < width:
            tile = shared_ref[FIELD_NAMES.index(name) * rows + layer * width + r]
            return jnp.concatenate([tile] * (GROUP // 8), axis=0)
        part, at = (rims[0], r + RIM) if r < 0 else (rims[1], r - width)
        at = layer * RIM + at
        return part[name][at : at + 1, :]

    found = [None] * 3

    def load(kind, r, layer):
        if (r, layer) in added.get(kind, {}):
            return added_ref[added[kind][r, layer]]
        return states[kind][kept[kind][r, layer], at_group, :]

    def store(kind, r, layer, values_in):
        added_ref[added[kind][r, layer]] = values_in

    for r in list(range(-RIM, 0)) + list(range(width, width + RIM)):
        ref, i = (low_ref, r + RIM) if r < 0 else (high_ref, r - width)
        for layer in range(layers):
            at = (i * layers + layer) * local_count + group * GROUP
            values = ref[pl.ds(pl.multiple_of(at, GROUP), GROUP), :].astype(jnp.float32)
            store("half", r, layer, 0.5 * jnp.exp(-values))
    arrive("half")
    for r in (-3, -2, -1, width - 1, width, width + 1):
        for layer in range(layers):
            face = reciprocal(load("half", r, layer) + load("half", r + 1, layer))
            if r == -1:
                face = face * has_low
            if r == width - 1:
                face = face * has_high
            store("face_x", r, layer, face)
    for r in (-2, -1, width, width + 1):
        for layer in range(layers):
            sides = [
                (load("face_x", r - 1, layer), r - 1), (load("face_x", r, layer), r + 1)
            ]
            top, bottom = cell_faces(load, store, field, r, layer, layers, sides)
            bottom = reciprocal(bottom)
            store("first", r, layer, top * bottom)
            store("inverse", r, layer, bottom)
    arrive(*(kind for kind in copies if kind != "half"))
    for r, face_row, towards in ((0, -1, -1), (width - 1, width - 1, width)):
        for layer in range(layers):
            face = load("face_x", face_row, layer)
            top = states["first"][kept["first"][r, layer], at_group, :]
            bottom = states["inverse"][kept["inverse"][r, layer], at_group, :]
            bottom = reciprocal(bottom + face)
            store("first", r, layer, (top + face * field("p0", towards, layer)) * bottom)
            store("inverse", r, layer, bottom)
    for r in (-1, 0, 1, width - 2, width - 1, width):
        second_sweep(load, store, field, r, layers)

    for first_row, last_row in ((0, 2), (width - 3, width - 1)):
        for r, layer, saturation in transported(load, field, first_row, last_row, layers):
            moved_ref[layer * width + r] = saturation

    for layer in range(layers):
        for r in range(width):
            press_ref[layer * width + r] = load("last", r, layer)
            if (r, layer) in kept["sat"]:
                moved_ref[layer * width + r] = load("sat", r, layer)

    for i, row in enumerate(moved):
        r, layer = row % width, row // width
        values_of = [(2, moved_ref[row])]
        if (r, layer) in added["last"]:
            values_of.append((1, load("last", r, layer)))
        find(found, values_of, place_ref[i * depth : (i + 1) * depth, :])
    for n in range(3):
        total = perf_ref[n, at_group, :]
        if found[n] is not None:
            total = total + joined(found[n])
        gathered_ref[n, at_group, :] = total

    @pl.when(group == local_count // GROUP - 1)
    def _():
        chosen = (
            (lax.broadcasted_iota(jnp.int32, (wells, slots), 0) == well_ref[...])
            .astype(jnp.float32)
            .astype(jnp.bfloat16)
        )
        bhp = pieces(jnp.broadcast_to(bhp_ref[...], (GROUP, wells)))
        bhp = jnp.dot(bhp, chosen, preferred_element_type=jnp.float32)
        perf_bhp = (bhp[:1] + bhp[GROUP : GROUP + 1]) + bhp[2 * GROUP : 2 * GROUP + 1]
        live = (lax.broadcasted_iota(jnp.int32, (1, slots), 1) < count_ref[0]).astype(jnp.float32)
        mobility = water_frac(gathered_ref[2]) * reciprocal(2.0 * gathered_ref[0])
        terms = mobility * (gathered_ref[1] - perf_bhp) * live
        sums = lax.dot_general(
            pieces(terms), chosen, (((1,), (1,)), ((), ())), preferred_element_type=jnp.float32
        )
        partial_rates = (sums[:local_count] + sums[local_count : 2 * local_count]) + sums[
            2 * local_count :
        ]
        rates_ref[...] = jnp.broadcast_to(partial_rates[None], rates_ref.shape)


def output_kernel(layers, width, *refs):
    halves = refs[0].shape[2] // LANES
    for source_ref, out_ref in zip(refs[:2], refs[2:]):
        for layer in range(layers):
            for h in range(halves):
                rows_of_x = [
                    source_ref[layer * width + x, :, h * LANES : (h + 1) * LANES]
                    for x in range(width)
                ]
                for where_tile, tile in members_apart(rows_of_x, layer, h, layers, halves):
                    out_ref[where_tile, :] = tile


def invert_panel(columns):
    row = lax.broadcasted_iota(jnp.int32, columns[0].shape, 0)
    columns = list(columns)
    for k in range(PANEL):
        inverse = 1.0 / columns[k][k : k + 1]
        pivot = columns[k]
        for j in range(PANEL):
            if j != k:
                factor = columns[j][k : k + 1] * inverse
                columns[j] = jnp.where(row == k, factor, columns[j] - pivot * factor)
        columns[k] = jnp.where(row == k, inverse, -pivot * inverse)
    return columns


def solve_blocks(gram_matrix, cross_matrix):
    size = gram_matrix.shape[0]
    count = size // PANEL
    row = lax.broadcasted_iota(jnp.int32, gram_matrix.shape, 0)
    lane = lax.broadcasted_iota(jnp.int32, gram_matrix.shape, 1)
    full = gram_matrix + (row == lane).astype(jnp.float32)
    left = [full[i * PANEL : (i + 1) * PANEL] for i in range(count)]
    right = [cross_matrix[i * PANEL : (i + 1) * PANEL] for i in range(count)]
    width = cross_matrix.shape[1]
    for p in range(count):
        columns = [
            [
                jnp.broadcast_to(left[i][:, p * PANEL + j : p * PANEL + j + 1], (PANEL, size))
                for j in range(PANEL)
            ]
            for i in range(count)
        ]
        inverse = invert_panel(columns[p])
        new_left = sum(inverse[j] * left[p][j : j + 1] for j in range(PANEL))
        new_right = sum(inverse[j][:, :width] * right[p][j : j + 1] for j in range(PANEL))
        for i in range(count):
            if i != p:
                for j in range(PANEL):
                    if p + 1 < count:
                        left[i] = left[i] - columns[i][j] * new_left[j : j + 1]
                    right[i] = right[i] - columns[i][j][:, :width] * new_right[j : j + 1]
        left[p], right[p] = new_left, new_right
    return jnp.concatenate(right, axis=0)


def update_kernel(
    dims, rank_ref, rates_ref, own_ref, noise_ref, observed_ref, var_ref, anomaly_ref, perm_ref,
    out_ref, held_ref, anomaly_buf, perm_buf, sems,
):
    local_count, layers, width = dims
    rows = layers * width
    halves = anomaly_ref.shape[1] // LANES
    copies = [
        pltpu.make_async_copy(anomaly_ref, anomaly_buf, sems.at[0]),
        pltpu.make_async_copy(perm_ref, perm_buf, sems.at[1]),
    ]
    for copy in copies:
        copy.start()
    wells, share = own_ref.shape[1], held_ref.shape[1]
    held_ref[...] = pltpu.roll(
        own_ref[...], lax.rem(wells - rank_ref[0] * share, wells), 1
    )[:, :share]
    rates = rates_ref[...]
    members = rates.shape[0]
    spread = jnp.sqrt(INFLATION * var_ref[...])
    mean_rate = jnp.sum(rates, 0, keepdims=True) / members
    scaled = (rates - mean_rate) / (spread * (members - 1) ** 0.5)
    innovation = (observed_ref[...] - own_ref[...]) / spread + noise_ref[...]
    contract = (((1,), (1,)), ((), ()))
    gram_matrix, cross_matrix = (
        lax.dot_general(
            scaled, other, contract, precision=lax.Precision.HIGHEST,
            preferred_element_type=jnp.float32,
        )
        for other in (scaled, innovation)
    )
    weights = solve_blocks(gram_matrix, cross_matrix).T.astype(jnp.bfloat16)
    for copy in copies:
        copy.wait()
    for layer in range(layers):
        updates = []
        for x in range(width):
            at = (layer * width + x) * local_count
            every = jnp.concatenate(
                [
                    anomaly_buf[first + at : first + at + local_count, :]
                    for first in range(0, members * rows, rows * local_count)
                ],
                axis=0,
            )
            updates.append(jnp.dot(weights, every, preferred_element_type=jnp.float32))
        for h in range(halves):
            rows_of_x = [update[:, h * LANES : (h + 1) * LANES] for update in updates]
            for where_tile, tile in members_apart(rows_of_x, layer, h, layers, halves):
                out_ref[where_tile, :] = perm_buf[where_tile, :] + tile


def per_device(
    log_perm,
    start_pressure,
    start_sat,
    source,
    storage,
    well_press,
    perf_cell,
    perf_well,
    perf_count,
    observed,
    obs_var,
    obs_noise,
):
    local_count, layers, strip_width, strip_depth = log_perm.shape
    tile_count = lax.axis_size("tile")
    members = local_count * lax.axis_size("member")
    well_count = well_press.shape[0]
    well_share = well_count // tile_count
    tile_rank = lax.axis_index("tile")
    rows = layers * strip_width
    slots = perf_cell.shape[0]
    flat_perm = fold(log_perm)
    fields = [
        array.reshape(rows, strip_depth) for array in (start_pressure, start_sat, source, storage)
    ]
    in_hbm = pl.BlockSpec(memory_space=pltpu.HBM)
    rim_blocks = RIM * layers + 2
    field_scratch = pltpu.VMEM((4, GROUP, strip_depth), jnp.float32)
    params = pltpu.CompilerParams(vmem_limit_bytes=60 * 2**20)

    def whole(array):
        return pl.BlockSpec(array.shape, lambda g: (0,) * array.ndim)

    def stacked(count):
        return pl.BlockSpec((count, GROUP, strip_depth), lambda g: (0, g, 0))

    block = pl.BlockSpec((GROUP * rows * (strip_depth // LANES), LANES), lambda g: (g, 0))
    up_rows, down_rows, anomaly = (
        array.reshape(-1, strip_depth)
        for array in pl.pallas_call(
            functools.partial(pack_kernel, (layers, strip_width), (members - 1) ** -0.5),
            grid=(local_count // GROUP,),
            in_specs=[block] + [whole(array) for array in fields],
            out_specs=[stacked(rim_blocks), stacked(rim_blocks), stacked(rows)],
            out_shape=[
                jax.ShapeDtypeStruct((count, local_count, strip_depth), jnp.bfloat16)
                for count in (rim_blocks, rim_blocks, rows)
            ],
            scratch_shapes=[field_scratch, field_scratch],
            compiler_params=params,
            cost_estimate=pl.CostEstimate(
                flops=4 * flat_perm.size, bytes_accessed=8 * flat_perm.size, transcendentals=0
            ),
        )(flat_perm, *fields)
    )
    low_rows, high_rows = send_both(up_rows, down_rows, "tile")
    anomaly_all = lax.all_gather(anomaly, "member", axis=0, tiled=True)

    kept, added = state_slots(layers, strip_width)
    smem, vmem = pl.BlockSpec(memory_space=pltpu.SMEM), pl.BlockSpec(memory_space=pltpu.VMEM)

    def f32(*shape):
        return jax.ShapeDtypeStruct(shape, jnp.float32)

    state_specs = [stacked(count) for count in [*map(len, kept.values()), 3]]
    shared_scratch = pltpu.VMEM((len(FIELD_NAMES) * rows, 8, strip_depth), jnp.float32)
    place_scratch = pltpu.VMEM((rows * strip_depth, slots), jnp.bfloat16)
    cells, wells, press = perf_cell[None], perf_well[None], well_press[None]
    cost = pl.CostEstimate(flops=10**10, bytes_accessed=24 * flat_perm.size, transcendentals=0)
    state = pl.pallas_call(
        functools.partial(inner_kernel, (layers, strip_width)),
        grid=(local_count // GROUP,),
        in_specs=[smem, smem, block] + [whole(array) for array in fields] + [whole(cells)],
        out_specs=state_specs,
        out_shape=[
            f32(count, local_count, strip_depth) for count in map(len, kept.values())
        ]
        + [f32(3, local_count, slots)],
        scratch_shapes=[shared_scratch, place_scratch]
        + [pltpu.VMEM((rows, GROUP, strip_depth), jnp.float32)] * len(WORK),
        compiler_params=params,
        cost_estimate=cost,
    )(tile_rank[None], perf_count, flat_perm, *fields, cells)
    press_rows, sat_rows, partial_rates = pl.pallas_call(
        functools.partial(edge_kernel, (local_count, layers, strip_width, tile_count)),
        grid=(local_count // GROUP,),
        in_specs=[smem, whole(low_rows), whole(high_rows)]
        + [whole(array) for array in fields]
        + [smem, whole(cells), whole(wells), whole(press)]
        + [in_hbm] * len(state),
        out_specs=[
            stacked(rows), stacked(rows),
            pl.BlockSpec((tile_count, local_count, well_count), lambda g: (0, 0, 0)),
        ],
        out_shape=[
            f32(rows, local_count, strip_depth), f32(rows, local_count, strip_depth),
            f32(tile_count, local_count, well_count),
        ],
        scratch_shapes=[
            pltpu.VMEM((sum(map(len, added.values())), GROUP, strip_depth), jnp.float32),
            pltpu.VMEM((3, local_count, slots), jnp.float32),
            shared_scratch,
            place_scratch,
            *(pltpu.VMEM(array.shape, jnp.float32) for array in state),
            pltpu.SemaphoreType.DMA((len(state),)),
        ],
        compiler_params=params,
        cost_estimate=cost,
    )(
        tile_rank[None], low_rows, high_rows, *fields, perf_count, cells, wells, press, *state
    )
    flat_press, flat_sat = pl.pallas_call(
        functools.partial(output_kernel, layers, strip_width),
        grid=(local_count // GROUP,),
        in_specs=[stacked(rows)] * 2,
        out_specs=[block] * 2,
        out_shape=[f32(*flat_perm.shape)] * 2,
        compiler_params=params,
        cost_estimate=pl.CostEstimate(
            flops=10**9, bytes_accessed=16 * flat_perm.size, transcendentals=0
        ),
    )(press_rows, sat_rows)
    own_rates = jnp.sum(lax.all_to_all(partial_rates, "tile", 0, 0), 0)
    rates_all = lax.all_gather(own_rates, "member", axis=0, tiled=True)
    new_flat, well_rates = pl.pallas_call(
        functools.partial(update_kernel, (local_count, layers, strip_width)),
        out_shape=(f32(*flat_perm.shape), f32(local_count, well_share)),
        in_specs=[smem] + [vmem] * 5 + [in_hbm] * 2,
        out_specs=(vmem, vmem),
        scratch_shapes=[
            pltpu.VMEM(anomaly_all.shape, jnp.bfloat16),
            pltpu.VMEM(flat_perm.shape, jnp.float32),
            pltpu.SemaphoreType.DMA((2,)),
        ],
        compiler_params=pltpu.CompilerParams(vmem_limit_bytes=60 * 2**20),
        cost_estimate=pl.CostEstimate(
            flops=12 * members**3, bytes_accessed=16 * flat_perm.size, transcendentals=0
        ),
    )(tile_rank[None], rates_all, own_rates, obs_noise, observed[None], obs_var[None], anomaly_all, flat_perm)
    new_log_perm = unfold(new_flat, log_perm.shape)
    pressure = unfold(flat_press, log_perm.shape)
    saturation = unfold(flat_sat, log_perm.shape)
    return (new_log_perm, pressure, saturation, well_rates)


def solution(mesh):
    return jax.shard_map(
        per_device,
        mesh=mesh,
        in_specs=(
            P("member", None, "tile", None),
            P(None, "tile", None),
            P(None, "tile", None),
            P(None, "tile", None),
            P(None, "tile", None),
            P(),
            P("tile"),
            P("tile"),
            P("tile"),
            P(),
            P(),
            P("member", None),
        ),
        out_specs=(
            P("member", None, "tile", None),
            P("member", None, "tile", None),
            P("member", None, "tile", None),
            P("member", "tile"),
        ),
        check_vma=False,
    )
```

```python
import functools

import jax
import jax.numpy as jnp
from jax import lax
from jax.experimental import pallas as pl
from jax.experimental.pallas import tpu as pltpu
from jax.sharding import PartitionSpec as P

SWEEPS = 2
RIM = SWEEPS + 1


VERTICAL = 0.5
VISCOSITY_RATIO = 2.0
STEP_COEF = 0.1
INFLATION = 4.0
PANEL = 8
GROUP = 16
LANES = 128


def fold(array):
    members, layers, width, depth = array.shape
    array = array.reshape(members, layers, width, depth // LANES, LANES)
    return array.transpose(0, 1, 3, 2, 4).reshape(-1, LANES)


def unfold(rows, shape):
    members, layers, width, depth = shape
    array = rows.reshape(members, layers, depth // LANES, width, LANES)
    return array.transpose(0, 1, 3, 2, 4).reshape(shape)


def turn(tiles):
    row = lax.broadcasted_iota(jnp.int32, tiles[0].shape, 0)
    for step in (4, 2, 1):
        stays = (row & step) == 0
        turned = list(tiles)
        for i in range(8):
            if i & step == 0:
                first, second = tiles[i], tiles[i + step]
                turned[i] = jnp.where(stays, first, pltpu.roll(second, step, 0))
                turned[i + step] = jnp.where(stays, pltpu.roll(first, 8 - step, 0), second)
        tiles = turned
    return tiles


def tile_rows(member, layer, half, layers, halves):
    return pl.ds(((member * layers + layer) * halves + half) * 8, 8)


def members_down(ref, layer, half, first, count, layers, halves):
    octets = [
        turn([ref[tile_rows(m + i, layer, half, layers, halves), :] for i in range(8)])
        for m in range(first, first + count, 8)
    ]
    return [jnp.concatenate([octet[x] for octet in octets], axis=0) for x in range(8)]


def members_apart(rows_of_x, layer, half, layers, halves):
    for m in range(0, rows_of_x[0].shape[0], 8):
        for i, tile in enumerate(turn([rows[m : m + 8] for rows in rows_of_x])):
            yield tile_rows(m + i, layer, half, layers, halves), tile


def send_both(up_rows, down_rows, axis):
    count = lax.axis_size(axis)
    forward = [(i, i + 1) for i in range(count - 1)]
    backward = [(target, source) for source, target in forward]
    return lax.ppermute(up_rows, axis, forward), lax.ppermute(down_rows, axis, backward)


def reciprocal(values_in):
    guess = pl.reciprocal(values_in, approx=True)
    return guess * (2.0 - values_in * guess)


def pieces(values_in, count=3):
    parts = []
    for _ in range(count):
        parts.append(values_in.astype(jnp.bfloat16))
        values_in = values_in - parts[-1].astype(jnp.float32)
    return jnp.concatenate(parts, axis=0)


def water_frac(values_in):
    squared = values_in * values_in
    rest = 1.0 - values_in
    return squared * reciprocal(squared + VISCOSITY_RATIO * rest * rest)


def pack_kernel(
    dims, scale, perm_ref, p0_ref, sat_ref, source_ref, storage_ref, up_ref, down_ref, anomaly_ref,
    up_rows, down_rows,
):
    layers, width = dims
    halves = anomaly_ref.shape[2] // LANES
    block = RIM * layers

    @pl.when(pl.program_id(0) == 0)
    def _():
        up_rows[...] = jnp.zeros_like(up_rows)
        down_rows[...] = jnp.zeros_like(down_rows)
        for f, fields_ref in enumerate((p0_ref, sat_ref, source_ref, storage_ref)):
            for layer in range(layers):
                at = layer * RIM
                first = layer * width
                down_rows[f, at : at + RIM, :] = fields_ref[first : first + RIM, :]
                up_rows[f, at : at + RIM, :] = fields_ref[first + width - RIM : first + width, :]

    for i in range(2):
        f = 2 * i + pl.program_id(0)
        up_ref[block + i] = up_rows[f].astype(jnp.bfloat16)
        down_ref[block + i] = down_rows[f].astype(jnp.bfloat16)
    for layer in range(layers):
        for half in range(halves):
            lanes = slice(half * LANES, (half + 1) * LANES)
            values_of_x = members_down(perm_ref, layer, half, 0, GROUP, layers, halves)
            for x, values in enumerate(values_of_x):
                anomaly_ref[layer * width + x, :, lanes] = (values * scale).astype(jnp.bfloat16)
                low_values = values.astype(jnp.bfloat16)
                if x < RIM:
                    down_ref[x * layers + layer, :, lanes] = low_values
                if x >= width - RIM:
                    up_ref[(x - width + RIM) * layers + layer, :, lanes] = low_values


WORK = ("half", "face_x", "face_y", "face_z", "inverse", "first", "last")
EDGE_NAMES = ("p0", "base", "sat", "frac", "frac_ahead")
FIELD_NAMES = ("p0", "sat", "storage", "base", "ahead", "behind", "frac", "frac_ahead")


def state_slots(layers, width):
    kept, added = {}, {}
    rim = list(range(-RIM, 0)) + list(range(width, width + RIM))
    near = [-2, -1, width, width + 1]

    def place(where, kind, rows, count=layers):
        where[kind] = {}
        for r in rows:
            for layer in range(count):
                where[kind][r, layer] = len(where[kind])

    place(kept, "half", (0, width - 1))
    place(kept, "face_x", [0, 1, 2, width - 4, width - 3, width - 2])
    outer = [0, 1, 2, width - 3, width - 2, width - 1]
    place(kept, "face_y", outer)
    place(kept, "face_z", outer, layers - 1)
    place(kept, "inverse", [0, 1, width - 2, width - 1])
    place(kept, "first", outer)
    place(kept, "last", range(2, width - 2))
    place(kept, "sat", range(3, width - 3))
    place(added, "half", rim)
    place(added, "face_x", [-3, -2, -1, width - 1, width, width + 1])
    place(added, "face_y", near)
    place(added, "face_z", near, layers - 1)
    place(added, "inverse", near + [0, width - 1])
    place(added, "first", near + [0, width - 1])
    place(added, "last", [-1, 0, 1, width - 2, width - 1, width])
    first = 0
    for places in added.values():
        for key in places:
            places[key], first = first, first + 1
    return kept, added


def ahead(values_in):
    return pltpu.roll(values_in, values_in.shape[1] - 1, 1)


def behind(values_in):
    return pltpu.roll(values_in, 1, 1)


def derived_fields(p0, sat, source, storage):
    frac = water_frac(sat)
    return dict(
        p0=p0, sat=sat, storage=storage, base=source + storage * p0,
        ahead=ahead(p0), behind=behind(p0), frac=frac, frac_ahead=ahead(frac),
    )


def cell_faces(load, store, field, r, layer, layers, sides):
    here = load("half", r, layer)
    lane = lax.broadcasted_iota(jnp.int32, here.shape, 1)
    up_y = jnp.where(lane < here.shape[1] - 1, reciprocal(here + ahead(here)), 0.0)
    low_y = behind(up_y)
    store("face_y", r, layer, up_y)
    flow = up_y * field("ahead", r, layer) + low_y * field("behind", r, layer)
    weight = up_y + low_y
    for face, towards in sides:
        flow = flow + face * field("p0", towards, layer)
        weight = weight + face
    if layer + 1 < layers:
        up_z = VERTICAL * reciprocal(here + load("half", r, layer + 1))
        store("face_z", r, layer, up_z)
        flow = flow + up_z * field("p0", r, layer + 1)
        weight = weight + up_z
    if layer > 0:
        low_z = load("face_z", r, layer - 1)
        flow = flow + low_z * field("p0", r, layer - 1)
        weight = weight + low_z
    return field("base", r, layer) + flow, field("storage", r, layer) + weight


def second_sweep(load, store, field, r, layers):
    for layer in range(layers):
        here = load("first", r, layer)
        up_y = load("face_y", r, layer)
        flow = (
            load("face_x", r - 1, layer) * load("first", r - 1, layer)
            + load("face_x", r, layer) * load("first", r + 1, layer)
            + up_y * ahead(here)
            + behind(up_y * here)
        )
        if layer + 1 < layers:
            flow = flow + load("face_z", r, layer) * load("first", r, layer + 1)
        if layer > 0:
            flow = flow + load("face_z", r, layer - 1) * load("first", r, layer - 1)
        store("last", r, layer, (field("base", r, layer) + flow) * load("inverse", r, layer))


def carried(face, low_press, up_press, low_frac, up_frac):
    velocity = face * (low_press - up_press)
    return velocity * jnp.where(velocity > 0, low_frac, up_frac)


def transported(load, field, first_row, last_row, layers):
    def side(r, layer):
        return carried(
            load("face_x", r, layer), load("last", r, layer), load("last", r + 1, layer),
            field("frac", r, layer), field("frac", r + 1, layer),
        )

    low_x = [side(first_row - 1, layer) for layer in range(layers)]
    for r in range(first_row, last_row + 1):
        low_z = None
        for layer in range(layers):
            here = load("last", r, layer)
            frac = field("frac", r, layer)
            up_x = side(r, layer)
            up_y = carried(
                load("face_y", r, layer), here, ahead(here), frac, field("frac_ahead", r, layer)
            )
            change = (low_x[layer] - up_x) + (behind(up_y) - up_y)
            low_x[layer] = up_x
            if low_z is not None:
                change = change + low_z
            if layer + 1 < layers:
                low_z = carried(
                    load("face_z", r, layer), here, load("last", r, layer + 1), frac,
                    field("frac", r, layer + 1),
                )
                change = change - low_z
            yield r, layer, field("sat", r, layer) + STEP_COEF * change


def put_places(dest_ref, cell_ref, cell_rows, depth):
    at = lax.broadcasted_iota(jnp.int32, (depth, cell_ref.shape[1]), 0)
    for i, row in enumerate(cell_rows):
        found = at + row * depth == cell_ref[...]
        dest_ref[i * depth : (i + 1) * depth, :] = found.astype(jnp.float32).astype(jnp.bfloat16)


def find(found, values_of, place):
    every = jnp.concatenate([pieces(values, 2) for _, values in values_of], axis=0)
    sums = jnp.dot(every, place, preferred_element_type=jnp.float32)
    for i, (n, _) in enumerate(values_of):
        part = sums[i * 2 * GROUP : (i + 1) * 2 * GROUP]
        found[n] = part if found[n] is None else found[n] + part


def joined(part):
    return part[:GROUP] + part[GROUP:]


def put_fields(dest_ref, field_refs, names):
    fields = derived_fields(*(ref[...] for ref in field_refs))
    rows, depth = field_refs[0].shape
    for n, name in enumerate(names):
        for row in range(rows):
            dest_ref[n * rows + row] = jnp.broadcast_to(fields[name][row : row + 1, :], (8, depth))


def inner_kernel(dims, rank_ref, count_ref, perm_ref, *refs):
    layers, width = dims
    rows = layers * width
    kept, _ = state_slots(layers, width)
    field_refs, cell_ref, refs = refs[:4], refs[4], refs[5:]
    states, refs = dict(zip(kept, refs)), refs[len(kept) :]
    perf_ref, shared_ref, place_ref = refs[:3]
    work_refs = dict(zip(WORK, refs[3:]))
    depth = field_refs[0].shape[1]
    halves = depth // LANES

    @pl.when(pl.program_id(0) == 0)
    def _():
        put_fields(shared_ref, field_refs, FIELD_NAMES)
        put_places(place_ref, cell_ref, range(rows), depth)

    def field(name, r, layer):
        tile = shared_ref[FIELD_NAMES.index(name) * rows + layer * width + r]
        return jnp.concatenate([tile] * (GROUP // 8), axis=0)

    found = [None] * 3

    def load(kind, r, layer):
        return work_refs[kind][layer * width + r]

    def store(kind, r, layer, values_in):
        if kind in work_refs:
            work_refs[kind][layer * width + r] = values_in
        if (r, layer) in kept[kind]:
            states[kind][kept[kind][r, layer]] = values_in

    for layer in range(layers):
        lane_tiles = [
            members_down(perm_ref, layer, h, 0, GROUP, layers, halves) for h in range(halves)
        ]
        for r in range(width):
            values = jnp.concatenate([tiles[r] for tiles in lane_tiles], axis=1)
            half = 0.5 * jnp.exp(-values)
            store("half", r, layer, half)
    for r in range(width - 1):
        for layer in range(layers):
            store(
                "face_x", r, layer,
                reciprocal(load("half", r, layer) + load("half", r + 1, layer)),
            )
    for r in range(width):
        for layer in range(layers):
            sides = []
            if r > 0:
                sides.append((load("face_x", r - 1, layer), r - 1))
            if r < width - 1:
                sides.append((load("face_x", r, layer), r + 1))
            top, bottom = cell_faces(load, store, field, r, layer, layers, sides)
            if 0 < r < width - 1:
                bottom = reciprocal(bottom)
                top = top * bottom
            store("first", r, layer, top)
            store("inverse", r, layer, bottom)
    for r in range(2, width - 2):
        second_sweep(load, store, field, r, layers)
    for r, layer, saturation in transported(load, field, 3, width - 4, layers):
        store("sat", r, layer, saturation)
    for r in range(width):
        for layer in range(layers):
            values_of = [(0, load("half", r, layer))]
            if (r, layer) in kept["last"]:
                values_of.append((1, load("last", r, layer)))
            if (r, layer) in kept["sat"]:
                values_of.append((2, states["sat"][kept["sat"][r, layer]]))
            first = (layer * width + r) * depth
            find(found, values_of, place_ref[first : first + depth, :])
    for n in range(3):
        perf_ref[n] = joined(found[n])


def edge_kernel(dims, rank_ref, low_ref, high_ref, *refs):
    local_count, layers, width, tile_count = dims
    rows = layers * width
    depth = low_ref.shape[1]
    halves = depth // LANES
    group = pl.program_id(0)
    kept, added = state_slots(layers, width)
    field_refs, count_ref, cell_ref, well_ref, bhp_ref = refs[:4], refs[4], refs[5], refs[6], refs[7]
    refs = refs[8:]
    states, refs = dict(zip(kept, refs)), refs[len(kept) :]
    perf_ref, press_ref, moved_ref, rates_ref = refs[:4]
    added_ref, gathered_ref, shared_ref, place_ref = refs[4:]
    rim_rows = RIM * layers * local_count
    has_low = (rank_ref[0] > 0).astype(jnp.float32)
    has_high = (rank_ref[0] < tile_count - 1).astype(jnp.float32)
    rims = [
        derived_fields(
            *(
                ref[rim_rows + f * GROUP : rim_rows + (f + 1) * GROUP, :].astype(jnp.float32)
                for f in range(4)
            )
        )
        for ref in (low_ref, high_ref)
    ]
    slots, wells = cell_ref.shape[1], bhp_ref.shape[1]

    moved = [layer * width + r for layer in range(layers) for r in range(width)]
    moved = [row for row in moved if (row % width, row // width) not in kept["sat"]]

    @pl.when(group == 0)
    def _():
        put_fields(shared_ref, field_refs, EDGE_NAMES)
        put_places(place_ref, cell_ref, moved, depth)

    def field(name, r, layer):
        if 0 <= r < width:
            tile = shared_ref[EDGE_NAMES.index(name) * rows + layer * width + r]
            return jnp.concatenate([tile] * (GROUP // 8), axis=0)
        part, at = (rims[0], r + RIM) if r < 0 else (rims[1], r - width)
        at = layer * RIM + at
        return part[name][at : at + 1, :]

    found = [None] * 3

    def load(kind, r, layer):
        if (r, layer) in added.get(kind, {}):
            return added_ref[added[kind][r, layer]]
        return states[kind][kept[kind][r, layer]]

    def store(kind, r, layer, values_in):
        added_ref[added[kind][r, layer]] = values_in

    for r in list(range(-RIM, 0)) + list(range(width, width + RIM)):
        ref, i = (low_ref, r + RIM) if r < 0 else (high_ref, r - width)
        for layer in range(layers):
            at = (i * layers + layer) * local_count + group * GROUP
            values = ref[pl.ds(pl.multiple_of(at, GROUP), GROUP), :].astype(jnp.float32)
            store("half", r, layer, 0.5 * jnp.exp(-values))
    for r in (-3, -2, -1, width - 1, width, width + 1):
        for layer in range(layers):
            face = reciprocal(load("half", r, layer) + load("half", r + 1, layer))
            if r == -1:
                face = face * has_low
            if r == width - 1:
                face = face * has_high
            store("face_x", r, layer, face)
    for r in (-2, -1, width, width + 1):
        for layer in range(layers):
            sides = [
                (load("face_x", r - 1, layer), r - 1), (load("face_x", r, layer), r + 1)
            ]
            top, bottom = cell_faces(load, store, field, r, layer, layers, sides)
            bottom = reciprocal(bottom)
            store("first", r, layer, top * bottom)
            store("inverse", r, layer, bottom)
    for r, face_row, towards in ((0, -1, -1), (width - 1, width - 1, width)):
        for layer in range(layers):
            face = load("face_x", face_row, layer)
            top = states["first"][kept["first"][r, layer]]
            bottom = states["inverse"][kept["inverse"][r, layer]]
            bottom = reciprocal(bottom + face)
            store("first", r, layer, (top + face * field("p0", towards, layer)) * bottom)
            store("inverse", r, layer, bottom)
    for r in (-1, 0, 1, width - 2, width - 1, width):
        second_sweep(load, store, field, r, layers)

    for first_row, last_row in ((0, 2), (width - 3, width - 1)):
        for r, layer, saturation in transported(load, field, first_row, last_row, layers):
            moved_ref[layer * width + r] = saturation

    for layer in range(layers):
        for r in range(width):
            press_ref[layer * width + r] = load("last", r, layer)
            if (r, layer) in kept["sat"]:
                moved_ref[layer * width + r] = load("sat", r, layer)

    for i, row in enumerate(moved):
        r, layer = row % width, row // width
        values_of = [(2, moved_ref[row])]
        if (r, layer) in added["last"]:
            values_of.append((1, load("last", r, layer)))
        find(found, values_of, place_ref[i * depth : (i + 1) * depth, :])
    for n in range(3):
        total = perf_ref[n] if found[n] is None else perf_ref[n] + joined(found[n])
        gathered_ref[n, pl.ds(pl.multiple_of(group * GROUP, GROUP), GROUP), :] = total

    @pl.when(group == local_count // GROUP - 1)
    def _():
        chosen = (
            (lax.broadcasted_iota(jnp.int32, (wells, slots), 0) == well_ref[...])
            .astype(jnp.float32)
            .astype(jnp.bfloat16)
        )
        bhp = pieces(jnp.broadcast_to(bhp_ref[...], (GROUP, wells)))
        bhp = jnp.dot(bhp, chosen, preferred_element_type=jnp.float32)
        perf_bhp = (bhp[:1] + bhp[GROUP : GROUP + 1]) + bhp[2 * GROUP : 2 * GROUP + 1]
        live = (lax.broadcasted_iota(jnp.int32, (1, slots), 1) < count_ref[0]).astype(jnp.float32)
        mobility = water_frac(gathered_ref[2]) * reciprocal(2.0 * gathered_ref[0])
        terms = mobility * (gathered_ref[1] - perf_bhp) * live
        sums = lax.dot_general(
            pieces(terms), chosen, (((1,), (1,)), ((), ())), preferred_element_type=jnp.float32
        )
        partial_rates = (sums[:local_count] + sums[local_count : 2 * local_count]) + sums[
            2 * local_count :
        ]
        rates_ref[...] = jnp.broadcast_to(partial_rates[None], rates_ref.shape)


def output_kernel(layers, width, *refs):
    halves = refs[0].shape[2] // LANES
    for source_ref, out_ref in zip(refs[:2], refs[2:]):
        for layer in range(layers):
            for h in range(halves):
                rows_of_x = [
                    source_ref[layer * width + x, :, h * LANES : (h + 1) * LANES]
                    for x in range(width)
                ]
                for where_tile, tile in members_apart(rows_of_x, layer, h, layers, halves):
                    out_ref[where_tile, :] = tile


def invert_panel(columns):
    row = lax.broadcasted_iota(jnp.int32, columns[0].shape, 0)
    columns = list(columns)
    for k in range(PANEL):
        inverse = 1.0 / columns[k][k : k + 1]
        pivot = columns[k]
        for j in range(PANEL):
            if j != k:
                factor = columns[j][k : k + 1] * inverse
                columns[j] = jnp.where(row == k, factor, columns[j] - pivot * factor)
        columns[k] = jnp.where(row == k, inverse, -pivot * inverse)
    return columns


def solve_blocks(gram_matrix, cross_matrix):
    size = gram_matrix.shape[0]
    count = size // PANEL
    row = lax.broadcasted_iota(jnp.int32, gram_matrix.shape, 0)
    lane = lax.broadcasted_iota(jnp.int32, gram_matrix.shape, 1)
    full = gram_matrix + (row == lane).astype(jnp.float32)
    left = [full[i * PANEL : (i + 1) * PANEL] for i in range(count)]
    right = [cross_matrix[i * PANEL : (i + 1) * PANEL] for i in range(count)]
    width = cross_matrix.shape[1]
    for p in range(count):
        columns = [
            [
                jnp.broadcast_to(left[i][:, p * PANEL + j : p * PANEL + j + 1], (PANEL, size))
                for j in range(PANEL)
            ]
            for i in range(count)
        ]
        inverse = invert_panel(columns[p])
        new_left = sum(inverse[j] * left[p][j : j + 1] for j in range(PANEL))
        new_right = sum(inverse[j][:, :width] * right[p][j : j + 1] for j in range(PANEL))
        for i in range(count):
            if i != p:
                for j in range(PANEL):
                    if p + 1 < count:
                        left[i] = left[i] - columns[i][j] * new_left[j : j + 1]
                    right[i] = right[i] - columns[i][j][:, :width] * new_right[j : j + 1]
        left[p], right[p] = new_left, new_right
    return jnp.concatenate(right, axis=0)


def update_kernel(
    dims, rank_ref, rates_ref, own_ref, noise_ref, observed_ref, var_ref, anomaly_ref, perm_ref,
    out_ref, held_ref, anomaly_buf, perm_buf, sems,
):
    local_count, layers, width = dims
    rows = layers * width
    halves = anomaly_ref.shape[1] // LANES
    copies = [
        pltpu.make_async_copy(anomaly_ref, anomaly_buf, sems.at[0]),
        pltpu.make_async_copy(perm_ref, perm_buf, sems.at[1]),
    ]
    for copy in copies:
        copy.start()
    wells, share = own_ref.shape[1], held_ref.shape[1]
    held_ref[...] = pltpu.roll(
        own_ref[...], lax.rem(wells - rank_ref[0] * share, wells), 1
    )[:, :share]
    rates = rates_ref[...]
    members = rates.shape[0]
    spread = jnp.sqrt(INFLATION * var_ref[...])
    mean_rate = jnp.sum(rates, 0, keepdims=True) / members
    scaled = (rates - mean_rate) / (spread * (members - 1) ** 0.5)
    innovation = (observed_ref[...] - own_ref[...]) / spread + noise_ref[...]
    contract = (((1,), (1,)), ((), ()))
    gram_matrix, cross_matrix = (
        lax.dot_general(
            scaled, other, contract, precision=lax.Precision.HIGHEST,
            preferred_element_type=jnp.float32,
        )
        for other in (scaled, innovation)
    )
    weights = solve_blocks(gram_matrix, cross_matrix).T.astype(jnp.bfloat16)
    for copy in copies:
        copy.wait()
    for layer in range(layers):
        updates = []
        for x in range(width):
            at = (layer * width + x) * local_count
            every = jnp.concatenate(
                [
                    anomaly_buf[first + at : first + at + local_count, :]
                    for first in range(0, members * rows, rows * local_count)
                ],
                axis=0,
            )
            updates.append(jnp.dot(weights, every, preferred_element_type=jnp.float32))
        for h in range(halves):
            rows_of_x = [update[:, h * LANES : (h + 1) * LANES] for update in updates]
            for where_tile, tile in members_apart(rows_of_x, layer, h, layers, halves):
                out_ref[where_tile, :] = perm_buf[where_tile, :] + tile


def per_device(
    log_perm,
    start_pressure,
    start_sat,
    source,
    storage,
    well_press,
    perf_cell,
    perf_well,
    perf_count,
    observed,
    obs_var,
    obs_noise,
):
    local_count, layers, strip_width, strip_depth = log_perm.shape
    tile_count = lax.axis_size("tile")
    members = local_count * lax.axis_size("member")
    well_count = well_press.shape[0]
    well_share = well_count // tile_count
    tile_rank = lax.axis_index("tile")
    rows = layers * strip_width
    slots = perf_cell.shape[0]
    flat_perm = fold(log_perm)
    fields = [
        array.reshape(rows, strip_depth) for array in (start_pressure, start_sat, source, storage)
    ]
    in_hbm = pl.BlockSpec(memory_space=pltpu.HBM)
    rim_blocks = RIM * layers + 2
    field_scratch = pltpu.VMEM((4, GROUP, strip_depth), jnp.float32)
    params = pltpu.CompilerParams(vmem_limit_bytes=60 * 2**20)

    def whole(array):
        return pl.BlockSpec(array.shape, lambda g: (0,) * array.ndim)

    def stacked(count):
        return pl.BlockSpec((count, GROUP, strip_depth), lambda g: (0, g, 0))

    block = pl.BlockSpec((GROUP * rows * (strip_depth // LANES), LANES), lambda g: (g, 0))
    up_rows, down_rows, anomaly = (
        array.reshape(-1, strip_depth)
        for array in pl.pallas_call(
            functools.partial(pack_kernel, (layers, strip_width), (members - 1) ** -0.5),
            grid=(local_count // GROUP,),
            in_specs=[block] + [whole(array) for array in fields],
            out_specs=[stacked(rim_blocks), stacked(rim_blocks), stacked(rows)],
            out_shape=[
                jax.ShapeDtypeStruct((count, local_count, strip_depth), jnp.bfloat16)
                for count in (rim_blocks, rim_blocks, rows)
            ],
            scratch_shapes=[field_scratch, field_scratch],
            compiler_params=params,
            cost_estimate=pl.CostEstimate(
                flops=4 * flat_perm.size, bytes_accessed=8 * flat_perm.size, transcendentals=0
            ),
        )(flat_perm, *fields)
    )
    low_rows, high_rows = send_both(up_rows, down_rows, "tile")
    anomaly_all = lax.all_gather(anomaly, "member", axis=0, tiled=True)

    kept, added = state_slots(layers, strip_width)
    smem, vmem = pl.BlockSpec(memory_space=pltpu.SMEM), pl.BlockSpec(memory_space=pltpu.VMEM)

    def f32(*shape):
        return jax.ShapeDtypeStruct(shape, jnp.float32)

    state_specs = [stacked(count) for count in [*map(len, kept.values()), 3]]
    shared_scratch = pltpu.VMEM((len(FIELD_NAMES) * rows, 8, strip_depth), jnp.float32)
    place_scratch = pltpu.VMEM((rows * strip_depth, slots), jnp.bfloat16)
    cells, wells, press = perf_cell[None], perf_well[None], well_press[None]
    cost = pl.CostEstimate(flops=10**10, bytes_accessed=24 * flat_perm.size, transcendentals=0)
    state = pl.pallas_call(
        functools.partial(inner_kernel, (layers, strip_width)),
        grid=(local_count // GROUP,),
        in_specs=[smem, smem, block] + [whole(array) for array in fields] + [whole(cells)],
        out_specs=state_specs,
        out_shape=[
            f32(count, local_count, strip_depth) for count in map(len, kept.values())
        ]
        + [f32(3, local_count, slots)],
        scratch_shapes=[shared_scratch, place_scratch]
        + [pltpu.VMEM((rows, GROUP, strip_depth), jnp.float32)] * len(WORK),
        compiler_params=params,
        cost_estimate=cost,
    )(tile_rank[None], perf_count, flat_perm, *fields, cells)
    press_rows, sat_rows, partial_rates = pl.pallas_call(
        functools.partial(edge_kernel, (local_count, layers, strip_width, tile_count)),
        grid=(local_count // GROUP,),
        in_specs=[smem, whole(low_rows), whole(high_rows)]
        + [whole(array) for array in fields]
        + [smem, whole(cells), whole(wells), whole(press)]
        + state_specs,
        out_specs=[
            stacked(rows), stacked(rows),
            pl.BlockSpec((tile_count, local_count, well_count), lambda g: (0, 0, 0)),
        ],
        out_shape=[
            f32(rows, local_count, strip_depth), f32(rows, local_count, strip_depth),
            f32(tile_count, local_count, well_count),
        ],
        scratch_shapes=[
            pltpu.VMEM((sum(map(len, added.values())), GROUP, strip_depth), jnp.float32),
            pltpu.VMEM((3, local_count, slots), jnp.float32),
            shared_scratch,
            place_scratch,
        ],
        compiler_params=params,
        cost_estimate=cost,
    )(
        tile_rank[None], low_rows, high_rows, *fields, perf_count, cells, wells, press, *state
    )
    flat_press, flat_sat = pl.pallas_call(
        functools.partial(output_kernel, layers, strip_width),
        grid=(local_count // GROUP,),
        in_specs=[stacked(rows)] * 2,
        out_specs=[block] * 2,
        out_shape=[f32(*flat_perm.shape)] * 2,
        compiler_params=params,
        cost_estimate=pl.CostEstimate(
            flops=10**9, bytes_accessed=16 * flat_perm.size, transcendentals=0
        ),
    )(press_rows, sat_rows)
    own_rates = jnp.sum(lax.all_to_all(partial_rates, "tile", 0, 0), 0)
    rates_all = lax.all_gather(own_rates, "member", axis=0, tiled=True)
    new_flat, well_rates = pl.pallas_call(
        functools.partial(update_kernel, (local_count, layers, strip_width)),
        out_shape=(f32(*flat_perm.shape), f32(local_count, well_share)),
        in_specs=[smem] + [vmem] * 5 + [in_hbm] * 2,
        out_specs=(vmem, vmem),
        scratch_shapes=[
            pltpu.VMEM(anomaly_all.shape, jnp.bfloat16),
            pltpu.VMEM(flat_perm.shape, jnp.float32),
            pltpu.SemaphoreType.DMA((2,)),
        ],
        compiler_params=pltpu.CompilerParams(vmem_limit_bytes=60 * 2**20),
        cost_estimate=pl.CostEstimate(
            flops=12 * members**3, bytes_accessed=16 * flat_perm.size, transcendentals=0
        ),
    )(tile_rank[None], rates_all, own_rates, obs_noise, observed[None], obs_var[None], anomaly_all, flat_perm)
    new_log_perm = unfold(new_flat, log_perm.shape)
    pressure = unfold(flat_press, log_perm.shape)
    saturation = unfold(flat_sat, log_perm.shape)
    return (new_log_perm, pressure, saturation, well_rates)


def solution(mesh):
    return jax.shard_map(
        per_device,
        mesh=mesh,
        in_specs=(
            P("member", None, "tile", None),
            P(None, "tile", None),
            P(None, "tile", None),
            P(None, "tile", None),
            P(None, "tile", None),
            P(),
            P("tile"),
            P("tile"),
            P("tile"),
            P(),
            P(),
            P("member", None),
        ),
        out_specs=(
            P("member", None, "tile", None),
            P("member", None, "tile", None),
            P("member", None, "tile", None),
            P("member", "tile"),
        ),
        check_vma=False,
    )
```
